32 devices in a mesh: dp: 8 (over y, x, core), tensor: 4 (over z).
Axes of the slice: x: 2, y: 2, z: 4, core: 2. Of those that a mesh axis runs over, the one named last changes fastest.
Arguments:
- tokens: bfloat16 [4096, 768], P(('dp', 'tensor')), may hold values from -6 to 6
- grids: int32 [8, 2], P('dp'), may hold values from 1 to 22, as said below
- qkv_weight: bfloat16 [768, 3, 768], P(None, None, 'tensor'), may hold values from -0.21875 to 0.21875
- qv_bias: float32 [2, 768], P(None, 'tensor'), may hold values from -0.6 to 0.6
- rel_table: float32 [12, 1852], P('tensor'), may hold values from -6 to 6
- proj_weight: bfloat16 [768, 768], P('tensor'), may hold values from -1.75 to 1.75
- fc1_weight: bfloat16 [768, 3072], P(None, 'tensor'), may hold values from -0.21875 to 0.21875
- fc1_bias: bfloat16 [3072], P('tensor'), may hold values from -1.796875 to 1.796875
- fc2_weight: bfloat16 [3072, 768], P('tensor'), may hold values from -0.109375 to 0.109375
- norm_gains: float32 [2, 768], replicated, may hold values from 0.25 to 1.75
- norm_biases: float32 [2, 768], replicated, may hold values from -1.8 to 1.8
- layer_scales: float32 [2, 768], replicated, may hold values from 0.5 to 2
- out_biases: float32 [2, 768], replicated, may hold values from -1.8 to 1.8
- cotangent: bfloat16 [4096, 768], P(('dp', 'tensor')), may hold values from -6 to 6
Outputs:
- output: bfloat16 [4096, 768], P(('dp', 'tensor'))
- input_grad: float32 [4096, 768], P(('dp', 'tensor'))
- grad_qkv_weight: float32 [768, 3, 768], P(None, None, 'tensor')
- grad_qv_bias: float32 [2, 768], P(None, 'tensor')
- grad_rel_table: float32 [12, 1852], P('tensor')
- grad_proj_weight: float32 [768, 768], P('tensor')
- grad_fc1_weight: float32 [768, 3072], P(None, 'tensor')
- grad_fc1_bias: float32 [3072], P('tensor')
- grad_fc2_weight: float32 [3072, 768], P('tensor')
- grad_norm_gains: float32 [2, 768], replicated
- grad_norm_biases: float32 [2, 768], replicated
- grad_layer_scales: float32 [2, 768], replicated
- grad_out_biases: float32 [2, 768], replicated
The draws below stay inside these ranges and needn't reach their ends.
Inputs may be any that keep to these rules, and one draw needn't show every extreme that they name: `grids`: each image's grid has 1 to 22 patches on a side. In each group of 1 images of one dp index one image, drawn from the seed, has at least (3) * 128 patches; in each aligned run of 8 dp indices one of these images has 22 x 22 patches.
All inputs are finite; a program needn't handle non-finite values.
Results may differ from the reference program's by a relative error of at most 0.018.
Values may be sent and summed in bfloat16 or wider, within the bound.
A program may use at most 192 MiB of HBM per device.

```python
import math
from functools import partial
import jax
import jax.numpy as jnp
from jax import lax

D = 768
HEADS = 12
HEAD = 64
FF = 3072
GRID = 22
SEQ = 512
IMGS = 1
IMAGES = 8
TOKENS = 4096
RELS = 1852
N_DP = 8
N_TENSOR = 4


def draw_grids(key, part):
    key = jax.random.fold_in(key, 7)
    keys_all = jax.random.split(key, 6)
    trims = jax.random.randint(keys_all[0], (IMAGES, 2), 0, GRID // 2 + 1)
    halves = jax.random.randint(keys_all[1], (IMAGES, 2), 0, 4)
    sides = jnp.maximum((GRID - trims) // (1 + (halves == 0).astype(jnp.int32)), 1)
    groups = IMAGES // IMGS
    needed = (N_TENSOR - 1) * SEQ // N_TENSOR
    lowest = (needed + GRID - 1) // GRID
    rows_big = jax.random.randint(keys_all[2], (groups,), lowest, GRID + 1)
    cols_floor = (needed + rows_big - 1) // rows_big
    cols_big = jax.random.randint(keys_all[3], (groups,), cols_floor, GRID + 1)
    eighth = jax.random.randint(keys_all[4], (), 0, 8)
    group_index = jnp.arange(groups, dtype=jnp.int32)
    full_group = group_index % 8 == eighth
    rows_big = jnp.where(full_group, GRID, rows_big)
    cols_big = jnp.where(full_group, GRID, cols_big)
    chosen = jax.random.randint(keys_all[5], (groups,), 0, IMGS)
    slots = jnp.arange(IMAGES, dtype=jnp.int32)
    group_of = slots // IMGS
    picked = slots % IMGS == chosen[group_of]
    big_sides = jnp.stack([rows_big[group_of], cols_big[group_of]], axis=1)
    sides = jnp.where(picked[:, None], big_sides, sides)
    return sides.astype(jnp.int32)


def levels(stream_key, dims, cuts, least, top_value):
    def one(dim, shards_of):
        steps = jax.random.uniform(jax.random.fold_in(jax.random.fold_in(stream_key, 6), dim), (shards_of,), jnp.float32, least / len(cuts), top_value / len(cuts))
        return jnp.repeat(jnp.exp(steps), dims[dim] // shards_of).reshape((-1,) + (1,) * (len(dims) - dim - 1))

    gain = one(*cuts[0])
    for cut in cuts[1:]:
        gain = gain * one(*cut)
    return gain


def scatter_about(key, extent, width, reach, cuts=(), held_as=jnp.bfloat16):
    entries = width * jax.random.normal(key, extent, jnp.float32)
    if cuts:
        entries = entries * levels(key, extent, cuts, -0.22, 0.18)
    return jnp.clip(entries, -reach, reach).astype(held_as)


def setup_inputs(seed: int = 0) -> dict:
    key_of = jax.random.split(jax.random.key(seed), 15)
    tokens = scatter_about(key_of[0], (TOKENS, D), 1.0, 6.0, ((0, 32),))
    grids = draw_grids(jax.random.fold_in(key_of[14], 71), 0)
    qkv_weight = scatter_about(key_of[2], (D, 3, D), D ** -0.5, 0.21875, ((2, 4),))
    qv_bias = scatter_about(key_of[3], (2, D), 0.1, 0.6, ((1, 4),), jnp.float32)
    rel_table = scatter_about(key_of[4], (HEADS, RELS), 1.0, 6.0, ((0, 4),), jnp.float32)
    proj_weight = scatter_about(key_of[5], (D, D), (max(D // 64, 4)) ** -0.5, 1.75, ((0, 4),))
    fc1_weight = scatter_about(key_of[6], (D, FF), D ** -0.5, 0.21875, ((1, 4),))
    fc1_bias = scatter_about(key_of[7], (FF,), 0.3, 1.796875, ((0, 4),))
    fc2_weight = scatter_about(key_of[8], (FF, D), FF ** -0.5, 0.109375, ((0, 4),))
    norm_gains = jnp.clip(1.0 + 0.15 * jax.random.normal(key_of[9], (2, D), jnp.float32), 0.25, 1.75)
    norm_biases = scatter_about(key_of[10], (2, D), 0.3, 1.8, (), jnp.float32)
    layer_scales = jnp.clip(jnp.exp(jax.random.uniform(key_of[11], (2, D), jnp.float32, math.log(0.5), math.log(2.0))), 0.5, 2.0)
    out_biases = scatter_about(key_of[12], (2, D), 0.3, 1.8, (), jnp.float32)
    cotangent = scatter_about(key_of[13], (TOKENS, D), 1.0, 6.0, ((0, 32),))
    return dict(tokens=tokens, grids=grids, qkv_weight=qkv_weight, qv_bias=qv_bias, rel_table=rel_table, proj_weight=proj_weight, fc1_weight=fc1_weight, fc1_bias=fc1_bias, fc2_weight=fc2_weight, norm_gains=norm_gains, norm_biases=norm_biases, layer_scales=layer_scales, out_biases=out_biases, cotangent=cotangent)


@jax.custom_vjp
def low(v):
    return lax.optimization_barrier(v.astype(jnp.bfloat16)).astype(jnp.float32)

@jax.custom_vjp
def low_back(v):
    return v

def low_keep(v):
    return (low(v), None)

def low_pass(kept, grad):
    return (grad,)

def back_keep(v):
    return (v, None)

def back_low(kept, grad):
    return (low(grad),)
low.defvjp(low_keep, low_pass)
low_back.defvjp(back_keep, back_low)
eps_norm = 1e-06
block_images = 4
highest = lax.Precision.HIGHEST

def normalize(values):
    center = values - lax.optimization_barrier(jnp.mean(values, axis=-1, keepdims=True))
    return center * lax.rsqrt(lax.optimization_barrier(jnp.mean(center * center, axis=-1, keepdims=True)) + eps_norm)

def token_layout(grid_sizes):
    position = jnp.arange(SEQ, dtype=jnp.int32)
    patch_index = position - 1
    is_patch = (position >= 1) & (patch_index < grid_sizes[0] * grid_sizes[1])
    clamped = jnp.where(is_patch, patch_index, 0).astype(jnp.int32)
    is_class = position == 0
    return (clamped // grid_sizes[1], clamped % grid_sizes[1], is_class, is_patch | is_class)

def relative_index(grid_row, grid_column, is_class):
    row_stride = 2 * GRID - 1
    inner = (grid_row[:, None] - grid_row[None, :] + GRID - 1) * row_stride + (grid_column[:, None] - grid_column[None, :] + GRID - 1)
    class_entry = row_stride * row_stride
    from_class = is_class[:, None] & jnp.logical_not(is_class[None, :])
    to_class = jnp.logical_not(is_class[:, None]) & is_class[None, :]
    class_pair = is_class[:, None] & is_class[None, :]
    return jnp.where(class_pair, class_entry + 2, jnp.where(from_class, class_entry, jnp.where(to_class, class_entry + 1, inner))).astype(jnp.int32)

def attend(rel_table, element):
    queries, keys_in, values_in, grid_sizes = element
    grid_row, grid_column, is_class, valid = token_layout(grid_sizes)
    rel_index = relative_index(grid_row, grid_column, is_class)
    logits = jnp.einsum('qhc,khc->hqk', queries, keys_in, precision=highest) + jnp.take(rel_table, rel_index, axis=1)
    logits = jnp.where(valid[None, None, :], low_back(logits), -1e+30)
    maximum = lax.optimization_barrier(jnp.max(logits, axis=-1, keepdims=True))
    raised = jnp.exp(logits - maximum)
    probabilities = raised / lax.optimization_barrier(jnp.sum(raised, axis=-1, keepdims=True))
    mixed_heads = jnp.einsum('hqk,khc->qhc', low(probabilities), values_in, precision=highest)
    return mixed_heads.reshape(SEQ, D)

def forward(inputs, grids, qkv_weight, qv_bias, rel_table, proj_weight, fc1_weight, fc1_bias, fc2_weight, norm_gains, norm_biases, layer_scales, out_biases):
    image_count = grids.shape[0]
    sent_one = low(normalize(inputs) * norm_gains[0] + norm_biases[0])
    projected = jnp.einsum('rd,dtc->rtc', sent_one, qkv_weight, precision=highest)
    queries = low(low_back((projected[:, 0] + qv_bias[0]) * 0.125))
    keys_in = low(low_back(projected[:, 1]))
    values_in = low(low_back(projected[:, 2] + qv_bias[1]))
    head_shape = (image_count, SEQ, HEADS, HEAD)
    mixed_heads = lax.map(jax.checkpoint(partial(attend, rel_table)), (queries.reshape(head_shape), keys_in.reshape(head_shape), values_in.reshape(head_shape), grids))
    mixed_heads = low(low_back(mixed_heads.reshape(image_count * SEQ, D)))
    branch_one = low_back(jnp.dot(mixed_heads, proj_weight, precision=highest)) + out_biases[0]
    after_one = inputs + layer_scales[0] * branch_one
    sent_two = low(normalize(after_one) * norm_gains[1] + norm_biases[1])
    hidden_pre = low_back(jnp.dot(sent_two, fc1_weight, precision=highest) + fc1_bias)
    hidden = low(jax.nn.gelu(hidden_pre, approximate=False))
    branch_two = low_back(jnp.dot(hidden, fc2_weight, precision=highest)) + out_biases[1]
    return after_one + layer_scales[1] * branch_two

def image_major(array):
    return jnp.transpose(array.reshape(N_DP, SEQ, IMGS, D), (0, 2, 1, 3)).reshape(IMAGES // block_images, block_images * SEQ, D)

def token_major(array):
    return jnp.transpose(array.reshape(N_DP, IMGS, SEQ, D), (0, 2, 1, 3)).reshape(TOKENS, D)

def reference(tokens, grids, qkv_weight, qv_bias, rel_table, proj_weight, fc1_weight, fc1_bias, fc2_weight, norm_gains, norm_biases, layer_scales, out_biases, cotangent):
    weights = tuple((entry.astype(jnp.float32) for entry in (qkv_weight, qv_bias, rel_table, proj_weight, fc1_weight, fc1_bias, fc2_weight, norm_gains, norm_biases, layer_scales, out_biases)))
    token_blocks = image_major(tokens)
    grad_blocks = image_major(cotangent)
    grid_blocks = grids.reshape(IMAGES // block_images, block_images, 2)

    def scan_step(totals, element):
        block_tokens, block_grids, block_grad = element

        def run_layer(inputs, *params):
            return forward(inputs, block_grids, *params)
        result, pullback = jax.vjp(run_layer, block_tokens.astype(jnp.float32), *weights)
        grads = pullback(block_grad.astype(jnp.float32))
        totals = tuple((summed + added for summed, added in zip(totals, grads[1:])))
        return (totals, (result.astype(jnp.bfloat16), grads[0]))
    initial = tuple((jnp.zeros_like(entry) for entry in weights))
    totals, (results, input_grads) = lax.scan(scan_step, initial, (token_blocks, grid_blocks, grad_blocks))
    return (token_major(results), token_major(input_grads), totals[0], totals[1], totals[2], totals[3], totals[4], totals[5], totals[6], totals[7], totals[8], totals[9], totals[10])
```

```python
import jax
import jax.numpy as jnp
from jax import lax
from jax.experimental import pallas as pl
from jax.experimental.pallas import tpu as pltpu
from jax.sharding import PartitionSpec as P

GRID = 22
SPAN = 2 * GRID - 1
CELLS = GRID * GRID
ENTRIES = SPAN * SPAN
MESH = pl.DeviceIdType.MESH
f32 = jnp.float32
bf16 = jnp.bfloat16
i32 = jnp.int32

eps_norm = 1e-06
masked = -1e30
NT = 4
CHIPS = 4
CORES = 2
GROUP = CHIPS * CORES
TABLE = 1920
WIDE = 1024
SMALL = 24
REP = 8


def dot(left, right):
    return lax.dot_general(left, right, (((1,), (0,)), ((), ())), preferred_element_type=f32)


def dot_nt(left, right):
    return lax.dot_general(left, right, (((1,), (1,)), ((), ())), preferred_element_type=f32)


def dot_tn(left, right):
    return lax.dot_general(left, right, (((0,), (0,)), ((), ())), preferred_element_type=f32)


def normalize(values):
    center = values - jnp.mean(values, axis=-1, keepdims=True)
    inverse = lax.rsqrt(jnp.mean(center * center, axis=-1, keepdims=True) + eps_norm)
    return center * inverse, inverse


def norm_back(grad_normed, normed, inverse):
    average = jnp.mean(grad_normed, axis=-1, keepdims=True)
    crossed = jnp.mean(grad_normed * normed, axis=-1, keepdims=True)
    return inverse * (grad_normed - average - normed * crossed)


def split_cell(place):
    row = (place * 2979) >> 16
    return row, place - row * GRID


def query_tokens(place, high, wide):
    row, back = split_cell(place)
    inside = (place < CELLS) & (row < high) & (GRID - 1 - back < wide)
    before = jnp.minimum(row, high) * wide + jnp.where(
        row < high, jnp.maximum(back - (GRID - wide), 0), 0
    )
    token = jnp.where(inside, 1 + row * wide + (GRID - 1 - back), high * wide + 1 + place - before)
    token = jnp.where(place == CELLS, 0, jnp.where(place > CELLS, place, token))
    padding = jnp.logical_not(inside) & (place != CELLS)
    return token, padding


def key_tokens(place, high, wide):
    row, back = split_cell(place)
    row = GRID - 1 - row
    column = GRID - 1 - back
    inside = (place < CELLS) & (row < high) & (column < wide)
    token = jnp.where(inside, 1 + row * wide + column, -1)
    return jnp.where(place == CELLS, 0, token)


def one_hot(left, right):
    return jnp.where(left == right, 1.0, 0.0).astype(bf16)


def main_kernel(
    grids, x_in, cot_in, wqkv_hbm, wproj_hbm, w1_hbm, w2_hbm, qvb, rel, b1, gains, biases, scales, obias,
    out, ingrad, summed, small_out, table_out,
    wqkv, wproj, w1, w2, w_sem,
    xg, dzg, z1r, n2g, dn2r, z2r, dz1g, dn1r,
    stage_a, stage_b, stage_c, stage_d,
    z_send, z_recv,
    mq, mqt, mk, mkt, bias, trow, gexp, uexp,
    n1g, qt, kt, vt, qh, kh, vh, prob, probb, op, ot,
    x1, xhat2, inv2, a1, dx1, own, dn2own,
    hid, du, dot_t, doh, ds, dsf, dqp, dkp, dvp, dqt, dkt, dvt,
    tab, sums, gbuf, d1, half, d2, d_send, d_recv, smr, sm_send, sm_recv, zmr,
):
    dp = lax.axis_index("dp")
    t = lax.axis_index("tensor")
    seq = x_in.shape[0] * NT
    rows = x_in.shape[0]
    width = x_in.shape[1]
    heads = rel.shape[0]
    hw = heads * 64
    base = (dp // GROUP) * GROUP
    mine = dp % GROUP
    chip = mine // CORES
    core = mine % CORES

    def in_plane(chip_index, core_index):
        return (base + chip_index * CORES + core_index, t)

    order = [t, t + 1 - 2 * (t % 2), 2 - t // 2, 3 - 3 * (t // 2)]

    loads = [
        pltpu.make_async_copy(src, dst, w_sem.at[i])
        for i, (src, dst) in enumerate(
            [(wqkv_hbm, wqkv), (wproj_hbm, wproj), (w1_hbm, w1), (w2_hbm, w2)]
        )
    ]
    for load in loads:
        load.start()

    barrier = pltpu.get_barrier_semaphore()
    for k in range(1, NT):
        pl.semaphore_signal(barrier, inc=1, device_id=(dp, (t + k) % NT), device_id_type=MESH)
    for k in range(1, GROUP):
        pl.semaphore_signal(barrier, inc=1, device_id=(base + (mine + k) % GROUP, t), device_id_type=MESH)
    pl.semaphore_wait(barrier, NT - 1 + GROUP - 1)

    def block(s):
        return pl.ds(pl.multiple_of(s * rows, rows), rows)

    def gather_copy(phase, buf, dst):
        return pltpu.make_async_remote_copy(
            src_ref=buf.at[t], dst_ref=buf.at[t],
            send_sem=z_send.at[phase, dst], recv_sem=z_recv.at[phase, t],
            device_id=(dp, dst), device_id_type=MESH,
        )

    def scatter_copy(phase, stage, buf, dst):
        return pltpu.make_async_remote_copy(
            src_ref=stage.at[dst], dst_ref=buf.at[t],
            send_sem=z_send.at[phase, dst], recv_sem=z_recv.at[phase, t],
            device_id=(dp, dst), device_id_type=MESH,
        )

    def arrived(phase, buf, src):
        pltpu.make_async_remote_copy(
            src_ref=buf.at[src], dst_ref=buf.at[src],
            send_sem=z_send.at[phase, src], recv_sem=z_recv.at[phase, src],
            device_id=(dp, src), device_id_type=MESH,
        ).wait_recv()

    xg[t] = x_in[...]
    for dst in order[1:]:
        gather_copy(0, xg, dst).start()
    cot = cot_in[...].astype(f32)
    dzg[t] = (cot * scales[1:2, :]).astype(bf16)

    high = grids[0, 0]
    wide = grids[0, 1]
    down = lax.broadcasted_iota(i32, (seq, 1), 0)
    across = lax.broadcasted_iota(i32, (1, seq), 1)
    token_q, pad_q = query_tokens(down, high, wide)
    token_q_across, _ = query_tokens(across, high, wide)
    token_k = key_tokens(down, high, wide)
    token_k_across = key_tokens(across, high, wide)
    mq[...] = one_hot(token_q, across)
    mqt[...] = one_hot(down, token_q_across)
    mk[...] = one_hot(token_k, across)
    mkt[...] = one_hot(down, token_k_across)

    trow[...] = jnp.zeros_like(trow)
    trow[0:heads, 0 : ENTRIES + 3] = rel[...]
    gexp[...] = jnp.zeros_like(gexp)
    for h in range(heads):
        table = trow[h : h + 1, :]
        spread = pltpu.roll(jnp.broadcast_to(table, (24, TABLE)), TABLE - (GRID - 1), 1)
        uexp[...] = pltpu.roll(spread, 0, 1, stride=1, stride_axis=0)
        for x in range(SPAN):
            gexp[:, x * GRID : (x + 1) * GRID] = uexp[:, x * SPAN : x * SPAN + GRID]
        hankel = gexp[...]
        for r in range(GRID):
            moved = hankel if r == 0 else pltpu.roll(hankel, WIDE - r * GRID, 1)
            bias[h, r * GRID : (r + 1) * GRID, :] = moved[0:GRID, 0:seq]
        bias[h, CELLS:seq, :] = jnp.zeros((seq - CELLS, seq), f32)
        origin = bias[h, GRID - 1 : GRID, :]
        from_class = table[:, ENTRIES : ENTRIES + 1]
        to_class = table[:, ENTRIES + 1 : ENTRIES + 2]
        class_pair = table[:, ENTRIES + 2 : ENTRIES + 3]

        def settle(i, carry):
            part = pl.ds(pl.multiple_of(i * 128, 128), 128)
            place = lax.broadcasted_iota(i32, (128, 1), 0) + i * 128
            _, padded = query_tokens(place, high, wide)
            values = jnp.where(padded, origin, bias[h, part, :])
            values = jnp.where(across == CELLS, to_class, values)
            values = jnp.where(
                place == CELLS, jnp.where(across == CELLS, class_pair, from_class), values
            )
            bias[h, part, :] = jnp.where(token_k_across >= 0, values, masked)
            return carry

        lax.fori_loop(0, seq // 128, settle, 0)

    loads[0].wait()
    gain_one, shift_one = gains[0:1, :], biases[0:1, :]
    for step, s in enumerate(order):
        if step > 0:
            arrived(0, xg, s)
        normed, _ = normalize(xg[s].astype(f32))
        sent = (normed * gain_one + shift_one).astype(bf16)
        part = block(s)
        n1g[part, :] = sent
        qt[part, :] = ((dot_nt(sent, wqkv[0:hw, :]) + qvb[0:1, :]) * 0.125).astype(bf16)
        kt[part, :] = dot_nt(sent, wqkv[hw : 2 * hw, :]).astype(bf16)
        vt[part, :] = (dot_nt(sent, wqkv[2 * hw : 3 * hw, :]) + qvb[1:2, :]).astype(bf16)
    for dst in order[1:]:
        gather_copy(1, dzg, dst).start()

    queries = dot(mq[...], qt[...]).astype(bf16)
    keys = dot(mk[...], kt[...]).astype(bf16)
    values = dot(mk[...], vt[...]).astype(bf16)
    for h in range(heads):
        lanes = slice(h * 64, (h + 1) * 64)
        qh[h] = queries[:, lanes]
        kh[h] = keys[:, lanes]
        vh[h] = values[:, lanes]
    for h in range(heads):

        def attend(i, carry):
            part = pl.ds(pl.multiple_of(i * 128, 128), 128)
            logits = dot_nt(qh[h, part, :], kh[h]) + bias[h, part, :]
            raised = jnp.exp(logits - jnp.max(logits, axis=-1, keepdims=True))
            weights = raised * (1.0 / jnp.sum(raised, axis=-1, keepdims=True))
            prob[h, part, :] = weights
            rounded = weights.astype(bf16)
            probb[h, part, :] = rounded
            op[part, h * 64 : (h + 1) * 64] = dot(rounded, vh[h]).astype(bf16)
            return carry

        lax.fori_loop(0, seq // 128, attend, 0)
    ot[...] = dot(mqt[...], op[...]).astype(bf16)

    loads[1].wait()
    for s in order[::-1]:
        piece = dot(ot[block(s), :], wproj[...])
        if s is t:
            own[...] = piece
        else:
            stage_a[s] = piece.astype(bf16)
            scatter_copy(2, stage_a, z1r, s).start()
    total = own[...]
    for s in order[1:]:
        arrived(2, z1r, s)
        total = total + z1r[s].astype(f32)
    branch_one = total + obias[0:1, :]
    a1[...] = branch_one
    after_one = x_in[...].astype(f32) + scales[0:1, :] * branch_one
    x1[...] = after_one
    normed, inverse = normalize(after_one)
    xhat2[...] = normed
    inv2[...] = jnp.broadcast_to(inverse, inv2.shape)
    n2g[t] = (normed * gains[1:2, :] + biases[1:2, :]).astype(bf16)
    for dst in order[1:]:
        gather_copy(3, n2g, dst).start()

    loads[2].wait()
    loads[3].wait()
    shift_up = b1[...].astype(f32)
    bias_up = jnp.zeros((1, w1.shape[1]), f32)
    for step, s in enumerate(order):
        if step > 0:
            arrived(1, dzg, s)
            arrived(3, n2g, s)
        part = block(s)
        before = dot(n2g[s], w1[...]) + shift_up
        cumulative = 0.5 * (1.0 + lax.erf(before * 0.7071067811865476))
        slope = cumulative + before * (jnp.exp(-0.5 * before * before) * 0.3989422804014327)
        hid[part, :] = (before * cumulative).astype(bf16)
        grad_pre = (dot_nt(dzg[s], w2[...]) * slope).astype(bf16)
        du[part, :] = grad_pre
        bias_up = bias_up + jnp.sum(grad_pre.astype(f32), axis=0, keepdims=True)
        back = dot_nt(grad_pre, w1[...])
        if step == 0:
            dn2own[...] = back
        else:
            stage_b[s] = back.astype(bf16)
            scatter_copy(4, stage_b, dn2r, s).start()
    for step, s in enumerate(order):
        piece = dot(hid[block(s), :], w2[...])
        if step == 0:
            own[...] = piece
        else:
            stage_c[s] = piece.astype(bf16)
            scatter_copy(5, stage_c, z2r, s).start()

    total = dn2own[...]
    for s in order[1:]:
        arrived(4, dn2r, s)
        total = total + dn2r[s].astype(f32)
    normed = xhat2[...]
    sums[3:4, :] = jnp.sum(total, axis=0, keepdims=True)
    sums[1:2, :] = jnp.sum(total * normed, axis=0, keepdims=True)
    cot = cot_in[...].astype(f32)
    after = cot + norm_back(total * gains[1:2, :], normed, inv2[:, 0:1])
    dx1[...] = after
    sums[4:5, :] = jnp.sum(after * a1[...], axis=0, keepdims=True)
    branch = after * scales[0:1, :]
    sums[6:7, :] = jnp.sum(branch, axis=0, keepdims=True)
    dz1g[t] = branch.astype(bf16)
    for dst in order[1:]:
        gather_copy(6, dz1g, dst).start()

    ff = w1.shape[1]
    down_rows = jnp.reshape(dzg[...], (seq, width))
    gbuf[0:ff, :] = dot_tn(hid[...], down_rows).astype(bf16)
    up_rows = jnp.reshape(n2g[...], (seq, width))
    gbuf[ff : ff + width, :] = dot_tn(up_rows, du[...]).astype(bf16)

    for step, s in enumerate(order):
        if step > 0:
            arrived(6, dz1g, s)
        dot_t[block(s), :] = dot_nt(dz1g[s], wproj[...]).astype(bf16)
    grad_mixed = dot(mq[...], dot_t[...]).astype(bf16)
    for h in range(heads):
        doh[h] = grad_mixed[:, h * 64 : (h + 1) * 64]
    proj_at = ff + width
    gbuf[proj_at : proj_at + hw, :] = dot_tn(ot[...], jnp.reshape(dz1g[...], (seq, width))).astype(bf16)
    row24 = lax.broadcasted_iota(i32, (24, 1), 0)
    lane_t = lax.broadcasted_iota(i32, (1, TABLE), 1)
    uexp[...] = jnp.zeros_like(uexp)
    gexp[...] = jnp.zeros_like(gexp)
    for h in range(heads):
        lanes = slice(h * 64, (h + 1) * 64)

        def attend_back(i, carry):
            class_row, class_column, pad_row = carry
            part = pl.ds(pl.multiple_of(i * 128, 128), 128)
            place = lax.broadcasted_iota(i32, (128, 1), 0) + i * 128
            _, padded = query_tokens(place, high, wide)
            grad_prob = dot_nt(doh[h, part, :], vh[h])
            weights = prob[h, part, :]
            crossed = jnp.sum(weights * grad_prob, axis=-1, keepdims=True)
            rounded = (weights * (grad_prob - crossed)).astype(bf16)
            ds[part, :] = rounded
            dqp[part, lanes] = dot(rounded, kh[h]).astype(bf16) * 0.125
            wide_grad = rounded.astype(f32)
            class_row = class_row + jnp.sum(
                jnp.where(place == CELLS, wide_grad, 0.0), axis=0, keepdims=True
            )
            class_column = class_column + jnp.sum(
                jnp.where((place != CELLS) & (across == CELLS), wide_grad, 0.0), axis=0, keepdims=True
            )
            cells = jnp.where(across < CELLS, wide_grad, 0.0)
            pad_row = pad_row + jnp.sum(jnp.where(padded, cells, 0.0), axis=0, keepdims=True)
            dsf[part, :] = jnp.where(padded, 0.0, cells)
            return class_row, class_column, pad_row

        zero = jnp.zeros((1, seq), f32)
        class_row, class_column, pad_row = lax.fori_loop(0, seq // 128, attend_back, (zero, zero, zero))
        dvp[:, lanes] = dot_tn(probb[h], doh[h]).astype(bf16)
        dkp[:, lanes] = dot_tn(ds[...], qh[h]).astype(bf16)
        blank = jnp.zeros((24, WIDE - seq), f32)
        folded = jnp.zeros((24, WIDE), f32)
        for r in range(GRID):
            cells = jnp.concatenate([dsf[r * GRID : r * GRID + 24, :], blank], axis=1)
            folded = folded + (cells if r == 0 else pltpu.roll(cells, r * GRID, 1))
        padded_row = jnp.concatenate([pad_row, jnp.zeros((1, WIDE - seq), f32)], axis=1)
        folded = jnp.where(row24 < GRID, folded, 0.0) + jnp.where(row24 == GRID - 1, padded_row, 0.0)
        for i in range(GRID):
            gexp[GRID - 1 - i : GRID - i, :] = folded[i : i + 1, :]
        for x in range(SPAN):
            uexp[:, x * SPAN : x * SPAN + GRID] = gexp[:, x * GRID : (x + 1) * GRID]
        lined = pltpu.roll(uexp[...], 0, 1, stride=1, stride_axis=0)
        table = jnp.sum(lined, axis=0, keepdims=True)
        from_class = jnp.sum(jnp.where(across != CELLS, class_row, 0.0), axis=1, keepdims=True)
        class_pair = jnp.sum(jnp.where(across == CELLS, class_row, 0.0), axis=1, keepdims=True)
        to_class = jnp.sum(class_column, axis=1, keepdims=True)
        table = jnp.where(lane_t == ENTRIES, from_class, table)
        table = jnp.where(lane_t == ENTRIES + 1, to_class, table)
        tab[h : h + 1, :] = jnp.where(lane_t == ENTRIES + 2, class_pair, table)

    dqt[...] = dot(mqt[...], dqp[...]).astype(bf16)
    dkt[...] = dot(mkt[...], dkp[...]).astype(bf16)
    dvt[...] = dot(mkt[...], dvp[...]).astype(bf16)

    shift_total = jnp.zeros((1, width), f32)
    gain_total = jnp.zeros((1, width), f32)
    for s in order[::-1]:
        part = block(s)
        piece = dot(dqt[part, :], wqkv[0:hw, :]) + dot(dkt[part, :], wqkv[hw : 2 * hw, :])
        piece = piece + dot(dvt[part, :], wqkv[2 * hw : 3 * hw, :])
        normed, _ = normalize(xg[s].astype(f32))
        shift_total = shift_total + jnp.sum(piece, axis=0, keepdims=True)
        gain_total = gain_total + jnp.sum(piece * normed, axis=0, keepdims=True)
        if s is t:
            dn2own[...] = piece
        else:
            stage_d[s] = piece.astype(bf16)
            scatter_copy(7, stage_d, dn1r, s).start()
    sums[2:3, :] = shift_total
    sums[0:1, :] = gain_total
    sums[8:9, :] = bias_up
    wide_q = jnp.sum(dqt[...].astype(f32), axis=0, keepdims=True)
    wide_v = jnp.sum(dvt[...].astype(f32), axis=0, keepdims=True)
    sums[9:10, 0:hw] = wide_q
    sums[10:11, 0:hw] = wide_v
    sums[9:11, hw:width] = jnp.zeros((2, width - hw), f32)
    for h in range(heads):
        sums[11 + 3 * h : 12 + 3 * h, :] = tab[h : h + 1, 0:width]
        sums[12 + 3 * h : 13 + 3 * h, :] = tab[h : h + 1, width : 2 * width]
        sums[13 + 3 * h : 14 + 3 * h, 0 : TABLE - 2 * width] = tab[h : h + 1, 2 * width : TABLE]
        sums[13 + 3 * h : 14 + 3 * h, TABLE - 2 * width : width] = jnp.zeros(
            (1, 3 * width - TABLE), f32
        )
    sums[11 + 3 * heads : SMALL, :] = jnp.zeros((SMALL - 11 - 3 * heads, width), f32)

    qkv_at = proj_at + hw
    gbuf[qkv_at : qkv_at + hw, :] = dot_tn(dqt[...], n1g[...]).astype(bf16)
    gbuf[qkv_at + hw : qkv_at + 2 * hw, :] = dot_tn(dkt[...], n1g[...]).astype(bf16)
    gbuf[qkv_at + 2 * hw : qkv_at + 3 * hw, :] = dot_tn(dvt[...], n1g[...]).astype(bf16)

    total = own[...]
    for s in order[1:]:
        arrived(5, z2r, s)
        total = total + z2r[s].astype(f32)
    branch_two = total + obias[1:2, :]
    out[...] = (x1[...] + scales[1:2, :] * branch_two).astype(bf16)
    cot = cot_in[...].astype(f32)
    sums[5:6, :] = jnp.sum(cot * branch_two, axis=0, keepdims=True)
    sums[7:8, :] = jnp.sum(cot * scales[1:2, :], axis=0, keepdims=True)

    def small_copy(k):
        return pltpu.make_async_remote_copy(
            src_ref=sums, dst_ref=smr.at[k - 1],
            send_sem=sm_send.at[k - 1], recv_sem=sm_recv.at[k - 1],
            device_id=(base + (mine + k) % GROUP, t), device_id_type=MESH,
        )

    for k in range(1, GROUP):
        small_copy(k).start()

    half_width = width // 2
    total_rows = gbuf.shape[0]
    my_lanes = pl.ds(pl.multiple_of(core * half_width, half_width), half_width)
    your_lanes = pl.ds(pl.multiple_of((1 - core) * half_width, half_width), half_width)
    segments = [(0, 2 * width), (2 * width, hw), (2 * width + hw, 3 * hw)]

    def core_copy(i):
        start, count = segments[i]
        return pltpu.make_async_remote_copy(
            src_ref=gbuf.at[start : start + count, your_lanes], dst_ref=d1.at[start : start + count, :],
            send_sem=d_send.at[i, 0], recv_sem=d_recv.at[i, 0],
            device_id=in_plane(chip, 1 - core), device_id_type=MESH,
        )

    def chip_rows(i, which):
        start, count = segments[i]
        return pl.ds(pl.multiple_of(start + which * (count // CHIPS), 16), count // CHIPS)

    def chip_copy(i, k):
        start, count = segments[i]
        to = (chip + k) % CHIPS
        return pltpu.make_async_remote_copy(
            src_ref=half.at[chip_rows(i, to), :],
            dst_ref=d2.at[k - 1, start // CHIPS : (start + count) // CHIPS, :],
            send_sem=d_send.at[i, k], recv_sem=d_recv.at[i, k],
            device_id=in_plane(to, core), device_id_type=MESH,
        )

    def back_copy(i, k):
        to = (chip + k) % CHIPS
        spot = summed.at[chip_rows(i, chip), my_lanes]
        return pltpu.make_async_remote_copy(
            src_ref=spot, dst_ref=spot,
            send_sem=d_send.at[i, 3 + k], recv_sem=d_recv.at[i, 3 + k],
            device_id=in_plane(to, core), device_id_type=MESH,
        )

    def back_arrived(i, k):
        spot = summed.at[chip_rows(i, (chip + CHIPS - k) % CHIPS), my_lanes]
        pltpu.make_async_remote_copy(
            src_ref=spot, dst_ref=spot,
            send_sem=d_send.at[i, 3 + k], recv_sem=d_recv.at[i, 3 + k],
            device_id=in_plane(chip, 1 - core), device_id_type=MESH,
        ).wait_recv()

    def pair_copy(i):
        start, count = segments[i]
        spot = summed.at[start : start + count, my_lanes]
        return pltpu.make_async_remote_copy(
            src_ref=spot, dst_ref=spot,
            send_sem=d_send.at[i, 7], recv_sem=d_recv.at[i, 7],
            device_id=in_plane(chip, 1 - core), device_id_type=MESH,
        )

    def pair_arrived(i):
        start, count = segments[i]
        spot = summed.at[start : start + count, your_lanes]
        pltpu.make_async_remote_copy(
            src_ref=spot, dst_ref=spot,
            send_sem=d_send.at[i, 7], recv_sem=d_recv.at[i, 7],
            device_id=in_plane(chip, 1 - core), device_id_type=MESH,
        ).wait_recv()

    tile = 48
    count_segments = range(len(segments))
    for i in count_segments:
        core_copy(i).start()
    for i in count_segments:
        start, count = segments[i]
        core_copy(i).wait_recv()

        def add_core(j, carry):
            part = pl.ds(pl.multiple_of(start + j * tile, 16), tile)
            half[part, :] = (gbuf[part, my_lanes].astype(f32) + d1[part, :].astype(f32)).astype(bf16)
            return carry

        lax.fori_loop(0, count // tile, add_core, 0)
        for k in range(1, CHIPS):
            chip_copy(i, k).start()
    for i in count_segments:
        start, count = segments[i]
        for k in range(1, CHIPS):
            chip_copy(i, k).wait_recv()

        def add_chips(j, carry):
            part = pl.ds(pl.multiple_of(start + chip * (count // CHIPS) + j * tile, 16), tile)
            spot = pl.ds(pl.multiple_of(start // CHIPS + j * tile, 16), tile)
            value = half[part, :].astype(f32)
            for k in range(1, CHIPS):
                value = value + d2[k - 1, spot, :].astype(f32)
            summed[part, my_lanes] = value.astype(bf16)
            return carry

        lax.fori_loop(0, count // CHIPS // tile, add_chips, 0)
        for k in range(1, CHIPS):
            back_copy(i, k).start()

    total = dn2own[...]
    for s in order[1:]:
        arrived(7, dn1r, s)
        total = total + dn1r[s].astype(f32)
    normed, inverse = normalize(x_in[...].astype(f32))
    ingrad[...] = dx1[...] + norm_back(total * gain_one, normed, inverse)

    value = sums[...]
    for k in range(1, GROUP):
        small_copy(k).wait_recv()
        value = value + smr[k - 1]
    zmr[t] = value[0:REP, :]

    def small_tensor(dst):
        return pltpu.make_async_remote_copy(
            src_ref=zmr.at[t], dst_ref=zmr.at[t],
            send_sem=z_send.at[8, dst], recv_sem=z_recv.at[8, t],
            device_id=(dp, dst), device_id_type=MESH,
        )

    for dst in order[1:]:
        small_tensor(dst).start()
    small_out[...] = value

    for i in count_segments:
        for k in range(1, CHIPS):
            back_arrived(i, k)
        pair_copy(i).start()
    for s in order[1:]:
        arrived(8, zmr, s)
    small_out[0:REP, :] = zmr[0] + zmr[1] + zmr[2] + zmr[3]
    for h in range(heads):
        for j in range(3):
            lanes = min(width, ENTRIES + 3 - j * width)
            table_out[h : h + 1, j * width : j * width + lanes] = small_out[
                11 + 3 * h + j : 12 + 3 * h + j, 0:lanes
            ]
    for i in count_segments:
        pair_arrived(i)

    for dst in order[1:]:
        gather_copy(0, xg, dst).wait_send()
        gather_copy(1, dzg, dst).wait_send()
        scatter_copy(2, stage_a, z1r, dst).wait_send()
        gather_copy(3, n2g, dst).wait_send()
        scatter_copy(4, stage_b, dn2r, dst).wait_send()
        scatter_copy(5, stage_c, z2r, dst).wait_send()
        gather_copy(6, dz1g, dst).wait_send()
        scatter_copy(7, stage_d, dn1r, dst).wait_send()
        small_tensor(dst).wait_send()
    for k in range(1, GROUP):
        small_copy(k).wait_send()
    for i in count_segments:
        core_copy(i).wait_send()
        for k in range(1, CHIPS):
            chip_copy(i, k).wait_send()
            back_copy(i, k).wait_send()
        pair_copy(i).wait_send()


def finish_kernel(
    summed, out_in, ingrad_in, small, table_in,
    out, ingrad, g_qkv, g_qv, g_table, g_proj, g_up, g_up_bias, g_down, g_gains, g_shifts, g_scales, g_biases,
):
    ff, width = g_down.shape
    hw = g_proj.shape[0]
    out[...] = out_in[...]
    ingrad[...] = ingrad_in[...]
    g_down[...] = summed[0:ff, :].astype(f32)
    g_up[...] = summed[ff : ff + width, :].astype(f32)
    g_proj[...] = summed[ff + width : ff + width + hw, :].astype(f32)
    g_qkv[...] = summed[ff + width + hw :, :].astype(f32)
    g_gains[...] = small[0:2, :]
    g_shifts[...] = small[2:4, :]
    g_scales[...] = small[4:6, :]
    g_biases[...] = small[6:8, :]
    g_up_bias[...] = small[8:9, :]
    g_qv[...] = small[9:11, 0:hw]
    g_table[...] = table_in[...]


def per_device(
    n_dp, tokens, grids, qkv_weight, qv_bias, rel_table, proj_weight, fc1_weight, fc1_bias, fc2_weight,
    norm_gains, norm_biases, layer_scales, out_biases, cotangent,
):
    rows, width = tokens.shape
    seq = rows * NT
    heads, entries = rel_table.shape
    hw = heads * 64
    ff = fc1_weight.shape[1]
    qkv_rows = jnp.transpose(qkv_weight, (1, 2, 0)).reshape(3 * hw, width)
    total_rows = ff + width + 4 * hw
    vm = pl.BlockSpec(memory_space=pltpu.VMEM)
    anywhere = pl.BlockSpec(memory_space=pl.ANY)
    scratch = [
        pltpu.VMEM((3 * hw, width), bf16), pltpu.VMEM((hw, width), bf16),
        pltpu.VMEM((width, ff), bf16), pltpu.VMEM((ff, width), bf16), pltpu.SemaphoreType.DMA((4,)),
    ]
    scratch += [pltpu.VMEM((NT, rows, width), bf16)] * 12
    scratch += [pltpu.SemaphoreType.DMA((9, NT)), pltpu.SemaphoreType.DMA((9, NT))]
    scratch += [pltpu.VMEM((seq, seq), bf16)] * 4
    scratch += [
        pltpu.VMEM((heads, seq, seq), f32), pltpu.VMEM((8, TABLE), f32),
        pltpu.VMEM((24, WIDE), f32), pltpu.VMEM((24, TABLE), f32),
    ]
    scratch += [pltpu.VMEM((seq, width), bf16)] + [pltpu.VMEM((seq, hw), bf16)] * 3
    scratch += [pltpu.VMEM((heads, seq, 64), bf16)] * 3
    scratch += [pltpu.VMEM((heads, seq, seq), f32), pltpu.VMEM((heads, seq, seq), bf16)]
    scratch += [pltpu.VMEM((seq, hw), bf16)] * 2
    scratch += [pltpu.VMEM((rows, width), f32)] * 2 + [pltpu.VMEM((rows, 128), f32)]
    scratch += [pltpu.VMEM((rows, width), f32)] * 4
    scratch += [pltpu.VMEM((seq, ff), bf16)] * 2
    scratch += [pltpu.VMEM((seq, hw), bf16), pltpu.VMEM((heads, seq, 64), bf16)]
    scratch += [pltpu.VMEM((seq, seq), bf16), pltpu.VMEM((seq, seq), f32)]
    scratch += [pltpu.VMEM((seq, hw), bf16)] * 6
    scratch += [
        pltpu.VMEM((8, TABLE), f32), pltpu.VMEM((SMALL, width), f32),
        pltpu.VMEM((total_rows, width), bf16), pltpu.VMEM((total_rows, width // 2), bf16),
        pltpu.VMEM((total_rows, width // 2), bf16),
        pltpu.VMEM((CHIPS - 1, total_rows // CHIPS, width // 2), bf16),
        pltpu.SemaphoreType.DMA((3, 8)), pltpu.SemaphoreType.DMA((3, 8)),
        pltpu.VMEM((GROUP - 1, SMALL, width), f32),
        pltpu.SemaphoreType.DMA((GROUP - 1,)), pltpu.SemaphoreType.DMA((GROUP - 1,)),
        pltpu.VMEM((NT, REP, width), f32),
    ]
    output, input_grad, summed, small, table = pl.pallas_call(
        main_kernel,
        out_shape=(
            jax.ShapeDtypeStruct((rows, width), bf16),
            jax.ShapeDtypeStruct((rows, width), f32),
            jax.ShapeDtypeStruct((total_rows, width), bf16),
            jax.ShapeDtypeStruct((SMALL, width), f32),
            jax.ShapeDtypeStruct((heads, entries), f32),
        ),
        in_specs=[pl.BlockSpec(memory_space=pltpu.SMEM), vm, vm]
        + [anywhere] * 4
        + [vm] * 7,
        out_specs=(vm,) * 5,
        scratch_shapes=scratch,
        compiler_params=pltpu.CompilerParams(
            collective_id=0, has_side_effects=True, vmem_limit_bytes=60 << 20
        ),
        name="layer",
    )(
        grids, tokens, cotangent, qkv_rows, proj_weight, fc1_weight, fc2_weight,
        qv_bias, rel_table, fc1_bias.reshape(1, ff), norm_gains, norm_biases, layer_scales, out_biases,
    )
    pair = jax.ShapeDtypeStruct((2, width), f32)
    results = pl.pallas_call(
        finish_kernel,
        out_shape=(
            jax.ShapeDtypeStruct((rows, width), bf16),
            jax.ShapeDtypeStruct((rows, width), f32),
            jax.ShapeDtypeStruct((3 * hw, width), f32),
            jax.ShapeDtypeStruct((2, hw), f32),
            jax.ShapeDtypeStruct((heads, entries), f32),
            jax.ShapeDtypeStruct((hw, width), f32),
            jax.ShapeDtypeStruct((width, ff), f32),
            jax.ShapeDtypeStruct((1, ff), f32),
            jax.ShapeDtypeStruct((ff, width), f32),
            pair, pair, pair, pair,
        ),
        in_specs=[vm] * 5,
        out_specs=(vm,) * 13,
        compiler_params=pltpu.CompilerParams(vmem_limit_bytes=40 << 20),
        name="finish",
    )(summed, output, input_grad, small, table)
    results = list(results)
    stride = GROUP
    while stride < n_dp:
        hops = [(i, i ^ stride) for i in range(n_dp)]
        results[2:] = [value + lax.ppermute(value, "dp", hops) for value in results[2:]]
        stride *= 2
    results[2] = jnp.transpose(results[2].reshape(3, hw, width), (2, 0, 1))
    results[7] = results[7].reshape(ff)
    return tuple(results)


def solution(mesh):
    n_dp = mesh.shape["dp"]
    blocks = P(("dp", "tensor"), None)
    placed = (
        blocks, P("dp", None), P(None, None, "tensor"), P(None, "tensor"), P("tensor", None), P("tensor", None),
        P(None, "tensor"), P("tensor"), P("tensor", None), P(), P(), P(), P(), blocks,
    )
    given = (
        blocks, blocks, P(None, None, "tensor"), P(None, "tensor"), P("tensor", None), P("tensor", None),
        P(None, "tensor"), P("tensor"), P("tensor", None), P(), P(), P(), P(),
    )

    def layer(*arrays):
        return per_device(n_dp, *arrays)

    return jax.shard_map(layer, mesh=mesh, in_specs=placed, out_specs=given, check_vma=False)
```

```python
import jax
import jax.numpy as jnp
from jax import lax
from jax.experimental import pallas as pl
from jax.experimental.pallas import tpu as pltpu
from jax.sharding import PartitionSpec as P

GRID = 22
SPAN = 2 * GRID - 1
CELLS = GRID * GRID
ENTRIES = SPAN * SPAN
MESH = pl.DeviceIdType.MESH
f32 = jnp.float32
bf16 = jnp.bfloat16
i32 = jnp.int32

eps_norm = 1e-06
masked = -1e30
NT = 4
CHIPS = 4
CORES = 2
GROUP = CHIPS * CORES
TABLE = 1920
WIDE = 1024
SMALL = 64
REP = 8


def dot(left, right):
    return lax.dot_general(left, right, (((1,), (0,)), ((), ())), preferred_element_type=f32)


def dot_nt(left, right):
    return lax.dot_general(left, right, (((1,), (1,)), ((), ())), preferred_element_type=f32)


def dot_tn(left, right):
    return lax.dot_general(left, right, (((0,), (0,)), ((), ())), preferred_element_type=f32)


def normalize(values):
    center = values - jnp.mean(values, axis=-1, keepdims=True)
    inverse = lax.rsqrt(jnp.mean(center * center, axis=-1, keepdims=True) + eps_norm)
    return center * inverse, inverse


def norm_back(grad_normed, normed, inverse):
    average = jnp.mean(grad_normed, axis=-1, keepdims=True)
    crossed = jnp.mean(grad_normed * normed, axis=-1, keepdims=True)
    return inverse * (grad_normed - average - normed * crossed)


def split_cell(place):
    row = (place * 2979) >> 16
    return row, place - row * GRID


def query_tokens(place, high, wide):
    row, back = split_cell(place)
    inside = (place < CELLS) & (row < high) & (GRID - 1 - back < wide)
    before = jnp.minimum(row, high) * wide + jnp.where(
        row < high, jnp.maximum(back - (GRID - wide), 0), 0
    )
    token = jnp.where(inside, 1 + row * wide + (GRID - 1 - back), high * wide + 1 + place - before)
    token = jnp.where(place == CELLS, 0, jnp.where(place > CELLS, place, token))
    padding = jnp.logical_not(inside) & (place != CELLS)
    return token, padding


def key_tokens(place, high, wide):
    row, back = split_cell(place)
    row = GRID - 1 - row
    column = GRID - 1 - back
    inside = (place < CELLS) & (row < high) & (column < wide)
    token = jnp.where(inside, 1 + row * wide + column, -1)
    return jnp.where(place == CELLS, 0, token)


def one_hot(left, right):
    return jnp.where(left == right, 1.0, 0.0).astype(bf16)


def main_kernel(
    grids, x_hbm, cot_hbm, wqkv_hbm, wproj_hbm, w1_hbm, w2_hbm, qvb_hbm, rel_hbm, b1_hbm,
    gains_hbm, biases_hbm, scales_hbm, obias_hbm,
    out, ingrad, t_down_hbm, t_up_hbm, t_proj_hbm, t_qkv_hbm, t_small_hbm,
    cot_in, wqkv, w1, w2, qvb, rel, b1, gains, biases, scales, obias, load_sem, store_sem,
    xg, dzg, n2g, og, pg, dn2r, z2r, dn1r, stage_b, stage_c, stage_d, doz, z_send, z_recv, z_fwd,
    mq, mqt, mk, mkt, bias, gexp, uexp,
    n1g, qt, kt, vt, qh, kh, vh, prob, probb, op, ot,
    x1, xhat2, inv2, a1, dx1, own, dn2own,
    hid, du, dot_t, doh, ds, dsf, dqp, dkp, dvp, dqt, dkt, dvt,
    tab, sums, zmr, gpz, p_send, p_recv,
    *plane,
):
    dp = lax.axis_index("dp")
    t = lax.axis_index("tensor")
    rows, width = x_hbm.shape
    seq = rows * NT
    heads = rel.shape[0]
    hw = heads * 64
    base = (dp // GROUP) * GROUP
    mine = dp % GROUP
    core = mine % CORES
    chip_x = (mine // 2) % 2
    chip_y = mine // 4
    to_x = 2 - 4 * chip_x
    to_y = 4 - 8 * chip_y
    sibling = base + mine + 1 - 2 * core
    first_peer = base + mine + (1 - core) * to_x + core * to_y
    second_peer = base + mine + core * to_x + (1 - core) * to_y
    bit_one = (1 - core) * chip_x + core * chip_y
    bit_two = core * chip_x + (1 - core) * chip_y
    quarter = bit_one * 2 + bit_two
    end = ((t - 1) * (t - 2)) // 2
    order = [t, t + 1 - 2 * (t % 2), 2 - t // 2, 3 - 3 * (t // 2)]

    pairs = [
        (x_hbm, xg.at[t]), (cot_hbm, cot_in), (scales_hbm, scales), (rel_hbm, rel), (wqkv_hbm, wqkv),
        (gains_hbm, gains), (biases_hbm, biases), (qvb_hbm, qvb), (wproj_hbm, pg.at[0]), (w1_hbm, w1),
        (w2_hbm, w2), (b1_hbm, b1), (obias_hbm, obias),
    ]
    loads = [pltpu.make_async_copy(src, dst, load_sem.at[i]) for i, (src, dst) in enumerate(pairs)]
    for load in loads:
        load.start()
    barrier = pltpu.get_barrier_semaphore()
    for k in range(1, NT):
        pl.semaphore_signal(barrier, inc=1, device_id=(dp, (t + k) % NT), device_id_type=MESH)
    for peer in (sibling, first_peer, second_peer):
        pl.semaphore_signal(barrier, inc=1, device_id=(peer, t), device_id_type=MESH)
    pl.semaphore_wait(barrier, NT - 1 + 3)

    def block(s):
        return pl.ds(pl.multiple_of(s * rows, rows), rows)

    def remote(src, dst, send, recv, device):
        return pltpu.make_async_remote_copy(
            src_ref=src, dst_ref=dst, send_sem=send, recv_sem=recv, device_id=device, device_id_type=MESH
        )

    def gather_copy(phase, buf, dst, src=None):
        return remote(
            buf.at[t] if src is None else src, buf.at[t],
            z_send.at[phase, dst], z_recv.at[phase, t], (dp, dst),
        )

    def gather_start(phase, buf, src=None):
        gather_copy(phase, buf, order[1], src).start()
        gather_copy(phase, buf, order[2], src).start()
        pl.when(end == 0)(gather_copy(phase, buf, order[3], src).start)

    def forward_copy(phase, buf):
        return remote(
            buf.at[order[3]], buf.at[order[3]],
            z_fwd.at[phase], z_recv.at[phase, order[3]], (dp, order[1]),
        )

    def gather_arrived(phase, buf, step):
        src = order[step]
        remote(
            buf.at[src], buf.at[src], z_send.at[phase, src], z_recv.at[phase, src], (dp, src)
        ).wait_recv()
        if step == 3:
            pl.when(end == 0)(forward_copy(phase, buf).start)

    def gather_sent(phase, buf, src=None):
        gather_copy(phase, buf, order[1], src).wait_send()
        gather_copy(phase, buf, order[2], src).wait_send()

        @pl.when(end == 0)
        def _():
            gather_copy(phase, buf, order[3], src).wait_send()
            forward_copy(phase, buf).wait_send()

    def scatter_copy(phase, stage, buf, i):
        if i == 2:
            dst, slot = order[1], 2
        else:
            dst = end * order[1] + (1 - end) * order[3 - i]
            slot = end * i + (1 - end) * 3
        return remote(
            stage.at[i], buf.at[slot], z_send.at[phase, i], z_recv.at[phase, slot], (dp, dst)
        )

    def slot_wait(phase, buf, slot):
        remote(
            buf.at[slot], buf.at[slot], z_send.at[phase, 0], z_recv.at[phase, slot], (dp, order[1])
        ).wait_recv()

    def scatter_send(phase, stage, buf, i):
        if i == 2:
            scatter_copy(phase, stage, buf, i).start()
        else:
            pl.when(end == 1)(scatter_copy(phase, stage, buf, i).start)

    def scatter_merge(phase, stage, buf, i):
        @pl.when(end == 0)
        def _():
            slot_wait(phase, buf, i)
            stage[i] = (stage[i].astype(f32) + buf[i].astype(f32)).astype(bf16)
            scatter_copy(phase, stage, buf, i).start()

    def scatter_total(phase, buf, total):
        for slot in (2, 3):
            slot_wait(phase, buf, slot)
            total = total + buf[slot].astype(f32)
        return total

    def piece_copy(phase, src, dst, k):
        return remote(
            src, dst, z_send.at[phase, k], z_recv.at[phase, NT - k], (dp, (t + k) % NT)
        )

    def piece_arrived(phase, dst, k):
        remote(dst, dst, z_send.at[phase, k], z_recv.at[phase, k], (dp, (t + k) % NT)).wait_recv()

    half_width = width // 2
    my_lanes = pl.ds(pl.multiple_of(core * half_width, half_width), half_width)
    your_lanes = pl.ds(pl.multiple_of((1 - core) * half_width, half_width), half_width)

    def span(start, count):
        return pl.ds(pl.multiple_of(start, 16), count)

    class Plane:
        def __init__(self, index, refs, target, tile):
            self.index, self.target, self.tile = index, target, tile
            self.count = target.shape[1]
            self.fours = self.count // 4
            if refs is not None:
                self.given, self.near, self.held, self.one, self.two = refs

        def copy(self, step, src, dst, peer):
            return remote(
                src, dst, p_send.at[self.index, step], p_recv.at[self.index, step], (peer, t)
            )

        def outgoing(self, step):
            c, f = self.count, self.fours
            if step == 0:
                return self.copy(0, self.given.at[:, :, your_lanes], self.near, sibling)
            if step == 1:
                src = self.held.at[:, span((1 - bit_one) * 2 * f, 2 * f), :]
                return self.copy(1, src, self.one, first_peer)
            if step == 2:
                src = self.held.at[:, span((bit_one * 2 + 1 - bit_two) * f, f), :]
                return self.copy(2, src, self.two, second_peer)
            if step == 3:
                spot, peer = self.target.at[:, span(quarter * f, f), my_lanes], second_peer
            elif step == 4:
                spot, peer = self.target.at[:, span(bit_one * 2 * f, 2 * f), my_lanes], first_peer
            else:
                spot, peer = self.target.at[:, :, my_lanes], sibling
            return self.copy(step, spot, spot, peer)

        def incoming(self, step):
            f = self.fours
            if step < 3:
                return self.outgoing(step)
            if step == 3:
                spot = self.target.at[:, span((bit_one * 2 + 1 - bit_two) * f, f), my_lanes]
            elif step == 4:
                spot = self.target.at[:, span((1 - bit_one) * 2 * f, 2 * f), my_lanes]
            else:
                spot = self.target.at[:, :, your_lanes]
            return self.copy(step, spot, spot, sibling)

        def send(self, step):
            self.outgoing(step).start()

        def take(self, step):
            self.incoming(step).wait_recv()

        def loop(self, count, body):
            tile = self.tile
            for q in range(self.held.shape[0]):

                def run(j, carry):
                    body(q, j * tile)
                    return carry

                lax.fori_loop(0, count // tile, run, 0)

        def add_core(self):
            self.take(0)

            def body(q, at):
                part = span(at, self.tile)
                value = self.given[q, part, my_lanes].astype(f32) + self.near[q, part, :].astype(f32)
                self.held[q, part, :] = value.astype(bf16)

            self.loop(self.count, body)
            self.send(1)

        def add_first(self):
            self.take(1)

            def body(q, at):
                part = span(bit_one * 2 * self.fours + at, self.tile)
                value = self.held[q, part, :].astype(f32) + self.one[q, span(at, self.tile), :].astype(f32)
                self.held[q, part, :] = value.astype(bf16)

            self.loop(2 * self.fours, body)
            self.send(2)

        def add_second(self, store=None):
            self.take(2)

            def body(q, at):
                part = span(quarter * self.fours + at, self.tile)
                value = self.held[q, part, :].astype(f32) + self.two[q, span(at, self.tile), :].astype(f32)
                if store is None:
                    self.target[q, part, my_lanes] = value.astype(bf16)
                else:
                    store(q, at, value)

            self.loop(self.fours, body)
            if store is None:
                self.send(3)

        def spread_first(self):
            self.take(3)
            self.send(4)

        def spread_second(self):
            self.take(4)
            self.send(5)

        def sent(self, first=0):
            for step in range(first, 6):
                self.outgoing(step).wait_send()

    down_refs, up_refs, proj_refs, qkv_refs, small_refs = (plane[5 * i : 5 * i + 5] for i in range(5))
    t_down, t_up, t_proj, t_qkv, t_small = plane[25:30]
    down_sum = Plane(0, down_refs, t_down, 48)
    up_sum = Plane(1, up_refs, t_up, 48)
    proj_sum = Plane(2, proj_refs, t_proj, 48)
    qkv_sum = Plane(3, qkv_refs, t_qkv, 48)
    small_sum = Plane(4, small_refs, t_small, 16)
    proj_all = Plane(5, None, pg.at[1:NT], 48)
    g_down, g_up, g_proj, g_qkv, g_small = (refs[0] for refs in (down_refs, up_refs, proj_refs, qkv_refs, small_refs))

    gather_start(0, xg, x_hbm)
    loads[1].wait()
    loads[2].wait()
    dzg[t] = (cot_in[...].astype(f32) * scales[1:2, :]).astype(bf16)
    high = grids[0, 0]
    wide = grids[0, 1]
    down = lax.broadcasted_iota(i32, (seq, 1), 0)
    across = lax.broadcasted_iota(i32, (1, seq), 1)
    token_q, _ = query_tokens(down, high, wide)
    token_q_across, _ = query_tokens(across, high, wide)
    token_k = key_tokens(down, high, wide)
    token_k_across = key_tokens(across, high, wide)
    mq[...] = one_hot(token_q, across)
    mqt[...] = one_hot(down, token_q_across)
    mk[...] = one_hot(token_k, across)
    mkt[...] = one_hot(down, token_k_across)
    gexp[...] = jnp.zeros_like(gexp)
    tab[...] = jnp.zeros_like(tab)
    loads[3].wait()
    tab[0:heads, 0 : ENTRIES + 3] = rel[...]
    for h in range(heads):
        table = tab[h : h + 1, :]
        lined = pltpu.roll(jnp.broadcast_to(table, (24, TABLE)), TABLE - (GRID - 1), 1)
        uexp[...] = pltpu.roll(lined, 0, 1, stride=1, stride_axis=0)
        for x in range(SPAN):
            gexp[:, x * GRID : (x + 1) * GRID] = uexp[:, x * SPAN : x * SPAN + GRID]
        hankel = gexp[...]
        for r in range(GRID):
            moved = hankel if r == 0 else pltpu.roll(hankel, WIDE - r * GRID, 1)
            bias[h, r * GRID : (r + 1) * GRID, :] = moved[0:GRID, 0:seq]
        bias[h, CELLS:seq, :] = jnp.zeros((seq - CELLS, seq), f32)
        origin = bias[h, GRID - 1 : GRID, :]
        from_class = table[:, ENTRIES : ENTRIES + 1]
        to_class = table[:, ENTRIES + 1 : ENTRIES + 2]
        class_pair = table[:, ENTRIES + 2 : ENTRIES + 3]

        def settle(i, carry):
            part = pl.ds(pl.multiple_of(i * 128, 128), 128)
            place = lax.broadcasted_iota(i32, (128, 1), 0) + i * 128
            _, padded = query_tokens(place, high, wide)
            values = jnp.where(padded, origin, bias[h, part, :])
            values = jnp.where(across == CELLS, to_class, values)
            values = jnp.where(
                place == CELLS, jnp.where(across == CELLS, class_pair, from_class), values
            )
            bias[h, part, :] = jnp.where(token_k_across >= 0, values, masked)
            return carry

        lax.fori_loop(0, seq // 128, settle, 0)

    for i in (0, 4, 5, 6, 7):
        loads[i].wait()
    gain_one, shift_one = gains[0:1, :], biases[0:1, :]
    for step, s in enumerate(order):
        if step > 0:
            gather_arrived(0, xg, step)
        normed, _ = normalize(xg[s].astype(f32))
        sent = (normed * gain_one + shift_one).astype(bf16)
        part = block(s)
        n1g[part, :] = sent
        qt[part, :] = ((dot_nt(sent, wqkv[0:hw, :]) + qvb[0:1, :]) * 0.125).astype(bf16)
        kt[part, :] = dot_nt(sent, wqkv[hw : 2 * hw, :]).astype(bf16)
        vt[part, :] = (dot_nt(sent, wqkv[2 * hw : 3 * hw, :]) + qvb[1:2, :]).astype(bf16)
    loads[8].wait()
    proj_rows = span(quarter * (hw // 4), hw // 4)

    def proj_piece(k):
        return piece_copy(8, pg.at[0, proj_rows, my_lanes], pg.at[NT - k, proj_rows, my_lanes], k)

    for k in range(1, NT):
        proj_piece(k).start()
    gather_start(1, dzg)

    queries = dot(mq[...], qt[...]).astype(bf16)
    keys = dot(mk[...], kt[...]).astype(bf16)
    values = dot(mk[...], vt[...]).astype(bf16)
    for h in range(heads):
        lanes = slice(h * 64, (h + 1) * 64)
        qh[h] = queries[:, lanes]
        kh[h] = keys[:, lanes]
        vh[h] = values[:, lanes]
    for h in range(heads):

        def attend(i, carry):
            part = pl.ds(pl.multiple_of(i * 128, 128), 128)
            logits = dot_nt(qh[h, part, :], kh[h]) + bias[h, part, :]
            raised = jnp.exp(logits - jnp.max(logits, axis=-1, keepdims=True))
            weights = raised * (1.0 / jnp.sum(raised, axis=-1, keepdims=True))
            prob[h, part, :] = weights
            rounded = weights.astype(bf16)
            probb[h, part, :] = rounded
            op[part, h * 64 : (h + 1) * 64] = dot(rounded, vh[h]).astype(bf16)
            return carry

        lax.fori_loop(0, seq // 128, attend, 0)
        if h == heads - 2:
            for k in range(1, NT):
                piece_arrived(8, pg.at[k, proj_rows, my_lanes], k)
            proj_all.send(3)
    ot[...] = dot(mqt[...], op[...]).astype(bf16)

    def mixed_piece(k):
        return piece_copy(2, ot.at[block((t + k) % NT), :], og.at[NT - k], k)

    for k in (2, 1, 3):
        mixed_piece(k).start()
    og[0] = ot[block(t), :]
    proj_all.spread_first()
    total = dot(og[0], pg[0])
    loads[12].wait()
    proj_all.spread_second()
    for k in range(1, NT):
        piece_arrived(2, og.at[k], k)
    proj_all.take(5)
    for k in range(1, NT):
        total = total + dot(og[k], pg[k])
    branch_one = total + obias[0:1, :]
    a1[...] = branch_one
    after_one = xg[t].astype(f32) + scales[0:1, :] * branch_one
    x1[...] = after_one
    normed, inverse = normalize(after_one)
    xhat2[...] = normed
    inv2[...] = jnp.broadcast_to(inverse, inv2.shape)
    n2g[t] = (normed * gains[1:2, :] + biases[1:2, :]).astype(bf16)
    gather_start(3, n2g)
    gather_arrived(1, dzg, 3)

    for i in (9, 10, 11):
        loads[i].wait()
    shift_up = b1[...].astype(f32)
    bias_up = jnp.zeros((1, w1.shape[1]), f32)
    for step, s in enumerate(order):
        if step > 0:
            gather_arrived(3, n2g, step)
            if step < 3:
                gather_arrived(1, dzg, step)
        part = block(s)
        before = dot(n2g[s], w1[...]) + shift_up
        cumulative = 0.5 * (1.0 + lax.erf(before * 0.7071067811865476))
        slope = cumulative + before * (jnp.exp(-0.5 * before * before) * 0.3989422804014327)
        hid[part, :] = (before * cumulative).astype(bf16)
        grad_pre = (dot_nt(dzg[s], w2[...]) * slope).astype(bf16)
        du[part, :] = grad_pre
        bias_up = bias_up + jnp.sum(grad_pre.astype(f32), axis=0, keepdims=True)
        back = dot_nt(grad_pre, w1[...])
        if step == 0:
            dn2own[...] = back
        else:
            stage_b[3 - step] = back.astype(bf16)
            scatter_send(4, stage_b, dn2r, 3 - step)
    sums[8:9, :] = bias_up
    down_rows = jnp.reshape(dzg[...], (seq, width))
    g_down[0] = dot_tn(hid[...], down_rows).astype(bf16)
    down_sum.send(0)
    scatter_merge(4, stage_b, dn2r, 1)
    scatter_merge(4, stage_b, dn2r, 0)
    up_rows = jnp.reshape(n2g[...], (seq, width))
    g_up[0] = dot_tn(up_rows, du[...]).astype(bf16)
    up_sum.send(0)
    for step, s in enumerate(order):
        piece = dot(hid[block(s), :], w2[...])
        if step == 0:
            own[...] = piece
        else:
            stage_c[3 - step] = piece.astype(bf16)
    down_sum.add_core()

    total = scatter_total(4, dn2r, dn2own[...])
    normed = xhat2[...]
    sums[3:4, :] = jnp.sum(total, axis=0, keepdims=True)
    sums[1:2, :] = jnp.sum(total * normed, axis=0, keepdims=True)
    after = cot_in[...].astype(f32) + norm_back(total * gains[1:2, :], normed, inv2[:, 0:1])
    dx1[...] = after
    branch = after * scales[0:1, :]
    grad_rows = branch.astype(bf16)

    def mixed_back(k):
        return piece_copy(6, doz.at[k], dot_t.at[block(t), :], k)

    for k in (2, 1, 3, 0):
        piece = dot_nt(grad_rows, pg[k]).astype(bf16)
        if k == 0:
            dot_t[block(t), :] = piece
        else:
            doz[k] = piece
            mixed_back(k).start()
    for i in range(NT - 1):
        scatter_send(5, stage_c, z2r, i)
    sums[4:5, :] = jnp.sum(after * a1[...], axis=0, keepdims=True)
    sums[6:7, :] = jnp.sum(branch, axis=0, keepdims=True)
    for k in range(NT):
        g_proj[k] = dot_tn(og[k], grad_rows).astype(bf16)
    proj_sum.send(0)
    up_sum.add_core()

    for k in range(1, NT):
        piece_arrived(6, dot_t.at[block((t + k) % NT), :], k)
    grad_mixed = dot(mq[...], dot_t[...]).astype(bf16)
    for h in range(heads):
        doh[h] = grad_mixed[:, h * 64 : (h + 1) * 64]
    zero = jnp.zeros((1, seq), f32)
    class_rows = []
    for h in range(heads):
        lanes = slice(h * 64, (h + 1) * 64)

        def attend_back(i, carry):
            class_row, class_column, pad_row = carry
            part = pl.ds(pl.multiple_of(i * 128, 128), 128)
            place = lax.broadcasted_iota(i32, (128, 1), 0) + i * 128
            _, padded = query_tokens(place, high, wide)
            grad_prob = dot_nt(doh[h, part, :], vh[h])
            weights = prob[h, part, :]
            crossed = jnp.sum(weights * grad_prob, axis=-1, keepdims=True)
            rounded = (weights * (grad_prob - crossed)).astype(bf16)
            ds[part, :] = rounded
            dqp[part, lanes] = dot(rounded, kh[h]).astype(bf16) * 0.125
            wide_grad = rounded.astype(f32)
            class_row = class_row + jnp.sum(
                jnp.where(place == CELLS, wide_grad, 0.0), axis=0, keepdims=True
            )
            class_column = class_column + jnp.sum(
                jnp.where((place != CELLS) & (across == CELLS), wide_grad, 0.0), axis=0, keepdims=True
            )
            cells = jnp.where(across < CELLS, wide_grad, 0.0)
            pad_row = pad_row + jnp.sum(jnp.where(padded, cells, 0.0), axis=0, keepdims=True)
            dsf[h, part, :] = jnp.where(padded, 0.0, cells)
            return class_row, class_column, pad_row

        class_rows.append(lax.fori_loop(0, seq // 128, attend_back, (zero, zero, zero)))
        dvp[:, lanes] = dot_tn(probb[h], doh[h]).astype(bf16)
        dkp[:, lanes] = dot_tn(ds[...], qh[h]).astype(bf16)
        if h == 0:
            down_sum.add_first()
            proj_sum.add_core()
            scatter_merge(5, stage_c, z2r, 0)
        elif h == 1:
            up_sum.add_first()
            down_sum.add_second()
            scatter_merge(5, stage_c, z2r, 1)
    dqt[...] = dot(mqt[...], dqp[...]).astype(bf16)
    dkt[...] = dot(mkt[...], dkp[...]).astype(bf16)
    dvt[...] = dot(mkt[...], dvp[...]).astype(bf16)

    shift_total = jnp.zeros((1, width), f32)
    gain_total = jnp.zeros((1, width), f32)
    for step in (3, 2, 1, 0):
        s = order[step]
        part = block(s)
        piece = dot(dqt[part, :], wqkv[0:hw, :]) + dot(dkt[part, :], wqkv[hw : 2 * hw, :])
        piece = piece + dot(dvt[part, :], wqkv[2 * hw : 3 * hw, :])
        if step == 0:
            dn2own[...] = piece
        else:
            stage_d[3 - step] = piece.astype(bf16)
            scatter_send(7, stage_d, dn1r, 3 - step)
        normed, _ = normalize(xg[s].astype(f32))
        shift_total = shift_total + jnp.sum(piece, axis=0, keepdims=True)
        gain_total = gain_total + jnp.sum(piece * normed, axis=0, keepdims=True)
    sums[2:3, :] = shift_total
    sums[0:1, :] = gain_total
    g_qkv[0, 0:hw, :] = dot_tn(dqt[...], n1g[...]).astype(bf16)
    g_qkv[0, hw : 2 * hw, :] = dot_tn(dkt[...], n1g[...]).astype(bf16)
    g_qkv[0, 2 * hw : 3 * hw, :] = dot_tn(dvt[...], n1g[...]).astype(bf16)
    qkv_sum.send(0)
    up_sum.add_second()
    down_sum.spread_first()
    scatter_merge(7, stage_d, dn1r, 0)
    scatter_merge(7, stage_d, dn1r, 1)

    branch_two = scatter_total(5, z2r, own[...]) + obias[1:2, :]
    out[...] = (x1[...] + scales[1:2, :] * branch_two).astype(bf16)
    cot = cot_in[...].astype(f32)
    sums[5:6, :] = jnp.sum(cot * branch_two, axis=0, keepdims=True)
    sums[7:8, :] = jnp.sum(cot * scales[1:2, :], axis=0, keepdims=True)
    zmr[t] = sums[0:REP, :]

    def small_tensor(k):
        return remote(
            zmr.at[t], zmr.at[t], z_send.at[10, k], z_recv.at[10, NT - k], (dp, (t + k) % NT)
        )

    for k in range(1, NT):
        small_tensor(k).start()
    qkv_sum.add_core()
    proj_sum.add_first()
    down_sum.spread_second()
    up_sum.spread_first()

    row24 = lax.broadcasted_iota(i32, (24, 1), 0)
    lane_t = lax.broadcasted_iota(i32, (1, TABLE), 1)
    uexp[...] = jnp.zeros_like(uexp)
    gexp[...] = jnp.zeros_like(gexp)
    for h in range(heads):
        class_row, class_column, pad_row = class_rows[h]
        blank = jnp.zeros((24, WIDE - seq), f32)
        folded = jnp.zeros((24, WIDE), f32)
        for r in range(GRID):
            cells = jnp.concatenate([dsf[h, r * GRID : r * GRID + 24, :], blank], axis=1)
            folded = folded + (cells if r == 0 else pltpu.roll(cells, r * GRID, 1))
        padded_row = jnp.concatenate([pad_row, jnp.zeros((1, WIDE - seq), f32)], axis=1)
        folded = jnp.where(row24 < GRID, folded, 0.0) + jnp.where(row24 == GRID - 1, padded_row, 0.0)
        for i in range(GRID):
            gexp[GRID - 1 - i : GRID - i, :] = folded[i : i + 1, :]
        for x in range(SPAN):
            uexp[:, x * SPAN : x * SPAN + GRID] = gexp[:, x * GRID : (x + 1) * GRID]
        lined = pltpu.roll(uexp[...], 0, 1, stride=1, stride_axis=0)
        table = jnp.sum(lined, axis=0, keepdims=True)
        from_class = jnp.sum(jnp.where(across != CELLS, class_row, 0.0), axis=1, keepdims=True)
        class_pair = jnp.sum(jnp.where(across == CELLS, class_row, 0.0), axis=1, keepdims=True)
        to_class = jnp.sum(class_column, axis=1, keepdims=True)
        table = jnp.where(lane_t == ENTRIES, from_class, table)
        table = jnp.where(lane_t == ENTRIES + 1, to_class, table)
        tab[h : h + 1, :] = jnp.where(lane_t == ENTRIES + 2, class_pair, table)
    sums[9:10, 0:hw] = jnp.sum(dqt[...].astype(f32), axis=0, keepdims=True)
    sums[10:11, 0:hw] = jnp.sum(dvt[...].astype(f32), axis=0, keepdims=True)
    sums[9:11, hw:width] = jnp.zeros((2, width - hw), f32)
    for h in range(heads):
        at = 11 + 3 * h
        sums[at : at + 1, :] = tab[h : h + 1, 0:width]
        sums[at + 1 : at + 2, :] = tab[h : h + 1, width : 2 * width]
        sums[at + 2 : at + 3, 0 : TABLE - 2 * width] = tab[h : h + 1, 2 * width : TABLE]
        sums[at + 2 : at + 3, TABLE - 2 * width : width] = jnp.zeros((1, 3 * width - TABLE), f32)
    sums[11 + 3 * heads : SMALL, :] = jnp.zeros((SMALL - 11 - 3 * heads, width), f32)

    for k in range(1, NT):
        piece_arrived(10, zmr.at[(t + k) % NT], k)
    sums[0:REP, :] = zmr[0] + zmr[1] + zmr[2] + zmr[3]
    g_small[0] = sums[...].astype(bf16)
    small_sum.send(0)
    qkv_sum.add_first()
    gpz_at = gpz

    def keep(q, at, value):
        gpz_at[q, span(at, 48), :] = value.astype(bf16)

    proj_sum.add_second(keep)

    def proj_exchange(k):
        return piece_copy(9, gpz.at[k], gpz.at[2 * NT - k], k)

    for k in range(1, NT):
        proj_exchange(k).start()
    up_sum.spread_second()
    small_sum.add_core()
    total = scatter_total(7, dn1r, dn2own[...])
    normed, inverse = normalize(xg[t].astype(f32))
    ingrad[...] = dx1[...] + norm_back(total * gain_one, normed, inverse)
    down_sum.take(5)
    stores = [
        pltpu.make_async_copy(src.at[0], dst, store_sem.at[i])
        for i, (src, dst) in enumerate(
            [(t_down, t_down_hbm), (t_up, t_up_hbm), (t_proj, t_proj_hbm), (t_qkv, t_qkv_hbm), (t_small, t_small_hbm)]
        )
    ]
    stores[0].start()
    qkv_sum.add_second()
    small_sum.add_first()
    value = gpz[0].astype(f32)
    for k in range(1, NT):
        piece_arrived(9, gpz.at[NT + k], k)
        value = value + gpz[NT + k].astype(f32)
    t_proj[0, proj_rows, my_lanes] = value.astype(bf16)
    proj_sum.send(3)
    up_sum.take(5)
    stores[1].start()
    small_sum.add_second()
    qkv_sum.spread_first()
    proj_sum.spread_first()
    small_sum.spread_first()
    qkv_sum.spread_second()
    proj_sum.spread_second()
    small_sum.spread_second()
    for i, part_sum in ((3, qkv_sum), (2, proj_sum), (4, small_sum)):
        part_sum.take(5)
        stores[i].start()

    gather_sent(0, xg, x_hbm)
    gather_sent(1, dzg)
    gather_sent(3, n2g)
    for phase, stage, buf in ((4, stage_b, dn2r), (5, stage_c, z2r), (7, stage_d, dn1r)):
        for i in range(NT - 1):
            scatter_copy(phase, stage, buf, i).wait_send()
    for k in range(1, NT):
        proj_piece(k).wait_send()
        mixed_piece(k).wait_send()
        mixed_back(k).wait_send()
        proj_exchange(k).wait_send()
        small_tensor(k).wait_send()
    for part_sum in (down_sum, up_sum, proj_sum, qkv_sum, small_sum):
        part_sum.sent()
    proj_all.sent(3)
    for store in stores:
        store.wait()


def finish_kernel(
    down_in, up_in, proj_in, qkv_in, small_in, out_in, ingrad_in,
    out, ingrad, g_qkv, g_qv, g_table, g_proj, g_up, g_up_bias, g_down, g_gains, g_shifts, g_scales, g_biases,
    down_v, up_v, proj_v, qkv_v, small_v, down_f, up_f, proj_f, qkv_f, load_sem, store_sem,
):
    width = g_down.shape[1]
    hw = g_proj.shape[0]
    heads, entries = g_table.shape
    moves = [
        pltpu.make_async_copy(src, dst, store_sem.at[i])
        for i, (src, dst) in enumerate(((out_in, out), (ingrad_in, ingrad)))
    ]
    parts = ((down_in, down_v, down_f, g_down), (up_in, up_v, up_f, g_up),
             (qkv_in, qkv_v, qkv_f, g_qkv), (proj_in, proj_v, proj_f, g_proj))
    loads = [pltpu.make_async_copy(part[0], part[1], load_sem.at[i]) for i, part in enumerate(parts)]
    loads.append(pltpu.make_async_copy(small_in, small_v, load_sem.at[4]))
    for copy in loads + moves:
        copy.start()
    for i, (_, rounded, widened, result) in enumerate(parts):
        loads[i].wait()
        widened[...] = rounded[...].astype(f32)
        moves.append(pltpu.make_async_copy(widened, result, store_sem.at[2 + i]))
        moves[-1].start()
    loads[4].wait()
    small = small_v[...].astype(f32)
    g_gains[...] = small[0:2, :]
    g_shifts[...] = small[2:4, :]
    g_scales[...] = small[4:6, :]
    g_biases[...] = small[6:8, :]
    g_up_bias[...] = small[8:9, :]
    g_qv[...] = small[9:11, 0:hw]
    for h in range(heads):
        for j in range(3):
            count = min(width, entries - j * width)
            g_table[h : h + 1, j * width : j * width + count] = small[
                11 + 3 * h + j : 12 + 3 * h + j, 0:count
            ]
    for copy in moves:
        copy.wait()


def per_device(
    n_dp, tokens, grids, qkv_weight, qv_bias, rel_table, proj_weight, fc1_weight, fc1_bias, fc2_weight,
    norm_gains, norm_biases, layer_scales, out_biases, cotangent,
):
    rows, width = tokens.shape
    seq = rows * NT
    heads, entries = rel_table.shape
    hw = heads * 64
    ff = fc1_weight.shape[1]
    qkv_rows = jnp.transpose(qkv_weight, (1, 2, 0)).reshape(3 * hw, width)
    vm = pl.BlockSpec(memory_space=pltpu.VMEM)
    anywhere = pl.BlockSpec(memory_space=pl.ANY)

    def many(count, shape, dtype):
        return [pltpu.VMEM(shape, dtype)] * count

    def sems(*shape):
        return [pltpu.SemaphoreType.DMA(shape)]

    half = width // 2
    scratch = [
        pltpu.VMEM((rows, width), bf16), pltpu.VMEM((3 * hw, width), bf16),
        pltpu.VMEM((width, ff), bf16), pltpu.VMEM((ff, width), bf16),
        pltpu.VMEM((2, hw), f32), pltpu.VMEM((heads, entries), f32), pltpu.VMEM((1, ff), bf16),
    ]
    scratch += many(4, (2, width), f32) + sems(13) + sems(5)
    scratch += many(3, (NT, rows, width), bf16)
    scratch += many(1, (NT, rows, hw), bf16) + many(1, (NT, hw, width), bf16)
    scratch += many(3, (NT, rows, width), bf16) + many(3, (NT - 1, rows, width), bf16)
    scratch += many(1, (NT, rows, hw), bf16) + sems(11, NT) + sems(11, NT) + sems(11)
    scratch += many(4, (seq, seq), bf16)
    scratch += many(1, (heads, seq, seq), f32) + many(1, (24, WIDE), f32) + many(1, (24, TABLE), f32)
    scratch += many(1, (seq, width), bf16) + many(3, (seq, hw), bf16)
    scratch += many(3, (heads, seq, 64), bf16)
    scratch += many(1, (heads, seq, seq), f32) + many(1, (heads, seq, seq), bf16)
    scratch += many(2, (seq, hw), bf16)
    scratch += many(2, (rows, width), f32) + many(1, (rows, 128), f32) + many(4, (rows, width), f32)
    scratch += many(2, (seq, ff), bf16) + many(1, (seq, hw), bf16) + many(1, (heads, seq, 64), bf16)
    scratch += many(1, (seq, seq), bf16) + many(1, (heads, seq, seq), f32) + many(6, (seq, hw), bf16)
    scratch += many(1, (8, TABLE), f32) + many(1, (SMALL, width), f32) + many(1, (NT, REP, width), f32)
    scratch += many(1, (2 * NT, hw // 4, half), bf16) + sems(6, 6) + sems(6, 6)
    kinds = ((1, ff), (1, width), (NT, hw), (1, 3 * hw), (1, SMALL))
    for lead, count in kinds:
        scratch += [
            pltpu.VMEM((lead, count, width), bf16), pltpu.VMEM((lead, count, half), bf16),
            pltpu.VMEM((lead, count, half), bf16), pltpu.VMEM((lead, count // 2, half), bf16),
            pltpu.VMEM((lead, count // 4, half), bf16),
        ]
    for lead, count in kinds:
        scratch += many(1, (1, count, width), bf16)
    flat = [jax.ShapeDtypeStruct((count, width), bf16) for lead, count in kinds]
    output, input_grad, *totals = pl.pallas_call(
        main_kernel,
        out_shape=[
            jax.ShapeDtypeStruct((rows, width), bf16),
            jax.ShapeDtypeStruct((rows, width), f32),
        ]
        + flat,
        in_specs=[pl.BlockSpec(memory_space=pltpu.SMEM)] + [anywhere] * 13,
        out_specs=[vm, vm] + [anywhere] * 5,
        scratch_shapes=scratch,
        compiler_params=pltpu.CompilerParams(
            collective_id=0, has_side_effects=True, vmem_limit_bytes=60 << 20
        ),
        name="layer",
    )(
        grids, tokens, cotangent, qkv_rows, proj_weight, fc1_weight, fc2_weight,
        qv_bias, rel_table, fc1_bias.reshape(1, ff), norm_gains, norm_biases, layer_scales, out_biases,
    )
    pair = jax.ShapeDtypeStruct((2, width), f32)
    results = pl.pallas_call(
        finish_kernel,
        out_shape=(
            jax.ShapeDtypeStruct((rows, width), bf16),
            jax.ShapeDtypeStruct((rows, width), f32),
            jax.ShapeDtypeStruct((3 * hw, width), f32),
            jax.ShapeDtypeStruct((2, hw), f32),
            jax.ShapeDtypeStruct((heads, entries), f32),
            jax.ShapeDtypeStruct((hw, width), f32),
            jax.ShapeDtypeStruct((width, ff), f32),
            jax.ShapeDtypeStruct((1, ff), f32),
            jax.ShapeDtypeStruct((ff, width), f32),
            pair, pair, pair, pair,
        ),
        in_specs=[anywhere] * 7,
        out_specs=(
            anywhere, anywhere, anywhere, vm, vm, anywhere, anywhere, vm, anywhere, vm, vm, vm, vm,
        ),
        scratch_shapes=[
            pltpu.VMEM((ff, width), bf16), pltpu.VMEM((width, ff), bf16), pltpu.VMEM((hw, width), bf16),
            pltpu.VMEM((3 * hw, width), bf16), pltpu.VMEM((SMALL, width), bf16),
            pltpu.VMEM((ff, width), f32), pltpu.VMEM((width, ff), f32), pltpu.VMEM((hw, width), f32),
            pltpu.VMEM((3 * hw, width), f32), pltpu.SemaphoreType.DMA((5,)), pltpu.SemaphoreType.DMA((6,)),
        ],
        compiler_params=pltpu.CompilerParams(vmem_limit_bytes=40 << 20),
        name="finish",
    )(*totals, output, input_grad)
    results = list(results)
    stride = GROUP
    while stride < n_dp:
        hops = [(i, i ^ stride) for i in range(n_dp)]
        results[2:] = [value + lax.ppermute(value, "dp", hops) for value in results[2:]]
        stride *= 2
    results[2] = jnp.transpose(results[2].reshape(3, hw, width), (2, 0, 1))
    results[7] = results[7].reshape(ff)
    return tuple(results)


def solution(mesh):
    n_dp = mesh.shape["dp"]
    blocks = P(("dp", "tensor"), None)
    placed = (
        blocks, P("dp", None), P(None, None, "tensor"), P(None, "tensor"), P("tensor", None), P("tensor", None),
        P(None, "tensor"), P("tensor"), P("tensor", None), P(), P(), P(), P(), blocks,
    )
    given = (
        blocks, blocks, P(None, None, "tensor"), P(None, "tensor"), P("tensor", None), P("tensor", None),
        P(None, "tensor"), P("tensor"), P("tensor", None), P(), P(), P(), P(),
    )

    def layer(*arrays):
        return per_device(n_dp, *arrays)

    return jax.shard_map(layer, mesh=mesh, in_specs=placed, out_specs=given, check_vma=False)
```

```python
import jax
import jax.numpy as jnp
from jax import lax
from jax.experimental import pallas as pl
from jax.experimental.pallas import tpu as pltpu
from jax.sharding import PartitionSpec as P

GRID = 22
SPAN = 2 * GRID - 1
CELLS = GRID * GRID
ENTRIES = SPAN * SPAN
MESH = pl.DeviceIdType.MESH
f32 = jnp.float32
bf16 = jnp.bfloat16
i32 = jnp.int32

eps_norm = 1e-06
masked = -1e30
NT = 4
CHIPS = 4
CORES = 2
GROUP = CHIPS * CORES
TABLE = 1920
WIDE = 1024
SMALL = 64
REP = 8
PIECE = 192


def dot(left, right):
    return lax.dot_general(left, right, (((1,), (0,)), ((), ())), preferred_element_type=f32)


def dot_nt(left, right):
    return lax.dot_general(left, right, (((1,), (1,)), ((), ())), preferred_element_type=f32)


def dot_tn(left, right):
    return lax.dot_general(left, right, (((0,), (0,)), ((), ())), preferred_element_type=f32)


def normalize(values):
    center = values - jnp.mean(values, axis=-1, keepdims=True)
    inverse = lax.rsqrt(jnp.mean(center * center, axis=-1, keepdims=True) + eps_norm)
    return center * inverse, inverse


def norm_back(grad_normed, normed, inverse):
    average = jnp.mean(grad_normed, axis=-1, keepdims=True)
    crossed = jnp.mean(grad_normed * normed, axis=-1, keepdims=True)
    return inverse * (grad_normed - average - normed * crossed)


def split_cell(place):
    row = (place * 2979) >> 16
    return row, place - row * GRID


def query_tokens(place, high, wide):
    row, back = split_cell(place)
    inside = (place < CELLS) & (row < high) & (GRID - 1 - back < wide)
    before = jnp.minimum(row, high) * wide + jnp.where(
        row < high, jnp.maximum(back - (GRID - wide), 0), 0
    )
    token = jnp.where(inside, 1 + row * wide + (GRID - 1 - back), high * wide + 1 + place - before)
    token = jnp.where(place == CELLS, 0, jnp.where(place > CELLS, place, token))
    padding = jnp.logical_not(inside) & (place != CELLS)
    return token, padding


def key_tokens(place, high, wide):
    row, back = split_cell(place)
    row = GRID - 1 - row
    column = GRID - 1 - back
    inside = (place < CELLS) & (row < high) & (column < wide)
    token = jnp.where(inside, 1 + row * wide + column, -1)
    return jnp.where(place == CELLS, 0, token)


def one_hot(left, right):
    return jnp.where(left == right, 1.0, 0.0).astype(bf16)


def main_kernel(
    grids, x_hbm, cot_hbm, wqkv_hbm, wproj_hbm, w1_hbm, w2_hbm, qvb_hbm, rel_hbm, b1_hbm,
    gains_hbm, biases_hbm, scales_hbm, obias_hbm,
    out, ingrad, t_down_hbm, t_up_hbm, t_proj_hbm, t_qkv_hbm, t_small_hbm,
    outv, ingradv, wqkv, w1, w2, qvb, rel, b1, gains, biases, scales, obias, load_sem, store_sem,
    xg, cg, dzg, n2g, og, pg, dn2r, z2r, dn1r, stage_b, stage_c, stage_d, doz, z_send, z_recv, z_half,
    mq, mqt, mk, mkt, bias, gexp, uexp,
    n1g, qt, kt, vt, qh, kh, vh, prob, probb, op, ot,
    x1, xhat2, inv2, a1, dx1, own, dn2own,
    hid, du, dot_t, doh, ds, dsf, dqp, dkp, dvp, dqt, dkt, dvt,
    tab, sums, zmr, gpz, p_send, p_recv,
    *plane,
):
    dp = lax.axis_index("dp")
    t = lax.axis_index("tensor")
    rows, width = x_hbm.shape
    seq = rows * NT
    heads = rel.shape[0]
    hw = heads * 64
    base = (dp // GROUP) * GROUP
    mine = dp % GROUP
    core = mine % CORES
    chip_x = (mine // 2) % 2
    chip_y = mine // 4
    to_x = 2 - 4 * chip_x
    to_y = 4 - 8 * chip_y
    sibling = base + mine + 1 - 2 * core
    first_peer = base + mine + (1 - core) * to_x + core * to_y
    second_peer = base + mine + core * to_x + (1 - core) * to_y
    bit_one = (1 - core) * chip_x + core * chip_y
    bit_two = core * chip_x + (1 - core) * chip_y
    quarter = bit_one * 2 + bit_two
    end = ((t - 1) * (t - 2)) // 2
    order = [t, t + 1 - 2 * (t % 2), 2 - t // 2, 3 - 3 * (t // 2)]

    pairs = [
        (x_hbm, xg.at[t]), (cot_hbm, cg.at[t]), (scales_hbm, scales), (rel_hbm, rel), (wqkv_hbm, wqkv),
        (gains_hbm, gains), (biases_hbm, biases), (qvb_hbm, qvb), (wproj_hbm, pg.at[0]), (w1_hbm, w1),
        (w2_hbm, w2), (b1_hbm, b1), (obias_hbm, obias),
    ]
    loads = [pltpu.make_async_copy(src, dst, load_sem.at[i]) for i, (src, dst) in enumerate(pairs)]
    for load in loads:
        load.start()
    barrier = pltpu.get_barrier_semaphore()
    for k in range(1, NT):
        pl.semaphore_signal(barrier, inc=1, device_id=(dp, (t + k) % NT), device_id_type=MESH)
    for peer in (sibling, first_peer, second_peer):
        pl.semaphore_signal(barrier, inc=1, device_id=(peer, t), device_id_type=MESH)
    pl.semaphore_wait(barrier, NT - 1 + 3)

    def block(s):
        return pl.ds(pl.multiple_of(s * rows, rows), rows)

    def remote(src, dst, send, recv, device):
        return pltpu.make_async_remote_copy(
            src_ref=src, dst_ref=dst, send_sem=send, recv_sem=recv, device_id=device, device_id_type=MESH
        )

    half_rows = rows // 2

    def half_copy(phase, buf, src, half, dst, way, given=None):
        spot = buf.at[src, half * half_rows : (half + 1) * half_rows, :]
        if given is not None:
            given = given.at[half * half_rows : (half + 1) * half_rows, :]
        return remote(
            spot if given is None else given, spot,
            z_half.at[phase, way, half], z_recv.at[phase, src * 2 + half], (dp, dst),
        )

    def gather_start(phase, buf, given=None):
        for half in range(2):
            half_copy(phase, buf, t, half, order[1], 0, given).start()
            pl.when(end == 0)(half_copy(phase, buf, t, half, order[2], 1, given).start)

    def half_arrived(phase, buf, step, half):
        half_copy(phase, buf, order[step], half, order[1], 0).wait_recv()

    def half_forward(phase, buf, step, half):
        to = order[2] if step == 1 else order[1]
        half_copy(phase, buf, order[step], half, to, 1 + step).start()

    def gather_near(phase, buf):
        @pl.when(end == 0)
        def _():
            for half in range(2):
                for step in (1, 2):
                    half_arrived(phase, buf, step, half)
                    half_forward(phase, buf, step, half)

    def gather_take(phase, buf, step):
        for half in range(2):
            if step < 3:
                pl.when(end == 1)(lambda: half_arrived(phase, buf, step, half))
            else:
                half_arrived(phase, buf, step, half)
                pl.when(end == 0)(lambda: half_forward(phase, buf, step, half))

    def gather_sent(phase, buf, given=None):
        for half in range(2):
            half_copy(phase, buf, t, half, order[1], 0, given).wait_send()

            @pl.when(end == 0)
            def _():
                half_copy(phase, buf, t, half, order[2], 1, given).wait_send()
                for step in (1, 2, 3):
                    half_copy(phase, buf, order[step], half, order[1], 1 + step).wait_send()

    def scatter_copy(phase, stage, buf, i):
        if i == 2:
            dst, slot = order[1], 2
        else:
            dst = end * order[1] + (1 - end) * order[3 - i]
            slot = end * i + (1 - end) * 3
        return remote(
            stage.at[i], buf.at[slot], z_send.at[phase, i], z_recv.at[phase, slot], (dp, dst)
        )

    def slot_wait(phase, buf, slot):
        remote(
            buf.at[slot], buf.at[slot], z_send.at[phase, 0], z_recv.at[phase, slot], (dp, order[1])
        ).wait_recv()

    def scatter_send(phase, stage, buf, i):
        if i == 2:
            scatter_copy(phase, stage, buf, i).start()
        else:
            pl.when(end == 1)(scatter_copy(phase, stage, buf, i).start)

    def scatter_merge(phase, stage, buf, i):
        @pl.when(end == 0)
        def _():
            slot_wait(phase, buf, i)
            stage[i] = (stage[i].astype(f32) + buf[i].astype(f32)).astype(bf16)
            scatter_copy(phase, stage, buf, i).start()

    def far_copy(phase, stage, buf):
        dst = order[3]
        slot = (1 - end) * 3
        return remote(stage.at[0], buf.at[slot], z_send.at[phase, 0], z_recv.at[phase, slot], (dp, dst))

    def scatter_total(phase, buf, total):
        for slot in (2, 3):
            slot_wait(phase, buf, slot)
            total = total + buf[slot].astype(f32)
        return total

    def piece_copy(phase, src, dst, k):
        return remote(
            src, dst, z_send.at[phase, k], z_recv.at[phase, NT - k], (dp, (t + k) % NT)
        )

    def piece_arrived(phase, dst, k):
        remote(dst, dst, z_send.at[phase, k], z_recv.at[phase, k], (dp, (t + k) % NT)).wait_recv()

    half_width = width // 2
    my_lanes = pl.ds(pl.multiple_of(core * half_width, half_width), half_width)
    your_lanes = pl.ds(pl.multiple_of((1 - core) * half_width, half_width), half_width)

    def span(start, count):
        return pl.ds(pl.multiple_of(start, 16), count)

    class Plane:
        def __init__(self, index, refs, target):
            self.index, self.target = index, target
            self.count = target.shape[1]
            self.fours = self.count // 4
            if refs is not None:
                self.given, self.near, self.held, self.one, self.two = refs
                self.lead = self.given.shape[0]

        def copy(self, step, src, dst, peer):
            return remote(
                src, dst, p_send.at[self.index, step], p_recv.at[self.index, step], (peer, t)
            )

        def outgoing(self, step):
            c, f = self.count, self.fours
            if step == 0:
                return self.copy(0, self.given.at[:, :, your_lanes], self.near, sibling)
            if step == 1:
                src = self.held.at[:, span((1 - bit_one) * 2 * f, 2 * f), :]
                return self.copy(1, src, self.one, first_peer)
            if step == 2:
                src = self.held.at[:, span((bit_one * 2 + 1 - bit_two) * f, f), :]
                return self.copy(2, src, self.two, second_peer)
            if step == 3:
                spot, peer = self.target.at[:, span(quarter * f, f), my_lanes], second_peer
            elif step == 4:
                spot, peer = self.target.at[:, span(bit_one * 2 * f, 2 * f), my_lanes], first_peer
            else:
                spot, peer = self.target.at[:, :, my_lanes], sibling
            return self.copy(step, spot, spot, peer)

        def incoming(self, step):
            f = self.fours
            if step < 3:
                return self.outgoing(step)
            if step == 3:
                spot = self.target.at[:, span((bit_one * 2 + 1 - bit_two) * f, f), my_lanes]
            elif step == 4:
                spot = self.target.at[:, span((1 - bit_one) * 2 * f, 2 * f), my_lanes]
            else:
                spot = self.target.at[:, :, your_lanes]
            return self.copy(step, spot, spot, sibling)

        def send(self, step):
            self.outgoing(step).start()

        def take(self, step):
            self.incoming(step).wait_recv()

        def add_core(self):
            self.take(0)
            for q in range(self.lead):
                value = self.given[q, :, my_lanes].astype(f32) + self.near[q].astype(f32)
                self.held[q] = value.astype(bf16)
            self.send(1)

        def add_first(self):
            self.take(1)
            part = span(bit_one * 2 * self.fours, 2 * self.fours)
            for q in range(self.lead):
                value = self.held[q, part, :].astype(f32) + self.one[q].astype(f32)
                self.held[q, part, :] = value.astype(bf16)
            self.send(2)

        def add_second(self, store=None):
            self.take(2)
            part = span(quarter * self.fours, self.fours)
            for q in range(self.lead):
                value = (self.held[q, part, :].astype(f32) + self.two[q].astype(f32)).astype(bf16)
                if store is None:
                    self.target[q, part, my_lanes] = value
                else:
                    store[q] = value
            if store is None:
                self.send(3)

        def spread_first(self):
            self.take(3)
            self.send(4)

        def spread_second(self):
            self.take(4)
            self.send(5)

        def sent(self, first=0):
            for step in range(first, 6):
                self.outgoing(step).wait_send()

    down_refs, up_refs, proj_refs, qkv_refs, small_refs = (plane[5 * i : 5 * i + 5] for i in range(5))
    t_down, t_up, t_proj, t_qkv, t_small = plane[25:30]
    down_sum = Plane(0, down_refs, t_down)
    up_sum = Plane(1, up_refs, t_up)
    proj_sum = Plane(2, proj_refs, t_proj)
    qkv_sum = Plane(3, qkv_refs, t_qkv)
    small_sum = Plane(4, small_refs, t_small)
    proj_all = Plane(5, None, pg.at[1:NT])
    g_down, g_up, g_proj, g_qkv, g_small = (refs[0] for refs in (down_refs, up_refs, proj_refs, qkv_refs, small_refs))

    gather_start(0, xg, x_hbm)
    proj_rows = span(quarter * (hw // 4), hw // 4)

    def proj_piece(k):
        return piece_copy(8, pg.at[0, proj_rows, my_lanes], pg.at[NT - k, proj_rows, my_lanes], k)

    loads[8].wait()
    for k in range(1, NT):
        proj_piece(k).start()
    high = grids[0, 0]
    wide = grids[0, 1]
    down = lax.broadcasted_iota(i32, (seq, 1), 0)
    across = lax.broadcasted_iota(i32, (1, seq), 1)
    token_q, pad_q = query_tokens(down, high, wide)
    token_q_across, _ = query_tokens(across, high, wide)
    token_k = key_tokens(down, high, wide)
    token_k_across = key_tokens(across, high, wide)
    mq[...] = one_hot(token_q, across)
    mqt[...] = one_hot(down, token_q_across)
    mk[...] = one_hot(token_k, across)
    mkt[...] = one_hot(down, token_k_across)
    gexp[...] = jnp.zeros_like(gexp)
    tab[...] = jnp.zeros_like(tab)
    loads[3].wait()
    tab[0:heads, 0 : ENTRIES + 3] = rel[...]
    for h in range(heads):
        table = tab[h : h + 1, :]
        lined = pltpu.roll(jnp.broadcast_to(table, (24, TABLE)), TABLE - (GRID - 1), 1)
        uexp[...] = pltpu.roll(lined, 0, 1, stride=1, stride_axis=0)
        for x in range(SPAN):
            gexp[:, x * GRID : (x + 1) * GRID] = uexp[:, x * SPAN : x * SPAN + GRID]
        hankel = gexp[...]
        for r in range(GRID):
            moved = hankel if r == 0 else pltpu.roll(hankel, WIDE - r * GRID, 1)
            bias[h, r * GRID : (r + 1) * GRID, :] = moved[0:GRID, 0:seq]
        bias[h, CELLS:seq, :] = jnp.zeros((seq - CELLS, seq), f32)
        origin = bias[h, GRID - 1 : GRID, :]
        from_class = table[:, ENTRIES : ENTRIES + 1]
        to_class = table[:, ENTRIES + 1 : ENTRIES + 2]
        class_pair = table[:, ENTRIES + 2 : ENTRIES + 3]

        def settle(i, carry):
            part = pl.ds(pl.multiple_of(i * 128, 128), 128)
            place = lax.broadcasted_iota(i32, (128, 1), 0) + i * 128
            _, padded = query_tokens(place, high, wide)
            values = jnp.where(padded, origin, bias[h, part, :])
            values = jnp.where(across == CELLS, to_class, values)
            values = jnp.where(
                place == CELLS, jnp.where(across == CELLS, class_pair, from_class), values
            )
            bias[h, part, :] = jnp.where(token_k_across >= 0, values, masked)
            return carry

        lax.fori_loop(0, seq // 128, settle, 0)

    for i in (0, 4, 5, 6, 7):
        loads[i].wait()
    gain_one, shift_one = gains[0:1, :], biases[0:1, :]

    def project(s):
        normed, _ = normalize(xg[s].astype(f32))
        sent = (normed * gain_one + shift_one).astype(bf16)
        part = block(s)
        n1g[part, :] = sent
        qt[part, :] = ((dot_nt(sent, wqkv[0:hw, :]) + qvb[0:1, :]) * 0.125).astype(bf16)
        kt[part, :] = dot_nt(sent, wqkv[hw : 2 * hw, :]).astype(bf16)
        vt[part, :] = (dot_nt(sent, wqkv[2 * hw : 3 * hw, :]) + qvb[1:2, :]).astype(bf16)

    project(t)
    gather_near(0, xg)
    gather_take(0, xg, 1)
    project(order[1])
    gather_take(0, xg, 2)
    project(order[2])
    for k in range(1, NT):
        piece_arrived(8, pg.at[k, proj_rows, my_lanes], k)
    proj_all.send(3)
    gather_take(0, xg, 3)
    project(order[3])
    proj_all.spread_first()

    queries = dot(mq[...], qt[...]).astype(bf16)
    keys = dot(mk[...], kt[...]).astype(bf16)
    values = dot(mk[...], vt[...]).astype(bf16)
    for h in range(heads):
        lanes = slice(h * 64, (h + 1) * 64)
        qh[h] = queries[:, lanes]
        kh[h] = keys[:, lanes]
        vh[h] = values[:, lanes]
    for h in range(heads):
        logits = dot_nt(qh[h], kh[h]) + bias[h]
        raised = jnp.exp(logits - jnp.max(logits, axis=-1, keepdims=True))
        weights = raised * (1.0 / jnp.sum(raised, axis=-1, keepdims=True))
        prob[h] = weights
        rounded = weights.astype(bf16)
        probb[h] = rounded
        op[:, h * 64 : (h + 1) * 64] = dot(rounded, vh[h]).astype(bf16)
    ot[...] = dot(mqt[...], op[...]).astype(bf16)

    def mixed_piece(k):
        return piece_copy(2, ot.at[block((t + k) % NT), :], og.at[NT - k], k)

    for k in (2, 1, 3):
        mixed_piece(k).start()
    loads[1].wait()
    gather_start(1, cg)
    og[0] = ot[block(t), :]
    total = dot(og[0], pg[0])
    loads[2].wait()
    loads[12].wait()
    proj_all.spread_second()
    for k in range(1, NT):
        piece_arrived(2, og.at[k], k)
    proj_all.take(5)
    for k in range(1, NT):
        total = total + dot(og[k], pg[k])
    branch_one = total + obias[0:1, :]
    a1[...] = branch_one
    after_one = xg[t].astype(f32) + scales[0:1, :] * branch_one
    x1[...] = after_one
    normed, inverse = normalize(after_one)
    xhat2[...] = normed
    inv2[...] = jnp.broadcast_to(inverse, inv2.shape)
    n2g[t] = (normed * gains[1:2, :] + biases[1:2, :]).astype(bf16)
    gather_start(3, n2g)

    for i in (9, 10, 11):
        loads[i].wait()
    shift_up = b1[...].astype(f32)

    def feed(step):
        s = order[step]
        part = block(s)
        before = dot(n2g[s], w1[...]) + shift_up
        cumulative = 0.5 * (1.0 + lax.erf(before * 0.7071067811865476))
        slope = cumulative + before * (jnp.exp(-0.5 * before * before) * 0.3989422804014327)
        hid[part, :] = (before * cumulative).astype(bf16)
        grad_rows = (cg[s].astype(f32) * scales[1:2, :]).astype(bf16)
        dzg[s] = grad_rows
        grad_pre = (dot_nt(grad_rows, w2[...]) * slope).astype(bf16)
        du[part, :] = grad_pre
        back = dot_nt(grad_pre, w1[...])
        if step == 0:
            dn2own[...] = back
        else:
            stage_b[3 - step] = back.astype(bf16)
        return jnp.sum(grad_pre.astype(f32), axis=0, keepdims=True)

    bias_up = feed(0)
    gather_near(1, cg)
    gather_near(3, n2g)
    gather_take(1, cg, 1)
    gather_take(3, n2g, 1)
    bias_up = bias_up + feed(1)
    scatter_copy(4, stage_b, dn2r, 2).start()
    gather_take(1, cg, 2)
    gather_take(1, cg, 3)
    gather_take(3, n2g, 2)
    bias_up = bias_up + feed(2)
    scatter_send(4, stage_b, dn2r, 1)
    gather_take(3, n2g, 3)
    bias_up = bias_up + feed(3)
    far_copy(4, stage_b, dn2r).start()
    sums[8:9, :] = bias_up
    scatter_merge(4, stage_b, dn2r, 1)
    down_rows = jnp.reshape(dzg[...], (seq, width))
    g_down[0] = dot_tn(hid[...], down_rows).astype(bf16)
    down_sum.send(0)
    up_rows = jnp.reshape(n2g[...], (seq, width))
    g_up[0] = dot_tn(up_rows, du[...]).astype(bf16)
    up_sum.send(0)
    shared = jnp.zeros((1, width), f32)
    for step, s in enumerate(order):
        piece = dot(hid[block(s), :], w2[...])
        shared = shared + jnp.sum(cg[s].astype(f32) * piece, axis=0, keepdims=True)
        if step == 0:
            own[...] = piece
        else:
            stage_c[3 - step] = piece.astype(bf16)
    cot = cg[t].astype(f32)
    cot_sum = jnp.sum(cot, axis=0, keepdims=True)
    sums[5:6, :] = shared + cot_sum * obias[1:2, :]
    sums[7:8, :] = cot_sum * scales[1:2, :]
    down_sum.add_core()
    up_sum.add_core()

    @pl.when(end == 1)
    def _():
        slot_wait(4, dn2r, 0)
        dn2own[...] = dn2own[...] + dn2r[0].astype(f32)

    total = scatter_total(4, dn2r, dn2own[...])
    normed = xhat2[...]
    sums[3:4, :] = jnp.sum(total, axis=0, keepdims=True)
    sums[1:2, :] = jnp.sum(total * normed, axis=0, keepdims=True)
    after = cg[t].astype(f32) + norm_back(total * gains[1:2, :], normed, inv2[:, 0:1])
    dx1[...] = after
    branch = after * scales[0:1, :]
    grad_rows = branch.astype(bf16)

    def mixed_back(k):
        return piece_copy(6, doz.at[k], dot_t.at[block(t), :], k)

    for k in (2, 1, 3, 0):
        piece = dot_nt(grad_rows, pg[k]).astype(bf16)
        if k == 0:
            dot_t[block(t), :] = piece
        else:
            doz[k] = piece
            mixed_back(k).start()
    for i in range(NT - 1):
        scatter_send(5, stage_c, z2r, i)
    sums[4:5, :] = jnp.sum(after * a1[...], axis=0, keepdims=True)
    sums[6:7, :] = jnp.sum(branch, axis=0, keepdims=True)
    for k in range(NT):
        g_proj[k] = dot_tn(og[k], grad_rows).astype(bf16)
    proj_sum.send(0)
    down_sum.add_first()
    proj_sum.add_core()

    for k in range(1, NT):
        piece_arrived(6, dot_t.at[block((t + k) % NT), :], k)
    grad_mixed = dot(mq[...], dot_t[...]).astype(bf16)
    for h in range(heads):
        doh[h] = grad_mixed[:, h * 64 : (h + 1) * 64]
    up_sum.add_first()
    for h in range(heads):
        lanes = slice(h * 64, (h + 1) * 64)

        grad_prob = dot_nt(doh[h], vh[h])
        weights = prob[h]
        crossed = jnp.sum(weights * grad_prob, axis=-1, keepdims=True)
        rounded = (weights * (grad_prob - crossed)).astype(bf16)
        ds[h] = rounded
        dqp[:, lanes] = dot(rounded, kh[h]).astype(bf16) * 0.125
        dvp[:, lanes] = dot_tn(probb[h], doh[h]).astype(bf16)
        dkp[:, lanes] = dot_tn(rounded, qh[h]).astype(bf16)
        if h == 0:
            down_sum.add_second()
            proj_sum.add_first()
            scatter_merge(5, stage_c, z2r, 0)
        elif h == 1:
            up_sum.add_second()
            scatter_merge(5, stage_c, z2r, 1)
    proj_sum.add_second(gpz)

    def proj_exchange(k):
        return piece_copy(9, gpz.at[k], gpz.at[2 * NT - k], k)

    for k in range(1, NT):
        proj_exchange(k).start()
    down_sum.spread_first()
    dqt[...] = dot(mqt[...], dqp[...]).astype(bf16)
    dkt[...] = dot(mkt[...], dkp[...]).astype(bf16)
    dvt[...] = dot(mkt[...], dvp[...]).astype(bf16)

    shift_total = jnp.zeros((1, width), f32)
    gain_total = jnp.zeros((1, width), f32)
    for step in (3, 2, 1, 0):
        s = order[step]
        part = block(s)
        piece = dot(dqt[part, :], wqkv[0:hw, :]) + dot(dkt[part, :], wqkv[hw : 2 * hw, :])
        piece = piece + dot(dvt[part, :], wqkv[2 * hw : 3 * hw, :])
        if step == 0:
            dn2own[...] = piece
        else:
            stage_d[3 - step] = piece.astype(bf16)
        normed, _ = normalize(xg[s].astype(f32))
        shift_total = shift_total + jnp.sum(piece, axis=0, keepdims=True)
        gain_total = gain_total + jnp.sum(piece * normed, axis=0, keepdims=True)
    sums[2:3, :] = shift_total
    sums[0:1, :] = gain_total
    zmr[t] = sums[0:REP, :]

    def small_tensor(k):
        return remote(
            zmr.at[t], zmr.at[t], z_send.at[10, k], z_recv.at[10, NT - k], (dp, (t + k) % NT)
        )

    for k in range(1, NT):
        small_tensor(k).start()
    for i in range(NT - 1):
        scatter_send(7, stage_d, dn1r, i)
    g_qkv[0, 0:hw, :] = dot_tn(dqt[...], n1g[...]).astype(bf16)
    g_qkv[0, hw : 2 * hw, :] = dot_tn(dkt[...], n1g[...]).astype(bf16)
    g_qkv[0, 2 * hw : 3 * hw, :] = dot_tn(dvt[...], n1g[...]).astype(bf16)
    qkv_sum.send(0)

    branch_two = scatter_total(5, z2r, own[...]) + obias[1:2, :]
    outv[...] = (x1[...] + scales[1:2, :] * branch_two).astype(bf16)
    stores = [pltpu.make_async_copy(outv, out, store_sem.at[5])]
    stores[0].start()
    qkv_sum.add_core()
    up_sum.spread_first()
    scatter_merge(7, stage_d, dn1r, 0)

    row24 = lax.broadcasted_iota(i32, (24, 1), 0)
    lane_t = lax.broadcasted_iota(i32, (1, TABLE), 1)
    uexp[...] = jnp.zeros_like(uexp)
    gexp[...] = jnp.zeros_like(gexp)
    for h in range(heads):
        grads = ds[h].astype(f32)
        class_row = grads[CELLS : CELLS + 1, :]
        class_column = jnp.sum(
            jnp.where((down != CELLS) & (across == CELLS), grads, 0.0), axis=0, keepdims=True
        )
        cells = jnp.where(across < CELLS, grads, 0.0)
        pad_row = jnp.sum(jnp.where(pad_q, cells, 0.0), axis=0, keepdims=True)
        dsf[...] = jnp.where(pad_q, 0.0, cells)
        blank = jnp.zeros((24, WIDE - seq), f32)
        folded = jnp.zeros((24, WIDE), f32)
        for r in range(GRID):
            cells = jnp.concatenate([dsf[r * GRID : r * GRID + 24, :], blank], axis=1)
            folded = folded + (cells if r == 0 else pltpu.roll(cells, r * GRID, 1))
        padded_row = jnp.concatenate([pad_row, jnp.zeros((1, WIDE - seq), f32)], axis=1)
        folded = jnp.where(row24 < GRID, folded, 0.0) + jnp.where(row24 == GRID - 1, padded_row, 0.0)
        for i in range(GRID):
            gexp[GRID - 1 - i : GRID - i, :] = folded[i : i + 1, :]
        for x in range(SPAN):
            uexp[:, x * SPAN : x * SPAN + GRID] = gexp[:, x * GRID : (x + 1) * GRID]
        lined = pltpu.roll(uexp[...], 0, 1, stride=1, stride_axis=0)
        table = jnp.sum(lined, axis=0, keepdims=True)
        from_class = jnp.sum(jnp.where(across != CELLS, class_row, 0.0), axis=1, keepdims=True)
        class_pair = jnp.sum(jnp.where(across == CELLS, class_row, 0.0), axis=1, keepdims=True)
        to_class = jnp.sum(class_column, axis=1, keepdims=True)
        table = jnp.where(lane_t == ENTRIES, from_class, table)
        table = jnp.where(lane_t == ENTRIES + 1, to_class, table)
        tab[h : h + 1, :] = jnp.where(lane_t == ENTRIES + 2, class_pair, table)
    sums[9:10, 0:hw] = jnp.sum(dqt[...].astype(f32), axis=0, keepdims=True)
    sums[10:11, 0:hw] = jnp.sum(dvt[...].astype(f32), axis=0, keepdims=True)
    sums[9:11, hw:width] = jnp.zeros((2, width - hw), f32)
    for h in range(heads):
        at = 11 + 3 * h
        sums[at : at + 1, :] = tab[h : h + 1, 0:width]
        sums[at + 1 : at + 2, :] = tab[h : h + 1, width : 2 * width]
        sums[at + 2 : at + 3, 0 : TABLE - 2 * width] = tab[h : h + 1, 2 * width : TABLE]
        sums[at + 2 : at + 3, TABLE - 2 * width : width] = jnp.zeros((1, 3 * width - TABLE), f32)
    sums[11 + 3 * heads : SMALL, :] = jnp.zeros((SMALL - 11 - 3 * heads, width), f32)

    qkv_sum.add_first()
    scatter_merge(7, stage_d, dn1r, 1)
    for k in range(1, NT):
        piece_arrived(10, zmr.at[(t + k) % NT], k)
    sums[0:REP, :] = zmr[0] + zmr[1] + zmr[2] + zmr[3]
    g_small[0] = sums[...].astype(bf16)
    small_sum.send(0)
    value = gpz[0].astype(f32)
    for k in range(1, NT):
        piece_arrived(9, gpz.at[NT + k], k)
        value = value + gpz[NT + k].astype(f32)
    t_proj[0, proj_rows, my_lanes] = value.astype(bf16)
    proj_sum.send(3)
    down_sum.spread_second()
    qkv_sum.add_second()
    small_sum.add_core()
    up_sum.spread_second()
    proj_sum.spread_first()
    small_sum.add_first()
    qkv_sum.spread_first()
    stores += [
        pltpu.make_async_copy(src.at[0], dst, store_sem.at[i])
        for i, (src, dst) in enumerate(
            [(t_down, t_down_hbm), (t_up, t_up_hbm), (t_proj, t_proj_hbm), (t_qkv, t_qkv_hbm), (t_small, t_small_hbm)]
        )
    ]
    down_sum.take(5)
    stores[1].start()
    small_sum.add_second()
    total = scatter_total(7, dn1r, dn2own[...])
    normed, inverse = normalize(xg[t].astype(f32))
    ingradv[...] = dx1[...] + norm_back(total * gain_one, normed, inverse)
    stores.append(pltpu.make_async_copy(ingradv, ingrad, store_sem.at[6]))
    stores[6].start()
    up_sum.take(5)
    stores[2].start()
    small_sum.spread_first()
    proj_sum.spread_second()
    qkv_sum.spread_second()
    small_sum.spread_second()
    proj_sum.take(5)
    stores[3].start()
    qkv_sum.take(5)
    stores[4].start()
    small_sum.take(5)
    stores[5].start()

    gather_sent(0, xg, x_hbm)
    gather_sent(1, cg)
    gather_sent(3, n2g)
    for phase, stage, buf in ((4, stage_b, dn2r), (5, stage_c, z2r), (7, stage_d, dn1r)):
        for i in range(NT - 1):
            if phase == 4 and i == 0:
                far_copy(phase, stage, buf).wait_send()
            else:
                scatter_copy(phase, stage, buf, i).wait_send()
    for k in range(1, NT):
        proj_piece(k).wait_send()
        mixed_piece(k).wait_send()
        mixed_back(k).wait_send()
        proj_exchange(k).wait_send()
        small_tensor(k).wait_send()
    for part_sum in (down_sum, up_sum, proj_sum, qkv_sum, small_sum):
        part_sum.sent()
    proj_all.sent(3)
    for store in stores:
        store.wait()


def finish_kernel(
    down_in, up_in, proj_in, qkv_in, small_in, out_in, ingrad_in,
    out, ingrad, g_qkv, g_qv, g_table, g_proj, g_up, g_up_bias, g_down, g_gains, g_shifts, g_scales, g_biases,
    down_v, up_v, proj_v, qkv_v, down_f, up_f, proj_f, qkv_f, small_v, out_v, ingrad_v, load_sem, store_sem,
):
    width = g_down.shape[1]
    hw = g_proj.shape[0]
    heads, entries = g_table.shape
    parts = []
    for given, rounded, widened, result in (
        (down_in, down_v, down_f, g_down), (up_in, up_v, up_f, g_up),
        (qkv_in, qkv_v, qkv_f, g_qkv), (proj_in, proj_v, proj_f, g_proj),
    ):
        for start in range(0, given.shape[0], PIECE):
            parts.append([ref.at[start : start + PIECE, :] for ref in (given, rounded, widened, result)])
    moved = [(small_in, small_v, None), (out_in, out_v, out), (ingrad_in, ingrad_v, ingrad)]
    count = len(parts)
    loads = [pltpu.make_async_copy(part[0], part[1], load_sem.at[i]) for i, part in enumerate(parts)]
    loads += [pltpu.make_async_copy(src, via, load_sem.at[count + i]) for i, (src, via, _) in enumerate(moved)]
    for copy in loads:
        copy.start()
    stores = []
    for i, (_, rounded, widened, result) in enumerate(parts):
        loads[i].wait()
        widened[...] = rounded[...].astype(f32)
        stores.append(pltpu.make_async_copy(widened, result, store_sem.at[i]))
        stores[-1].start()
    for i, (_, via, dst) in enumerate(moved):
        loads[count + i].wait()
        if dst is not None:
            stores.append(pltpu.make_async_copy(via, dst, store_sem.at[count + i]))
            stores[-1].start()
    small = small_v[...].astype(f32)
    g_gains[...] = small[0:2, :]
    g_shifts[...] = small[2:4, :]
    g_scales[...] = small[4:6, :]
    g_biases[...] = small[6:8, :]
    g_up_bias[...] = small[8:9, :]
    g_qv[...] = small[9:11, 0:hw]
    for h in range(heads):
        for j in range(3):
            lanes = min(width, entries - j * width)
            g_table[h : h + 1, j * width : j * width + lanes] = small[
                11 + 3 * h + j : 12 + 3 * h + j, 0:lanes
            ]
    for copy in stores:
        copy.wait()


def per_device(
    n_dp, tokens, grids, qkv_weight, qv_bias, rel_table, proj_weight, fc1_weight, fc1_bias, fc2_weight,
    norm_gains, norm_biases, layer_scales, out_biases, cotangent,
):
    rows, width = tokens.shape
    seq = rows * NT
    heads, entries = rel_table.shape
    hw = heads * 64
    ff = fc1_weight.shape[1]
    qkv_rows = jnp.transpose(qkv_weight, (1, 2, 0)).reshape(3 * hw, width)
    vm = pl.BlockSpec(memory_space=pltpu.VMEM)
    anywhere = pl.BlockSpec(memory_space=pl.ANY)

    def many(count, shape, dtype):
        return [pltpu.VMEM(shape, dtype)] * count

    def sems(*shape):
        return [pltpu.SemaphoreType.DMA(shape)]

    half = width // 2
    scratch = [
        pltpu.VMEM((rows, width), bf16), pltpu.VMEM((rows, width), f32), pltpu.VMEM((3 * hw, width), bf16),
        pltpu.VMEM((width, ff), bf16), pltpu.VMEM((ff, width), bf16),
        pltpu.VMEM((2, hw), f32), pltpu.VMEM((heads, entries), f32), pltpu.VMEM((1, ff), bf16),
    ]
    scratch += many(4, (2, width), f32) + sems(13) + sems(7)
    scratch += many(4, (NT, rows, width), bf16)
    scratch += many(1, (NT, rows, hw), bf16) + many(1, (NT, hw, width), bf16)
    scratch += many(3, (NT, rows, width), bf16) + many(3, (NT - 1, rows, width), bf16)
    scratch += many(1, (NT, rows, hw), bf16) + sems(11, NT) + sems(11, 2 * NT) + sems(4, 5, 2)
    scratch += many(4, (seq, seq), bf16)
    scratch += many(1, (heads, seq, seq), f32) + many(1, (24, WIDE), f32) + many(1, (24, TABLE), f32)
    scratch += many(1, (seq, width), bf16) + many(3, (seq, hw), bf16)
    scratch += many(3, (heads, seq, 64), bf16)
    scratch += many(1, (heads, seq, seq), f32) + many(1, (heads, seq, seq), bf16)
    scratch += many(2, (seq, hw), bf16)
    scratch += many(2, (rows, width), f32) + many(1, (rows, 128), f32) + many(4, (rows, width), f32)
    scratch += many(2, (seq, ff), bf16) + many(1, (seq, hw), bf16) + many(1, (heads, seq, 64), bf16)
    scratch += many(1, (heads, seq, seq), bf16) + many(1, (seq, seq), f32) + many(6, (seq, hw), bf16)
    scratch += many(1, (8, TABLE), f32) + many(1, (SMALL, width), f32) + many(1, (NT, REP, width), f32)
    scratch += many(1, (2 * NT, hw // 4, half), bf16) + sems(6, 6) + sems(6, 6)
    kinds = ((1, ff), (1, width), (NT, hw), (1, 3 * hw), (1, SMALL))
    for lead, count in kinds:
        scratch += [
            pltpu.VMEM((lead, count, width), bf16), pltpu.VMEM((lead, count, half), bf16),
            pltpu.VMEM((lead, count, half), bf16), pltpu.VMEM((lead, count // 2, half), bf16),
            pltpu.VMEM((lead, count // 4, half), bf16),
        ]
    for lead, count in kinds:
        scratch += many(1, (1, count, width), bf16)
    flat = [jax.ShapeDtypeStruct((count, width), bf16) for lead, count in kinds]
    output, input_grad, *totals = pl.pallas_call(
        main_kernel,
        out_shape=[
            jax.ShapeDtypeStruct((rows, width), bf16),
            jax.ShapeDtypeStruct((rows, width), f32),
        ]
        + flat,
        in_specs=[pl.BlockSpec(memory_space=pltpu.SMEM)] + [anywhere] * 13,
        out_specs=[anywhere] * 7,
        scratch_shapes=scratch,
        compiler_params=pltpu.CompilerParams(
            collective_id=0, has_side_effects=True, vmem_limit_bytes=60 << 20
        ),
        name="layer",
    )(
        grids, tokens, cotangent, qkv_rows, proj_weight, fc1_weight, fc2_weight,
        qv_bias, rel_table, fc1_bias.reshape(1, ff), norm_gains, norm_biases, layer_scales, out_biases,
    )
    pair = jax.ShapeDtypeStruct((2, width), f32)
    pieces = sum(-(-count // PIECE) for count in (ff, width, hw, 3 * hw))
    results = pl.pallas_call(
        finish_kernel,
        out_shape=(
            jax.ShapeDtypeStruct((rows, width), bf16),
            jax.ShapeDtypeStruct((rows, width), f32),
            jax.ShapeDtypeStruct((3 * hw, width), f32),
            jax.ShapeDtypeStruct((2, hw), f32),
            jax.ShapeDtypeStruct((heads, entries), f32),
            jax.ShapeDtypeStruct((hw, width), f32),
            jax.ShapeDtypeStruct((width, ff), f32),
            jax.ShapeDtypeStruct((1, ff), f32),
            jax.ShapeDtypeStruct((ff, width), f32),
            pair, pair, pair, pair,
        ),
        in_specs=[anywhere] * 7,
        out_specs=(
            anywhere, anywhere, anywhere, vm, vm, anywhere, anywhere, vm, anywhere, vm, vm, vm, vm,
        ),
        scratch_shapes=[
            pltpu.VMEM((ff, width), bf16), pltpu.VMEM((width, ff), bf16), pltpu.VMEM((hw, width), bf16),
            pltpu.VMEM((3 * hw, width), bf16),
            pltpu.VMEM((ff, width), f32), pltpu.VMEM((width, ff), f32), pltpu.VMEM((hw, width), f32),
            pltpu.VMEM((3 * hw, width), f32), pltpu.VMEM((SMALL, width), bf16),
            pltpu.VMEM((rows, width), bf16), pltpu.VMEM((rows, width), f32),
            *sems(pieces + 3), *sems(pieces + 3),
        ],
        compiler_params=pltpu.CompilerParams(vmem_limit_bytes=60 << 20),
        name="finish",
    )(*totals, output, input_grad)
    results = list(results)
    stride = GROUP
    while stride < n_dp:
        hops = [(i, i ^ stride) for i in range(n_dp)]
        results[2:] = [value + lax.ppermute(value, "dp", hops) for value in results[2:]]
        stride *= 2
    results[2] = jnp.transpose(results[2].reshape(3, hw, width), (2, 0, 1))
    results[7] = results[7].reshape(ff)
    return tuple(results)


def solution(mesh):
    n_dp = mesh.shape["dp"]
    blocks = P(("dp", "tensor"), None)
    placed = (
        blocks, P("dp", None), P(None, None, "tensor"), P(None, "tensor"), P("tensor", None), P("tensor", None),
        P(None, "tensor"), P("tensor"), P("tensor", None), P(), P(), P(), P(), blocks,
    )
    given = (
        blocks, blocks, P(None, None, "tensor"), P(None, "tensor"), P("tensor", None), P("tensor", None),
        P(None, "tensor"), P("tensor"), P("tensor", None), P(), P(), P(), P(),
    )

    def layer(*arrays):
        return per_device(n_dp, *arrays)

    return jax.shard_map(layer, mesh=mesh, in_specs=placed, out_specs=given, check_vma=False)
```

```python
import jax
import jax.numpy as jnp
from jax import lax
from jax.experimental import pallas as pl
from jax.experimental.pallas import tpu as pltpu
from jax.sharding import PartitionSpec as P

GRID = 22
SPAN = 2 * GRID - 1
CELLS = GRID * GRID
ENTRIES = SPAN * SPAN
MESH = pl.DeviceIdType.MESH
f32 = jnp.float32
bf16 = jnp.bfloat16
i32 = jnp.int32

eps_norm = 1e-06
masked = -1e30
NT = 4
CHIPS = 4
CORES = 2
GROUP = CHIPS * CORES
TABLE = 1920
WIDE = 1024
SMALL = 64
REP = 8
PIECE = 192


def dot(left, right):
    return lax.dot_general(left, right, (((1,), (0,)), ((), ())), preferred_element_type=f32)


def dot_nt(left, right):
    return lax.dot_general(left, right, (((1,), (1,)), ((), ())), preferred_element_type=f32)


def dot_tn(left, right):
    return lax.dot_general(left, right, (((0,), (0,)), ((), ())), preferred_element_type=f32)


def normalize(values):
    center = values - jnp.mean(values, axis=-1, keepdims=True)
    inverse = lax.rsqrt(jnp.mean(center * center, axis=-1, keepdims=True) + eps_norm)
    return center * inverse, inverse


def norm_back(grad_normed, normed, inverse):
    average = jnp.mean(grad_normed, axis=-1, keepdims=True)
    crossed = jnp.mean(grad_normed * normed, axis=-1, keepdims=True)
    return inverse * (grad_normed - average - normed * crossed)


def split_cell(place):
    row = (place * 2979) >> 16
    return row, place - row * GRID


def query_tokens(place, high, wide):
    row, back = split_cell(place)
    inside = (place < CELLS) & (row < high) & (GRID - 1 - back < wide)
    before = jnp.minimum(row, high) * wide + jnp.where(
        row < high, jnp.maximum(back - (GRID - wide), 0), 0
    )
    token = jnp.where(inside, 1 + row * wide + (GRID - 1 - back), high * wide + 1 + place - before)
    token = jnp.where(place == CELLS, 0, jnp.where(place > CELLS, place, token))
    padding = jnp.logical_not(inside) & (place != CELLS)
    return token, padding


def key_tokens(place, high, wide):
    row, back = split_cell(place)
    row = GRID - 1 - row
    column = GRID - 1 - back
    inside = (place < CELLS) & (row < high) & (column < wide)
    token = jnp.where(inside, 1 + row * wide + column, -1)
    return jnp.where(place == CELLS, 0, token)


def one_hot(left, right):
    return jnp.where(left == right, 1.0, 0.0).astype(bf16)


def main_kernel(
    grids, x_hbm, cot_hbm, wqkv_hbm, wproj_hbm, w1_hbm, w2_hbm, qvb_hbm, rel_hbm, b1_hbm,
    gains_hbm, biases_hbm, scales_hbm, obias_hbm,
    out, ingrad, t_down_hbm, t_up_hbm, t_proj_hbm, t_qkv_hbm, t_small_hbm,
    outv, ingradv, wqkv, w1, w2, qvb, rel, b1, gains, biases, scales, obias, load_sem, store_sem,
    xg, cg, dzg, n2g, og, pg, dn2r, z2r, dn1r, stage_b, stage_c, stage_d, doz, z_send, z_recv, z_half,
    mq, mqt, mk, mkt, bias, gexp, uexp,
    n1g, qt, kt, vt, qh, kh, vh, prob, probb, op, ot,
    x1, xhat2, inv2, a1, dx1, own, dn2own,
    hid, du, dot_t, doh, ds, dsf, dqp, dkp, dvp, dqt, dkt, dvt,
    tab, sums, zmr, gpz, p_send, p_recv,
    *plane,
):
    dp = lax.axis_index("dp")
    t = lax.axis_index("tensor")
    rows, width = x_hbm.shape
    seq = rows * NT
    heads = rel.shape[0]
    hw = heads * 64
    base = (dp // GROUP) * GROUP
    mine = dp % GROUP
    core = mine % CORES
    chip_x = (mine // 2) % 2
    chip_y = mine // 4
    to_x = 2 - 4 * chip_x
    to_y = 4 - 8 * chip_y
    sibling = base + mine + 1 - 2 * core
    first_peer = base + mine + (1 - core) * to_x + core * to_y
    second_peer = base + mine + core * to_x + (1 - core) * to_y
    bit_one = (1 - core) * chip_x + core * chip_y
    bit_two = core * chip_x + (1 - core) * chip_y
    quarter = bit_one * 2 + bit_two
    end = ((t - 1) * (t - 2)) // 2
    order = [t, t + 1 - 2 * (t % 2), 2 - t // 2, 3 - 3 * (t // 2)]

    pairs = [
        (x_hbm, xg.at[t]), (cot_hbm, cg.at[t]), (scales_hbm, scales), (rel_hbm, rel), (wqkv_hbm, wqkv),
        (gains_hbm, gains), (biases_hbm, biases), (qvb_hbm, qvb), (wproj_hbm, pg.at[0]), (w1_hbm, w1),
        (w2_hbm, w2), (b1_hbm, b1), (obias_hbm, obias),
    ]
    loads = [pltpu.make_async_copy(src, dst, load_sem.at[i]) for i, (src, dst) in enumerate(pairs)]
    for load in loads:
        load.start()
    barrier = pltpu.get_barrier_semaphore()
    for k in range(1, NT):
        pl.semaphore_signal(barrier, inc=1, device_id=(dp, (t + k) % NT), device_id_type=MESH)
    chip = mine // CORES
    others = [base + ((chip + k) % CHIPS) * CORES + core for k in range(CHIPS)]
    for peer in (sibling, *others[1:]):
        pl.semaphore_signal(barrier, inc=1, device_id=(peer, t), device_id_type=MESH)
    pl.semaphore_wait(barrier, NT - 1 + CHIPS)

    def block(s):
        return pl.ds(pl.multiple_of(s * rows, rows), rows)

    def remote(src, dst, send, recv, device):
        return pltpu.make_async_remote_copy(
            src_ref=src, dst_ref=dst, send_sem=send, recv_sem=recv, device_id=device, device_id_type=MESH
        )

    half_rows = rows // 2

    def half_copy(phase, buf, src, half, dst, way, given=None):
        spot = buf.at[src, half * half_rows : (half + 1) * half_rows, :]
        if given is not None:
            given = given.at[half * half_rows : (half + 1) * half_rows, :]
        return remote(
            spot if given is None else given, spot,
            z_half.at[phase, way, half], z_recv.at[phase, src * 2 + half], (dp, dst),
        )

    def gather_start(phase, buf, given=None):
        for half in range(2):
            half_copy(phase, buf, t, half, order[1], 0, given).start()
            pl.when(end == 0)(half_copy(phase, buf, t, half, order[2], 1, given).start)

    def half_arrived(phase, buf, step, half):
        half_copy(phase, buf, order[step], half, order[1], 0).wait_recv()

    def half_forward(phase, buf, step, half):
        to = order[2] if step == 1 else order[1]
        half_copy(phase, buf, order[step], half, to, 1 + step).start()

    def gather_near(phase, buf):
        @pl.when(end == 0)
        def _():
            for half in range(2):
                for step in (1, 2):
                    half_arrived(phase, buf, step, half)
                    half_forward(phase, buf, step, half)

    def forward_both(phase, buf, step):
        @pl.when(end == 0)
        def _():
            for half in range(2):
                half_arrived(phase, buf, step, half)
                half_forward(phase, buf, step, half)

    def end_take(phase, buf, step):
        for half in range(2):
            pl.when(end == 1)(lambda: half_arrived(phase, buf, step, half))

    def gather_take(phase, buf, step):
        for half in range(2):
            if step < 3:
                pl.when(end == 1)(lambda: half_arrived(phase, buf, step, half))
            else:
                half_arrived(phase, buf, step, half)
                pl.when(end == 0)(lambda: half_forward(phase, buf, step, half))

    def gather_sent(phase, buf, given=None):
        for half in range(2):
            half_copy(phase, buf, t, half, order[1], 0, given).wait_send()

            @pl.when(end == 0)
            def _():
                half_copy(phase, buf, t, half, order[2], 1, given).wait_send()
                for step in (1, 2, 3):
                    half_copy(phase, buf, order[step], half, order[1], 1 + step).wait_send()

    def scatter_copy(phase, stage, buf, i):
        if i == 2:
            dst, slot = order[1], 2
        else:
            dst = end * order[1] + (1 - end) * order[3 - i]
            slot = end * i + (1 - end) * 3
        return remote(
            stage.at[i], buf.at[slot], z_send.at[phase, i], z_recv.at[phase, slot], (dp, dst)
        )

    def slot_wait(phase, buf, slot):
        remote(
            buf.at[slot], buf.at[slot], z_send.at[phase, 0], z_recv.at[phase, slot], (dp, order[1])
        ).wait_recv()

    def scatter_send(phase, stage, buf, i):
        if i == 2:
            scatter_copy(phase, stage, buf, i).start()
        else:
            pl.when(end == 1)(scatter_copy(phase, stage, buf, i).start)

    def scatter_merge(phase, stage, buf, i):
        @pl.when(end == 0)
        def _():
            slot_wait(phase, buf, i)
            stage[i] = (stage[i].astype(f32) + buf[i].astype(f32)).astype(bf16)
            scatter_copy(phase, stage, buf, i).start()

    def far_copy(phase, stage, buf):
        dst = order[3]
        slot = (1 - end) * 3
        return remote(stage.at[0], buf.at[slot], z_send.at[phase, 0], z_recv.at[phase, slot], (dp, dst))

    def scatter_total(phase, buf, total):
        for slot in (2, 3):
            slot_wait(phase, buf, slot)
            total = total + buf[slot].astype(f32)
        return total

    def piece_copy(phase, src, dst, k):
        return remote(
            src, dst, z_send.at[phase, k], z_recv.at[phase, NT - k], (dp, (t + k) % NT)
        )

    def piece_arrived(phase, dst, k):
        remote(dst, dst, z_send.at[phase, k], z_recv.at[phase, k], (dp, (t + k) % NT)).wait_recv()

    half_width = width // 2
    my_lanes = pl.ds(pl.multiple_of(core * half_width, half_width), half_width)
    your_lanes = pl.ds(pl.multiple_of((1 - core) * half_width, half_width), half_width)

    def span(start, count):
        return pl.ds(pl.multiple_of(start, 16), count)

    class Plane:
        def __init__(self, index, refs, target):
            self.index, self.target = index, target
            self.count = target.shape[1]
            self.fours = self.count // 4
            if refs is not None:
                self.given, self.near, self.held, self.one, self.two = refs
                self.lead = self.given.shape[0]

        def copy(self, step, src, dst, peer):
            return remote(
                src, dst, p_send.at[self.index, step], p_recv.at[self.index, step], (peer, t)
            )

        def outgoing(self, step):
            c, f = self.count, self.fours
            if step == 0:
                return self.copy(0, self.given.at[:, :, your_lanes], self.near, sibling)
            if step == 1:
                src = self.held.at[:, span((1 - bit_one) * 2 * f, 2 * f), :]
                return self.copy(1, src, self.one, first_peer)
            if step == 2:
                src = self.held.at[:, span((bit_one * 2 + 1 - bit_two) * f, f), :]
                return self.copy(2, src, self.two, second_peer)
            if step == 3:
                spot, peer = self.target.at[:, span(quarter * f, f), my_lanes], second_peer
            elif step == 4:
                spot, peer = self.target.at[:, span(bit_one * 2 * f, 2 * f), my_lanes], first_peer
            else:
                spot, peer = self.target.at[:, :, my_lanes], sibling
            return self.copy(step, spot, spot, peer)

        def incoming(self, step):
            f = self.fours
            if step < 3:
                return self.outgoing(step)
            if step == 3:
                spot = self.target.at[:, span((bit_one * 2 + 1 - bit_two) * f, f), my_lanes]
            elif step == 4:
                spot = self.target.at[:, span((1 - bit_one) * 2 * f, 2 * f), my_lanes]
            else:
                spot = self.target.at[:, :, your_lanes]
            return self.copy(step, spot, spot, sibling)

        def send(self, step):
            self.outgoing(step).start()

        def take(self, step):
            self.incoming(step).wait_recv()

        def add_core(self):
            self.take(0)
            for q in range(self.lead):
                value = self.given[q, :, my_lanes].astype(f32) + self.near[q].astype(f32)
                self.held[q] = value.astype(bf16)
            self.send(1)

        def add_first(self):
            self.take(1)
            part = span(bit_one * 2 * self.fours, 2 * self.fours)
            for q in range(self.lead):
                value = self.held[q, part, :].astype(f32) + self.one[q].astype(f32)
                self.held[q, part, :] = value.astype(bf16)
            self.send(2)

        def add_second(self, store=None):
            self.take(2)
            part = span(quarter * self.fours, self.fours)
            for q in range(self.lead):
                value = (self.held[q, part, :].astype(f32) + self.two[q].astype(f32)).astype(bf16)
                if store is None:
                    self.target[q, part, my_lanes] = value
                else:
                    store[q] = value
            if store is None:
                self.send(3)

        def spread_first(self):
            self.take(3)
            self.send(4)

        def spread_second(self):
            self.take(4)
            self.send(5)

        def sent(self, first=0):
            for step in range(first, 6):
                self.outgoing(step).wait_send()

    class Direct:
        def __init__(self, index, refs, target):
            self.index, self.target = index, target
            self.fours = target.shape[1] // CHIPS
            self.given, self.near, self.held, self.parts = refs

        def copy(self, step, src, dst, peer):
            return remote(
                src, dst, p_send.at[self.index, step], p_recv.at[self.index, step], (peer, t)
            )

        def rows_of(self, k):
            return span(((chip + k) % CHIPS) * self.fours, self.fours)

        def core_copy(self):
            return self.copy(0, self.given.at[:, your_lanes], self.near, sibling)

        def part_copy(self, k):
            return self.copy(k, self.held.at[self.rows_of(k), :], self.parts.at[k - 1], others[k])

        def back_copy(self, k):
            spot = self.target.at[0, self.rows_of(0), my_lanes]
            return self.copy(3 + k, spot, spot, others[k])

        def pair_copy(self):
            spot = self.target.at[0, :, my_lanes]
            return self.copy(7, spot, spot, sibling)

        def send(self):
            self.core_copy().start()

        def add_core(self):
            self.core_copy().wait_recv()
            value = self.given[:, my_lanes].astype(f32) + self.near[...].astype(f32)
            self.held[...] = value.astype(bf16)
            for k in (2, 1, 3):
                self.part_copy(k).start()

        def add_parts(self):
            value = self.held[self.rows_of(0), :].astype(f32)
            for k in range(1, CHIPS):
                self.part_copy(k).wait_recv()
                value = value + self.parts[k - 1].astype(f32)
            self.target[0, self.rows_of(0), my_lanes] = value.astype(bf16)
            for k in (2, 1, 3):
                self.back_copy(k).start()

        def spread(self):
            for k in range(1, CHIPS):
                spot = self.target.at[0, self.rows_of(CHIPS - k), my_lanes]
                self.copy(3 + k, spot, spot, others[k]).wait_recv()
            self.pair_copy().start()

        def take(self):
            spot = self.target.at[0, :, your_lanes]
            self.copy(7, spot, spot, sibling).wait_recv()

        def sent(self):
            self.core_copy().wait_send()
            for k in range(1, CHIPS):
                self.part_copy(k).wait_send()
                self.back_copy(k).wait_send()
            self.pair_copy().wait_send()

    down_refs, up_refs, proj_refs = (plane[5 * i : 5 * i + 5] for i in range(3))
    direct_refs = [plane[15 + 4 * i : 19 + 4 * i] for i in range(heads + 1)]
    t_down, t_up, t_proj, t_qkv, t_small = plane[19 + 4 * heads :]
    down_sum = Plane(0, down_refs, t_down)
    up_sum = Plane(1, up_refs, t_up)
    proj_sum = Plane(2, proj_refs, t_proj)
    proj_all = Plane(3, None, pg.at[1:NT])
    small_sum = Direct(4, direct_refs[heads], t_small)
    qkv_sums = [Direct(5 + h, direct_refs[h], t_qkv.at[h : h + 1]) for h in range(heads)]
    g_down, g_up, g_proj, g_small = (refs[0] for refs in (down_refs, up_refs, proj_refs, direct_refs[heads]))

    gather_start(0, xg, x_hbm)
    proj_rows = span(quarter * (hw // 4), hw // 4)

    def proj_piece(k):
        return piece_copy(8, pg.at[0, proj_rows, my_lanes], pg.at[NT - k, proj_rows, my_lanes], k)

    loads[8].wait()
    for k in range(1, NT):
        proj_piece(k).start()
    for half in range(2):
        pl.when(end == 1)(half_copy(1, cg, t, half, order[1], 0, cot_hbm).start)
    high = grids[0, 0]
    wide = grids[0, 1]
    down = lax.broadcasted_iota(i32, (seq, 1), 0)
    across = lax.broadcasted_iota(i32, (1, seq), 1)
    token_q, pad_q = query_tokens(down, high, wide)
    token_q_across, _ = query_tokens(across, high, wide)
    token_k = key_tokens(down, high, wide)
    token_k_across = key_tokens(across, high, wide)
    mq[...] = one_hot(token_q, across)
    mqt[...] = one_hot(down, token_q_across)
    mk[...] = one_hot(token_k, across)
    mkt[...] = one_hot(down, token_k_across)
    gexp[...] = jnp.zeros_like(gexp)
    tab[...] = jnp.zeros_like(tab)
    loads[3].wait()
    tab[0:heads, 0 : ENTRIES + 3] = rel[...]
    for h in range(heads):
        table = tab[h : h + 1, :]
        lined = pltpu.roll(jnp.broadcast_to(table, (24, TABLE)), TABLE - (GRID - 1), 1)
        uexp[...] = pltpu.roll(lined, 0, 1, stride=1, stride_axis=0)
        for x in range(SPAN):
            gexp[:, x * GRID : (x + 1) * GRID] = uexp[:, x * SPAN : x * SPAN + GRID]
        hankel = gexp[...]
        for r in range(GRID):
            moved = hankel if r == 0 else pltpu.roll(hankel, WIDE - r * GRID, 1)
            bias[h, r * GRID : (r + 1) * GRID, :] = moved[0:GRID, 0:seq]
        bias[h, CELLS:seq, :] = jnp.zeros((seq - CELLS, seq), f32)
        origin = bias[h, GRID - 1 : GRID, :]
        from_class = table[:, ENTRIES : ENTRIES + 1]
        to_class = table[:, ENTRIES + 1 : ENTRIES + 2]
        class_pair = table[:, ENTRIES + 2 : ENTRIES + 3]

        def settle(i, carry):
            part = pl.ds(pl.multiple_of(i * 128, 128), 128)
            place = lax.broadcasted_iota(i32, (128, 1), 0) + i * 128
            _, padded = query_tokens(place, high, wide)
            values = jnp.where(padded, origin, bias[h, part, :])
            values = jnp.where(across == CELLS, to_class, values)
            values = jnp.where(
                place == CELLS, jnp.where(across == CELLS, class_pair, from_class), values
            )
            bias[h, part, :] = jnp.where(token_k_across >= 0, values, masked)
            return carry

        lax.fori_loop(0, seq // 128, settle, 0)

    for i in (0, 4, 5, 6, 7):
        loads[i].wait()
    gain_one, shift_one = gains[0:1, :], biases[0:1, :]

    def project(s):
        normed, _ = normalize(xg[s].astype(f32))
        sent = (normed * gain_one + shift_one).astype(bf16)
        part = block(s)
        n1g[part, :] = sent
        qt[part, :] = ((dot_nt(sent, wqkv[0:hw, :]) + qvb[0:1, :]) * 0.125).astype(bf16)
        kt[part, :] = dot_nt(sent, wqkv[hw : 2 * hw, :]).astype(bf16)
        vt[part, :] = (dot_nt(sent, wqkv[2 * hw : 3 * hw, :]) + qvb[1:2, :]).astype(bf16)

    project(t)
    gather_near(0, xg)
    for half in range(2):
        pl.when(end == 0)(half_copy(1, cg, t, half, order[2], 1, cot_hbm).start)
    gather_take(0, xg, 1)
    project(order[1])
    gather_take(0, xg, 2)
    project(order[2])
    for k in range(1, NT):
        piece_arrived(8, pg.at[k, proj_rows, my_lanes], k)
    proj_all.send(3)
    gather_take(0, xg, 3)
    for half in range(2):
        pl.when(end == 0)(half_copy(1, cg, t, half, order[1], 0, cot_hbm).start)
    forward_both(1, cg, 1)
    project(order[3])
    proj_all.spread_first()

    queries = dot(mq[...], qt[...]).astype(bf16)
    keys = dot(mk[...], kt[...]).astype(bf16)
    values = dot(mk[...], vt[...]).astype(bf16)
    for h in range(heads):
        lanes = slice(h * 64, (h + 1) * 64)
        qh[h] = queries[:, lanes]
        kh[h] = keys[:, lanes]
        vh[h] = values[:, lanes]
    forward_both(1, cg, 2)
    for h in range(heads):
        logits = dot_nt(qh[h], kh[h]) + bias[h]
        raised = jnp.exp(logits - jnp.max(logits, axis=-1, keepdims=True))
        weights = raised * (1.0 / jnp.sum(raised, axis=-1, keepdims=True))
        prob[h] = weights
        rounded = weights.astype(bf16)
        probb[h] = rounded
        op[:, h * 64 : (h + 1) * 64] = dot(rounded, vh[h]).astype(bf16)
    forward_both(1, cg, 3)
    ot[...] = dot(mqt[...], op[...]).astype(bf16)

    def mixed_piece(k):
        return piece_copy(2, ot.at[block((t + k) % NT), :], og.at[NT - k], k)

    for k in (2, 1, 3):
        mixed_piece(k).start()
    og[0] = ot[block(t), :]
    total = dot(og[0], pg[0])
    loads[2].wait()
    loads[12].wait()
    proj_all.spread_second()
    for k in range(1, NT):
        piece_arrived(2, og.at[k], k)
    proj_all.take(5)
    for k in range(1, NT):
        total = total + dot(og[k], pg[k])
    branch_one = total + obias[0:1, :]
    a1[...] = branch_one
    after_one = xg[t].astype(f32) + scales[0:1, :] * branch_one
    x1[...] = after_one
    normed, inverse = normalize(after_one)
    xhat2[...] = normed
    inv2[...] = jnp.broadcast_to(inverse, inv2.shape)
    n2g[t] = (normed * gains[1:2, :] + biases[1:2, :]).astype(bf16)
    gather_start(3, n2g)

    for i in (9, 10, 11):
        loads[i].wait()
    shift_up = jnp.reshape(b1[...].astype(f32), (1, b1.shape[0]))

    def feed(step):
        s = order[step]
        part = block(s)
        before = dot(n2g[s], w1[...]) + shift_up
        cumulative = 0.5 * (1.0 + lax.erf(before * 0.7071067811865476))
        slope = cumulative + before * (jnp.exp(-0.5 * before * before) * 0.3989422804014327)
        hid[part, :] = (before * cumulative).astype(bf16)
        grad_rows = (cg[s].astype(f32) * scales[1:2, :]).astype(bf16)
        dzg[s] = grad_rows
        grad_pre = (dot_nt(grad_rows, w2[...]) * slope).astype(bf16)
        du[part, :] = grad_pre
        back = dot_nt(grad_pre, w1[...])
        if step == 0:
            dn2own[...] = back
        else:
            stage_b[3 - step] = back.astype(bf16)
        return jnp.sum(grad_pre.astype(f32), axis=0, keepdims=True)

    loads[1].wait()
    bias_up = feed(0)
    gather_near(3, n2g)
    end_take(1, cg, 1)
    gather_take(3, n2g, 1)
    bias_up = bias_up + feed(1)
    scatter_copy(4, stage_b, dn2r, 2).start()
    end_take(1, cg, 2)
    end_take(1, cg, 3)
    gather_take(3, n2g, 2)
    bias_up = bias_up + feed(2)
    scatter_send(4, stage_b, dn2r, 1)
    gather_take(3, n2g, 3)
    bias_up = bias_up + feed(3)
    far_copy(4, stage_b, dn2r).start()
    sums[8:9, :] = bias_up
    scatter_merge(4, stage_b, dn2r, 1)
    down_rows = jnp.reshape(dzg[...], (seq, width))
    g_down[0] = dot_tn(hid[...], down_rows).astype(bf16)
    down_sum.send(0)
    up_rows = jnp.reshape(n2g[...], (seq, width))
    g_up[0] = dot_tn(up_rows, du[...]).astype(bf16)
    up_sum.send(0)
    shared = jnp.zeros((1, width), f32)
    for step, s in enumerate(order):
        piece = dot(hid[block(s), :], w2[...])
        shared = shared + jnp.sum(cg[s].astype(f32) * piece, axis=0, keepdims=True)
        if step == 0:
            own[...] = piece
        else:
            stage_c[3 - step] = piece.astype(bf16)
    scatter_send(5, stage_c, z2r, 1)
    scatter_send(5, stage_c, z2r, 2)
    cot = cg[t].astype(f32)
    cot_sum = jnp.sum(cot, axis=0, keepdims=True)
    sums[5:6, :] = shared + cot_sum * obias[1:2, :]
    sums[7:8, :] = cot_sum * scales[1:2, :]
    down_sum.add_core()
    up_sum.add_core()
    down_sum.add_first()

    @pl.when(end == 1)
    def _():
        slot_wait(4, dn2r, 0)
        dn2own[...] = dn2own[...] + dn2r[0].astype(f32)

    total = scatter_total(4, dn2r, dn2own[...])
    normed = xhat2[...]
    sums[3:4, :] = jnp.sum(total, axis=0, keepdims=True)
    sums[1:2, :] = jnp.sum(total * normed, axis=0, keepdims=True)
    after = cg[t].astype(f32) + norm_back(total * gains[1:2, :], normed, inv2[:, 0:1])
    dx1[...] = after
    branch = after * scales[0:1, :]
    grad_rows = branch.astype(bf16)

    def mixed_back(k):
        return piece_copy(6, doz.at[k], dot_t.at[block(t), :], k)

    for k in (2, 1, 3, 0):
        piece = dot_nt(grad_rows, pg[k]).astype(bf16)
        if k == 0:
            dot_t[block(t), :] = piece
        else:
            doz[k] = piece
            mixed_back(k).start()
    scatter_send(5, stage_c, z2r, 0)
    sums[4:5, :] = jnp.sum(after * a1[...], axis=0, keepdims=True)
    sums[6:7, :] = jnp.sum(branch, axis=0, keepdims=True)
    for k in range(NT):
        g_proj[k] = dot_tn(og[k], grad_rows).astype(bf16)
    proj_sum.send(0)
    up_sum.add_first()
    down_sum.add_second()
    scatter_merge(5, stage_c, z2r, 1)
    proj_sum.add_core()
    up_sum.add_second()
    down_sum.spread_first()

    for k in range(1, NT):
        piece_arrived(6, dot_t.at[block((t + k) % NT), :], k)
    grad_mixed = dot(mq[...], dot_t[...]).astype(bf16)
    for h in range(heads):
        doh[h] = grad_mixed[:, h * 64 : (h + 1) * 64]
    for h in range(heads):
        lanes = slice(h * 64, (h + 1) * 64)

        grad_prob = dot_nt(doh[h], vh[h])
        weights = prob[h]
        crossed = jnp.sum(weights * grad_prob, axis=-1, keepdims=True)
        rounded = (weights * (grad_prob - crossed)).astype(bf16)
        ds[h] = rounded
        dqp[:, lanes] = dot(rounded, kh[h]).astype(bf16) * 0.125
        dvp[:, lanes] = dot_tn(probb[h], doh[h]).astype(bf16)
        dkp[:, lanes] = dot_tn(rounded, qh[h]).astype(bf16)
        part_q = dot(mqt[...], dqp[:, lanes]).astype(bf16)
        part_k = dot(mkt[...], dkp[:, lanes]).astype(bf16)
        part_v = dot(mkt[...], dvp[:, lanes]).astype(bf16)
        dqt[:, lanes] = part_q
        dkt[:, lanes] = part_k
        dvt[:, lanes] = part_v
        for i, part in enumerate((part_q, part_k, part_v)):
            direct_refs[h][0][64 * i : 64 * (i + 1), :] = dot_tn(part, n1g[...]).astype(bf16)
        qkv_sums[h].send()
        if h == 0:
            proj_sum.add_first()
            scatter_merge(5, stage_c, z2r, 0)
        elif h == 1:
            up_sum.spread_first()
            qkv_sums[0].add_core()
    down_sum.spread_second()
    qkv_sums[1].add_core()

    shift_total = jnp.zeros((1, width), f32)
    gain_total = jnp.zeros((1, width), f32)
    for step in (3, 2, 1, 0):
        s = order[step]
        part = block(s)
        piece = dot(dqt[part, :], wqkv[0:hw, :]) + dot(dkt[part, :], wqkv[hw : 2 * hw, :])
        piece = piece + dot(dvt[part, :], wqkv[2 * hw : 3 * hw, :])
        if step == 0:
            dn2own[...] = piece
        else:
            stage_d[3 - step] = piece.astype(bf16)
        normed, _ = normalize(xg[s].astype(f32))
        shift_total = shift_total + jnp.sum(piece, axis=0, keepdims=True)
        gain_total = gain_total + jnp.sum(piece * normed, axis=0, keepdims=True)
    proj_sum.add_second(gpz)

    def proj_exchange(k):
        return piece_copy(9, gpz.at[k], gpz.at[2 * NT - k], k)

    for k in range(1, NT):
        proj_exchange(k).start()
    sums[2:3, :] = shift_total
    sums[0:1, :] = gain_total
    zmr[t] = sums[0:REP, :]

    def small_tensor(k):
        return remote(
            zmr.at[t], zmr.at[t], z_send.at[10, k], z_recv.at[10, NT - k], (dp, (t + k) % NT)
        )

    for k in range(1, NT):
        small_tensor(k).start()
    for i in range(NT - 1):
        scatter_send(7, stage_d, dn1r, i)
    qkv_sums[2].add_core()

    branch_two = scatter_total(5, z2r, own[...]) + obias[1:2, :]
    outv[...] = (x1[...] + scales[1:2, :] * branch_two).astype(bf16)
    stores = [pltpu.make_async_copy(outv, out, store_sem.at[0])]
    stores[0].start()
    qkv_sums[0].add_parts()
    up_sum.spread_second()

    row24 = lax.broadcasted_iota(i32, (24, 1), 0)
    lane_t = lax.broadcasted_iota(i32, (1, TABLE), 1)
    uexp[...] = jnp.zeros_like(uexp)
    gexp[...] = jnp.zeros_like(gexp)
    for h in range(heads):
        grads = ds[h].astype(f32)
        class_row = grads[CELLS : CELLS + 1, :]
        class_column = jnp.sum(
            jnp.where((down != CELLS) & (across == CELLS), grads, 0.0), axis=0, keepdims=True
        )
        cells = jnp.where(across < CELLS, grads, 0.0)
        pad_row = jnp.sum(jnp.where(pad_q, cells, 0.0), axis=0, keepdims=True)
        dsf[...] = jnp.where(pad_q, 0.0, cells)
        blank = jnp.zeros((24, WIDE - seq), f32)
        folded = jnp.zeros((24, WIDE), f32)
        for r in range(GRID):
            cells = jnp.concatenate([dsf[r * GRID : r * GRID + 24, :], blank], axis=1)
            folded = folded + (cells if r == 0 else pltpu.roll(cells, r * GRID, 1))
        padded_row = jnp.concatenate([pad_row, jnp.zeros((1, WIDE - seq), f32)], axis=1)
        folded = jnp.where(row24 < GRID, folded, 0.0) + jnp.where(row24 == GRID - 1, padded_row, 0.0)
        for i in range(GRID):
            gexp[GRID - 1 - i : GRID - i, :] = folded[i : i + 1, :]
        for x in range(SPAN):
            uexp[:, x * SPAN : x * SPAN + GRID] = gexp[:, x * GRID : (x + 1) * GRID]
        lined = pltpu.roll(uexp[...], 0, 1, stride=1, stride_axis=0)
        table = jnp.sum(lined, axis=0, keepdims=True)
        from_class = jnp.sum(jnp.where(across != CELLS, class_row, 0.0), axis=1, keepdims=True)
        class_pair = jnp.sum(jnp.where(across == CELLS, class_row, 0.0), axis=1, keepdims=True)
        to_class = jnp.sum(class_column, axis=1, keepdims=True)
        table = jnp.where(lane_t == ENTRIES, from_class, table)
        table = jnp.where(lane_t == ENTRIES + 1, to_class, table)
        tab[h : h + 1, :] = jnp.where(lane_t == ENTRIES + 2, class_pair, table)
        if h == 0:
            qkv_sums[1].add_parts()
        elif h == 1:
            scatter_merge(7, stage_d, dn1r, 0)
    sums[9:10, 0:hw] = jnp.sum(dqt[...].astype(f32), axis=0, keepdims=True)
    sums[10:11, 0:hw] = jnp.sum(dvt[...].astype(f32), axis=0, keepdims=True)
    sums[9:11, hw:width] = jnp.zeros((2, width - hw), f32)
    for h in range(heads):
        at = 11 + 3 * h
        sums[at : at + 1, :] = tab[h : h + 1, 0:width]
        sums[at + 1 : at + 2, :] = tab[h : h + 1, width : 2 * width]
        sums[at + 2 : at + 3, 0 : TABLE - 2 * width] = tab[h : h + 1, 2 * width : TABLE]
        sums[at + 2 : at + 3, TABLE - 2 * width : width] = jnp.zeros((1, 3 * width - TABLE), f32)
    sums[11 + 3 * heads : SMALL, :] = jnp.zeros((SMALL - 11 - 3 * heads, width), f32)

    for k in range(1, NT):
        piece_arrived(10, zmr.at[(t + k) % NT], k)
    sums[0:REP, :] = zmr[0] + zmr[1] + zmr[2] + zmr[3]
    g_small[...] = sums[...].astype(bf16)
    small_sum.send()
    value = gpz[0].astype(f32)
    for k in range(1, NT):
        piece_arrived(9, gpz.at[NT + k], k)
        value = value + gpz[NT + k].astype(f32)
    t_proj[0, proj_rows, my_lanes] = value.astype(bf16)
    proj_sum.send(3)
    small_sum.add_core()
    qkv_sums[2].add_parts()
    qkv_sums[0].spread()
    scatter_merge(7, stage_d, dn1r, 1)
    proj_sum.spread_first()
    qkv_sums[1].spread()
    small_sum.add_parts()
    sources = [(t_down.at[0], t_down_hbm), (t_up.at[0], t_up_hbm), (t_proj.at[0], t_proj_hbm), (t_small.at[0], t_small_hbm)]
    sources += [(t_qkv.at[h], t_qkv_hbm.at[192 * h : 192 * (h + 1), :]) for h in range(heads)]
    sources += [(ingradv, ingrad)]
    stores += [pltpu.make_async_copy(src, dst, store_sem.at[i + 1]) for i, (src, dst) in enumerate(sources)]
    down_sum.take(5)
    stores[1].start()
    up_sum.take(5)
    stores[2].start()
    proj_sum.spread_second()
    qkv_sums[2].spread()
    total = scatter_total(7, dn1r, dn2own[...])
    normed, inverse = normalize(xg[t].astype(f32))
    ingradv[...] = dx1[...] + norm_back(total * gain_one, normed, inverse)
    stores[8].start()
    small_sum.spread()
    for h in range(heads):
        qkv_sums[h].take()
        stores[5 + h].start()
    proj_sum.take(5)
    stores[3].start()
    small_sum.take()
    stores[4].start()

    gather_sent(0, xg, x_hbm)
    gather_sent(1, cg, cot_hbm)
    gather_sent(3, n2g)
    for phase, stage, buf in ((4, stage_b, dn2r), (5, stage_c, z2r), (7, stage_d, dn1r)):
        for i in range(NT - 1):
            if phase == 4 and i == 0:
                far_copy(phase, stage, buf).wait_send()
            else:
                scatter_copy(phase, stage, buf, i).wait_send()
    for k in range(1, NT):
        proj_piece(k).wait_send()
        mixed_piece(k).wait_send()
        mixed_back(k).wait_send()
        proj_exchange(k).wait_send()
        small_tensor(k).wait_send()
    for part_sum in (down_sum, up_sum, proj_sum, small_sum, *qkv_sums):
        part_sum.sent()
    proj_all.sent(3)
    for store in stores:
        store.wait()


def finish_kernel(
    down_in, up_in, proj_in, qkv_in, small_in, out_in, ingrad_in,
    out, ingrad, g_qkv, g_qv, g_table, g_proj, g_up, g_up_bias, g_down, g_gains, g_shifts, g_scales, g_biases,
    down_v, up_v, proj_v, qkv_v, down_f, up_f, proj_f, qkv_f, small_v, out_v, ingrad_v, load_sem, store_sem,
):
    width = g_down.shape[1]
    hw = g_proj.shape[0]
    heads, entries = g_table.shape
    parts = []
    for given, rounded, widened, result in (
        (down_in, down_v, down_f, g_down), (up_in, up_v, up_f, g_up),
        (qkv_in, qkv_v, qkv_f, g_qkv), (proj_in, proj_v, proj_f, g_proj),
    ):
        for start in range(0, given.shape[0], PIECE):
            piece = [ref.at[start : start + PIECE, :] for ref in (given, rounded, widened, result)]
            parts.append(piece + [given is qkv_in])
    moved = [(small_in, small_v, None), (out_in, out_v, out), (ingrad_in, ingrad_v, ingrad)]
    count = len(parts)
    loads = [pltpu.make_async_copy(part[0], part[1], load_sem.at[i]) for i, part in enumerate(parts)]
    loads += [pltpu.make_async_copy(src, via, load_sem.at[count + i]) for i, (src, via, _) in enumerate(moved)]
    for copy in loads:
        copy.start()
    stores = []
    by_head = [i for i, part in enumerate(parts) if part[4]]
    for i, (_, rounded, widened, result, mixed) in enumerate(parts):
        if mixed:
            which = i - by_head[0]
            for h, j in enumerate(by_head):
                if which == 0:
                    loads[j].wait()
                widened[64 * h : 64 * (h + 1), :] = parts[j][1][64 * which : 64 * (which + 1), :].astype(f32)
        else:
            loads[i].wait()
            widened[...] = rounded[...].astype(f32)
        stores.append(pltpu.make_async_copy(widened, result, store_sem.at[i]))
        stores[-1].start()
    for i, (_, via, dst) in enumerate(moved):
        loads[count + i].wait()
        if dst is not None:
            stores.append(pltpu.make_async_copy(via, dst, store_sem.at[count + i]))
            stores[-1].start()
    small = small_v[...].astype(f32)
    g_gains[...] = small[0:2, :]
    g_shifts[...] = small[2:4, :]
    g_scales[...] = small[4:6, :]
    g_biases[...] = small[6:8, :]
    g_up_bias[...] = jnp.reshape(small[8:9, :], (width,))
    g_qv[...] = small[9:11, 0:hw]
    for h in range(heads):
        for j in range(3):
            lanes = min(width, entries - j * width)
            g_table[h : h + 1, j * width : j * width + lanes] = small[
                11 + 3 * h + j : 12 + 3 * h + j, 0:lanes
            ]
    for copy in stores:
        copy.wait()


def per_device(
    n_dp, tokens, grids, qkv_weight, qv_bias, rel_table, proj_weight, fc1_weight, fc1_bias, fc2_weight,
    norm_gains, norm_biases, layer_scales, out_biases, cotangent,
):
    rows, width = tokens.shape
    seq = rows * NT
    heads, entries = rel_table.shape
    hw = heads * 64
    ff = fc1_weight.shape[1]
    qkv_rows = jnp.transpose(qkv_weight, (1, 2, 0)).reshape(3 * hw, width)
    vm = pl.BlockSpec(memory_space=pltpu.VMEM)
    anywhere = pl.BlockSpec(memory_space=pl.ANY)

    def many(count, shape, dtype):
        return [pltpu.VMEM(shape, dtype)] * count

    def sems(*shape):
        return [pltpu.SemaphoreType.DMA(shape)]

    half = width // 2
    scratch = [
        pltpu.VMEM((rows, width), bf16), pltpu.VMEM((rows, width), f32), pltpu.VMEM((3 * hw, width), bf16),
        pltpu.VMEM((width, ff), bf16), pltpu.VMEM((ff, width), bf16),
        pltpu.VMEM((2, hw), f32), pltpu.VMEM((heads, entries), f32), pltpu.VMEM((ff,), bf16),
    ]
    scratch += many(4, (2, width), f32) + sems(13) + sems(9)
    scratch += many(4, (NT, rows, width), bf16)
    scratch += many(1, (NT, rows, hw), bf16) + many(1, (NT, hw, width), bf16)
    scratch += many(3, (NT, rows, width), bf16) + many(3, (NT - 1, rows, width), bf16)
    scratch += many(1, (NT, rows, hw), bf16) + sems(11, NT) + sems(11, 2 * NT) + sems(4, 5, 2)
    scratch += many(4, (seq, seq), bf16)
    scratch += many(1, (heads, seq, seq), f32) + many(1, (24, WIDE), f32) + many(1, (24, TABLE), f32)
    scratch += many(1, (seq, width), bf16) + many(3, (seq, hw), bf16)
    scratch += many(3, (heads, seq, 64), bf16)
    scratch += many(1, (heads, seq, seq), f32) + many(1, (heads, seq, seq), bf16)
    scratch += many(2, (seq, hw), bf16)
    scratch += many(2, (rows, width), f32) + many(1, (rows, 128), f32) + many(4, (rows, width), f32)
    scratch += many(2, (seq, ff), bf16) + many(1, (seq, hw), bf16) + many(1, (heads, seq, 64), bf16)
    scratch += many(1, (heads, seq, seq), bf16) + many(1, (seq, seq), f32) + many(6, (seq, hw), bf16)
    scratch += many(1, (8, TABLE), f32) + many(1, (SMALL, width), f32) + many(1, (NT, REP, width), f32)
    scratch += many(1, (2 * NT, hw // 4, half), bf16) + sems(5 + heads, 8) + sems(5 + heads, 8)
    for lead, count in ((1, ff), (1, width), (NT, hw)):
        scratch += [
            pltpu.VMEM((lead, count, width), bf16), pltpu.VMEM((lead, count, half), bf16),
            pltpu.VMEM((lead, count, half), bf16), pltpu.VMEM((lead, count // 2, half), bf16),
            pltpu.VMEM((lead, count // 4, half), bf16),
        ]
    for count in (192,) * heads + (SMALL,):
        scratch += [
            pltpu.VMEM((count, width), bf16), pltpu.VMEM((count, half), bf16), pltpu.VMEM((count, half), bf16),
            pltpu.VMEM((CHIPS - 1, count // CHIPS, half), bf16),
        ]
    for lead, count in ((1, ff), (1, width), (1, hw), (heads, 192), (1, SMALL)):
        scratch += many(1, (lead, count, width), bf16)
    flat = [jax.ShapeDtypeStruct((count, width), bf16) for count in (ff, width, hw, 3 * hw, SMALL)]
    output, input_grad, *totals = pl.pallas_call(
        main_kernel,
        out_shape=[
            jax.ShapeDtypeStruct((rows, width), bf16),
            jax.ShapeDtypeStruct((rows, width), f32),
        ]
        + flat,
        in_specs=[pl.BlockSpec(memory_space=pltpu.SMEM)] + [anywhere] * 13,
        out_specs=[anywhere] * 7,
        scratch_shapes=scratch,
        compiler_params=pltpu.CompilerParams(
            collective_id=0, has_side_effects=True, vmem_limit_bytes=60 << 20
        ),
        name="layer",
    )(
        grids, tokens, cotangent, qkv_rows, proj_weight, fc1_weight, fc2_weight,
        qv_bias, rel_table, fc1_bias, norm_gains, norm_biases, layer_scales, out_biases,
    )
    pair = jax.ShapeDtypeStruct((2, width), f32)
    pieces = sum(-(-count // PIECE) for count in (ff, width, hw, 3 * hw))
    results = pl.pallas_call(
        finish_kernel,
        out_shape=(
            jax.ShapeDtypeStruct((rows, width), bf16),
            jax.ShapeDtypeStruct((rows, width), f32),
            jax.ShapeDtypeStruct((3 * hw, width), f32),
            jax.ShapeDtypeStruct((2, hw), f32),
            jax.ShapeDtypeStruct((heads, entries), f32),
            jax.ShapeDtypeStruct((hw, width), f32),
            jax.ShapeDtypeStruct((width, ff), f32),
            jax.ShapeDtypeStruct((ff,), f32),
            jax.ShapeDtypeStruct((ff, width), f32),
            pair, pair, pair, pair,
        ),
        in_specs=[anywhere] * 7,
        out_specs=(
            anywhere, anywhere, anywhere, vm, vm, anywhere, anywhere, vm, anywhere, vm, vm, vm, vm,
        ),
        scratch_shapes=[
            pltpu.VMEM((ff, width), bf16), pltpu.VMEM((width, ff), bf16), pltpu.VMEM((hw, width), bf16),
            pltpu.VMEM((3 * hw, width), bf16),
            pltpu.VMEM((ff, width), f32), pltpu.VMEM((width, ff), f32), pltpu.VMEM((hw, width), f32),
            pltpu.VMEM((3 * hw, width), f32), pltpu.VMEM((SMALL, width), bf16),
            pltpu.VMEM((rows, width), bf16), pltpu.VMEM((rows, width), f32),
            *sems(pieces + 3), *sems(pieces + 3),
        ],
        compiler_params=pltpu.CompilerParams(vmem_limit_bytes=60 << 20),
        name="finish",
    )(*totals, output, input_grad)
    results = list(results)
    stride = GROUP
    while stride < n_dp:
        hops = [(i, i ^ stride) for i in range(n_dp)]
        results[2:] = [value + lax.ppermute(value, "dp", hops) for value in results[2:]]
        stride *= 2
    results[2] = jnp.transpose(results[2].reshape(3, hw, width), (2, 0, 1))
    return tuple(results)


def solution(mesh):
    n_dp = mesh.shape["dp"]
    blocks = P(("dp", "tensor"), None)
    placed = (
        blocks, P("dp", None), P(None, None, "tensor"), P(None, "tensor"), P("tensor", None), P("tensor", None),
        P(None, "tensor"), P("tensor"), P("tensor", None), P(), P(), P(), P(), blocks,
    )
    given = (
        blocks, blocks, P(None, None, "tensor"), P(None, "tensor"), P("tensor", None), P("tensor", None),
        P(None, "tensor"), P("tensor"), P("tensor", None), P(), P(), P(), P(),
    )

    def layer(*arrays):
        return per_device(n_dp, *arrays)

    return jax.shard_map(layer, mesh=mesh, in_specs=placed, out_specs=given, check_vma=False)
```

```python
import jax
import jax.numpy as jnp
from jax import lax
from jax.experimental import pallas as pl
from jax.experimental.pallas import tpu as pltpu
from jax.sharding import PartitionSpec as P

GRID = 22
SPAN = 2 * GRID - 1
CELLS = GRID * GRID
ENTRIES = SPAN * SPAN
MESH = pl.DeviceIdType.MESH
f32 = jnp.float32
bf16 = jnp.bfloat16
i32 = jnp.int32

eps_norm = 1e-06
masked = -1e30
NT = 4
CHIPS = 4
CORES = 2
GROUP = CHIPS * CORES
TABLE = 1920
WIDE = 1024
SMALL = 64
REP = 8
PIECE = 192


def dot(left, right):
    return lax.dot_general(left, right, (((1,), (0,)), ((), ())), preferred_element_type=f32)


def dot_nt(left, right):
    return lax.dot_general(left, right, (((1,), (1,)), ((), ())), preferred_element_type=f32)


def dot_tn(left, right):
    return lax.dot_general(left, right, (((0,), (0,)), ((), ())), preferred_element_type=f32)


def normalize(values):
    center = values - jnp.mean(values, axis=-1, keepdims=True)
    inverse = lax.rsqrt(jnp.mean(center * center, axis=-1, keepdims=True) + eps_norm)
    return center * inverse, inverse


def norm_back(grad_normed, normed, inverse):
    average = jnp.mean(grad_normed, axis=-1, keepdims=True)
    crossed = jnp.mean(grad_normed * normed, axis=-1, keepdims=True)
    return inverse * (grad_normed - average - normed * crossed)


def split_cell(place):
    row = (place * 2979) >> 16
    return row, place - row * GRID


def query_tokens(place, high, wide):
    row, back = split_cell(place)
    inside = (place < CELLS) & (row < high) & (GRID - 1 - back < wide)
    before = jnp.minimum(row, high) * wide + jnp.where(
        row < high, jnp.maximum(back - (GRID - wide), 0), 0
    )
    token = jnp.where(inside, 1 + row * wide + (GRID - 1 - back), high * wide + 1 + place - before)
    token = jnp.where(place == CELLS, 0, jnp.where(place > CELLS, place, token))
    padding = jnp.logical_not(inside) & (place != CELLS)
    return token, padding


def key_tokens(place, high, wide):
    row, back = split_cell(place)
    row = GRID - 1 - row
    column = GRID - 1 - back
    inside = (place < CELLS) & (row < high) & (column < wide)
    token = jnp.where(inside, 1 + row * wide + column, -1)
    return jnp.where(place == CELLS, 0, token)


def one_hot(left, right):
    return jnp.where(left == right, 1.0, 0.0).astype(bf16)


def main_kernel(
    grids, x_hbm, cot_hbm, wqkv_hbm, wproj_hbm, w1_hbm, w2_hbm, qvb_hbm, rel_hbm, b1_hbm,
    gains_hbm, biases_hbm, scales_hbm, obias_hbm,
    out, ingrad, t_down_hbm, t_up_hbm, t_proj_hbm, t_qkv_hbm, t_small_hbm,
    outv, ingradv, wqkv, w1, w2, qvb, rel, b1, gains, biases, scales, obias, load_sem, store_sem,
    xg, cg, dzg, n2g, og, pg, dn2r, z2r, dn1r, stage_b, stage_c, stage_d, doz, z_send, z_recv, z_half,
    mq, mqt, mk, mkt, bias, gexp, uexp,
    n1g, qt, kt, vt, qh, kh, vh, prob, probb, op, ot,
    x1, xhat2, inv2, a1, dx1, own, dn2own,
    hid, du, dot_t, doh, ds, dsf, dqp, dkp, dvp, dqt, dkt, dvt,
    tab, sums, zmr, gpz, p_send, p_recv,
    *plane,
):
    dp = lax.axis_index("dp")
    t = lax.axis_index("tensor")
    rows, width = x_hbm.shape
    seq = rows * NT
    heads = rel.shape[0]
    hw = heads * 64
    base = (dp // GROUP) * GROUP
    mine = dp % GROUP
    core = mine % CORES
    chip_x = (mine // 2) % 2
    chip_y = mine // 4
    to_x = 2 - 4 * chip_x
    to_y = 4 - 8 * chip_y
    sibling = base + mine + 1 - 2 * core
    first_peer = base + mine + (1 - core) * to_x + core * to_y
    second_peer = base + mine + core * to_x + (1 - core) * to_y
    bit_one = (1 - core) * chip_x + core * chip_y
    bit_two = core * chip_x + (1 - core) * chip_y
    quarter = bit_one * 2 + bit_two
    end = ((t - 1) * (t - 2)) // 2
    order = [t, t + 1 - 2 * (t % 2), 2 - t // 2, 3 - 3 * (t // 2)]

    pairs = [
        (x_hbm, xg.at[t]), (cot_hbm, cg.at[t]), (scales_hbm, scales), (rel_hbm, rel), (wqkv_hbm, wqkv),
        (gains_hbm, gains), (biases_hbm, biases), (qvb_hbm, qvb), (wproj_hbm, pg.at[0]), (w1_hbm, w1),
        (w2_hbm, w2), (b1_hbm, b1), (obias_hbm, obias),
    ]
    loads = [pltpu.make_async_copy(src, dst, load_sem.at[i]) for i, (src, dst) in enumerate(pairs)]
    for load in loads:
        load.start()
    barrier = pltpu.get_barrier_semaphore()
    for k in range(1, NT):
        pl.semaphore_signal(barrier, inc=1, device_id=(dp, (t + k) % NT), device_id_type=MESH)
    chip = mine // CORES
    others = [base + ((chip + k) % CHIPS) * CORES + core for k in range(CHIPS)]
    for peer in (sibling, *others[1:]):
        pl.semaphore_signal(barrier, inc=1, device_id=(peer, t), device_id_type=MESH)
    pl.semaphore_wait(barrier, NT - 1 + CHIPS)

    def block(s):
        return pl.ds(pl.multiple_of(s * rows, rows), rows)

    def remote(src, dst, send, recv, device):
        return pltpu.make_async_remote_copy(
            src_ref=src, dst_ref=dst, send_sem=send, recv_sem=recv, device_id=device, device_id_type=MESH
        )

    half_rows = rows // 2

    def half_copy(phase, buf, src, half, dst, way, given=None):
        spot = buf.at[src, half * half_rows : (half + 1) * half_rows, :]
        if given is not None:
            given = given.at[half * half_rows : (half + 1) * half_rows, :]
        return remote(
            spot if given is None else given, spot,
            z_half.at[phase, way, half], z_recv.at[phase, src * 2 + half], (dp, dst),
        )

    def gather_start(phase, buf, given=None):
        for half in range(2):
            half_copy(phase, buf, t, half, order[1], 0, given).start()
            pl.when(end == 0)(half_copy(phase, buf, t, half, order[2], 1, given).start)

    def half_arrived(phase, buf, step, half):
        half_copy(phase, buf, order[step], half, order[1], 0).wait_recv()

    def half_forward(phase, buf, step, half):
        to = order[2] if step == 1 else order[1]
        half_copy(phase, buf, order[step], half, to, 1 + step).start()

    def gather_near(phase, buf):
        @pl.when(end == 0)
        def _():
            for half in range(2):
                for step in (1, 2):
                    half_arrived(phase, buf, step, half)
                    half_forward(phase, buf, step, half)

    def forward_both(phase, buf, step):
        @pl.when(end == 0)
        def _():
            for half in range(2):
                half_arrived(phase, buf, step, half)
                half_forward(phase, buf, step, half)

    def end_take(phase, buf, step):
        for half in range(2):
            pl.when(end == 1)(lambda: half_arrived(phase, buf, step, half))

    def gather_take(phase, buf, step):
        for half in range(2):
            if step < 3:
                pl.when(end == 1)(lambda: half_arrived(phase, buf, step, half))
            else:
                half_arrived(phase, buf, step, half)
                pl.when(end == 0)(lambda: half_forward(phase, buf, step, half))

    def gather_sent(phase, buf, given=None):
        for half in range(2):
            half_copy(phase, buf, t, half, order[1], 0, given).wait_send()

            @pl.when(end == 0)
            def _():
                half_copy(phase, buf, t, half, order[2], 1, given).wait_send()
                for step in (1, 2, 3):
                    half_copy(phase, buf, order[step], half, order[1], 1 + step).wait_send()

    def scatter_part(phase, stage, buf, i, dst, slot, half):
        if half is None:
            return remote(
                stage.at[i], buf.at[slot], z_send.at[phase, i], z_recv.at[phase, slot], (dp, dst)
            )
        part = slice(half * half_rows, (half + 1) * half_rows)
        return remote(
            stage.at[i, part, :], buf.at[slot, part, :],
            z_send.at[phase, i + NT * half], z_recv.at[phase, slot + NT * half], (dp, dst),
        )

    def scatter_copy(phase, stage, buf, i, half=None):
        if i == 2:
            dst, slot = order[1], 2
        else:
            dst = end * order[1] + (1 - end) * order[3 - i]
            slot = end * i + (1 - end) * 3
        return scatter_part(phase, stage, buf, i, dst, slot, half)

    def far_copy(phase, stage, buf, half):
        return scatter_part(phase, stage, buf, 0, order[3], (1 - end) * 3, half)

    def slot_wait(phase, buf, slot, half=None):
        scatter_part(phase, buf, buf, slot, order[1], slot, half).wait_recv()

    def scatter_send(phase, stage, buf, i, half=None):
        if i == 2:
            scatter_copy(phase, stage, buf, i, half).start()
        else:
            pl.when(end == 1)(scatter_copy(phase, stage, buf, i, half).start)

    def scatter_merge(phase, stage, buf, i, half=None):
        part = slice(None) if half is None else slice(half * half_rows, (half + 1) * half_rows)

        @pl.when(end == 0)
        def _():
            slot_wait(phase, buf, i, half)
            stage[i, part, :] = (stage[i, part, :].astype(f32) + buf[i, part, :].astype(f32)).astype(bf16)
            scatter_copy(phase, stage, buf, i, half).start()

    def scatter_total(phase, buf, total, halves=()):
        for slot in (2, 3):
            if slot in halves:
                slot_wait(phase, buf, slot, 0)
                slot_wait(phase, buf, slot, 1)
            else:
                slot_wait(phase, buf, slot)
            total = total + buf[slot].astype(f32)
        return total

    def piece_copy(phase, src, dst, k):
        return remote(
            src, dst, z_send.at[phase, k], z_recv.at[phase, NT - k], (dp, (t + k) % NT)
        )

    def piece_arrived(phase, dst, k):
        remote(dst, dst, z_send.at[phase, k], z_recv.at[phase, k], (dp, (t + k) % NT)).wait_recv()

    half_width = width // 2
    my_lanes = pl.ds(pl.multiple_of(core * half_width, half_width), half_width)
    your_lanes = pl.ds(pl.multiple_of((1 - core) * half_width, half_width), half_width)

    def span(start, count):
        return pl.ds(pl.multiple_of(start, 16), count)

    class Plane:
        def __init__(self, index, refs, target):
            self.index, self.target = index, target
            self.count = target.shape[1]
            self.fours = self.count // 4
            if refs is not None:
                self.given, self.near, self.held, self.one, self.two = refs
                self.lead = self.given.shape[0]

        def copy(self, step, src, dst, peer):
            return remote(
                src, dst, p_send.at[self.index, step], p_recv.at[self.index, step], (peer, t)
            )

        def outgoing(self, step):
            c, f = self.count, self.fours
            if step == 0:
                return self.copy(0, self.given.at[:, :, your_lanes], self.near, sibling)
            if step == 1:
                src = self.held.at[:, span((1 - bit_one) * 2 * f, 2 * f), :]
                return self.copy(1, src, self.one, first_peer)
            if step == 2:
                src = self.held.at[:, span((bit_one * 2 + 1 - bit_two) * f, f), :]
                return self.copy(2, src, self.two, second_peer)
            if step == 3:
                spot, peer = self.target.at[:, span(quarter * f, f), my_lanes], second_peer
            elif step == 4:
                spot, peer = self.target.at[:, span(bit_one * 2 * f, 2 * f), my_lanes], first_peer
            else:
                spot, peer = self.target.at[:, :, my_lanes], sibling
            return self.copy(step, spot, spot, peer)

        def incoming(self, step):
            f = self.fours
            if step < 3:
                return self.outgoing(step)
            if step == 3:
                spot = self.target.at[:, span((bit_one * 2 + 1 - bit_two) * f, f), my_lanes]
            elif step == 4:
                spot = self.target.at[:, span((1 - bit_one) * 2 * f, 2 * f), my_lanes]
            else:
                spot = self.target.at[:, :, your_lanes]
            return self.copy(step, spot, spot, sibling)

        def send(self, step):
            self.outgoing(step).start()

        def take(self, step):
            self.incoming(step).wait_recv()

        def add_core(self):
            self.take(0)
            for q in range(self.lead):
                value = self.given[q, :, my_lanes].astype(f32) + self.near[q].astype(f32)
                self.held[q] = value.astype(bf16)
            self.send(1)

        def add_first(self):
            self.take(1)
            part = span(bit_one * 2 * self.fours, 2 * self.fours)
            for q in range(self.lead):
                value = self.held[q, part, :].astype(f32) + self.one[q].astype(f32)
                self.held[q, part, :] = value.astype(bf16)
            self.send(2)

        def add_second(self, store=None):
            self.take(2)
            part = span(quarter * self.fours, self.fours)
            for q in range(self.lead):
                value = (self.held[q, part, :].astype(f32) + self.two[q].astype(f32)).astype(bf16)
                if store is None:
                    self.target[q, part, my_lanes] = value
                else:
                    store[q] = value
            if store is None:
                self.send(3)

        def spread_first(self):
            self.take(3)
            self.send(4)

        def spread_second(self):
            self.take(4)
            self.send(5)

        def sent(self, first=0):
            for step in range(first, 6):
                self.outgoing(step).wait_send()

    class Direct:
        def __init__(self, index, refs, target):
            self.index, self.target = index, target
            self.fours = target.shape[1] // CHIPS
            self.given, self.near, self.held, self.parts = refs

        def copy(self, step, src, dst, peer):
            return remote(
                src, dst, p_send.at[self.index, step], p_recv.at[self.index, step], (peer, t)
            )

        def rows_of(self, k):
            return span(((chip + k) % CHIPS) * self.fours, self.fours)

        def core_copy(self):
            return self.copy(0, self.given.at[:, your_lanes], self.near, sibling)

        def part_copy(self, k):
            return self.copy(k, self.held.at[self.rows_of(k), :], self.parts.at[k - 1], others[k])

        def back_copy(self, k):
            spot = self.target.at[0, self.rows_of(0), my_lanes]
            return self.copy(3 + k, spot, spot, others[k])

        def pair_copy(self):
            spot = self.target.at[0, :, my_lanes]
            return self.copy(7, spot, spot, sibling)

        def send(self):
            self.core_copy().start()

        def add_core(self):
            self.core_copy().wait_recv()
            value = self.given[:, my_lanes].astype(f32) + self.near[...].astype(f32)
            self.held[...] = value.astype(bf16)
            for k in (2, 1, 3):
                self.part_copy(k).start()

        def add_parts(self):
            value = self.held[self.rows_of(0), :].astype(f32)
            for k in range(1, CHIPS):
                self.part_copy(k).wait_recv()
                value = value + self.parts[k - 1].astype(f32)
            self.target[0, self.rows_of(0), my_lanes] = value.astype(bf16)
            for k in (2, 1, 3):
                self.back_copy(k).start()

        def spread(self):
            for k in range(1, CHIPS):
                spot = self.target.at[0, self.rows_of(CHIPS - k), my_lanes]
                self.copy(3 + k, spot, spot, others[k]).wait_recv()
            self.pair_copy().start()

        def take(self):
            spot = self.target.at[0, :, your_lanes]
            self.copy(7, spot, spot, sibling).wait_recv()

        def sent(self):
            self.core_copy().wait_send()
            for k in range(1, CHIPS):
                self.part_copy(k).wait_send()
                self.back_copy(k).wait_send()
            self.pair_copy().wait_send()

    down_refs, up_refs, proj_refs = (plane[5 * i : 5 * i + 5] for i in range(3))
    direct_refs = [plane[15 + 4 * i : 19 + 4 * i] for i in range(heads + 1)]
    t_down, t_up, t_proj, t_qkv, t_small = plane[19 + 4 * heads :]
    down_sum = Plane(0, down_refs, t_down)
    up_sum = Plane(1, up_refs, t_up)
    proj_sum = Plane(2, proj_refs, t_proj)
    proj_all = Plane(3, None, pg.at[1:NT])
    small_sum = Direct(4, direct_refs[heads], t_small)
    qkv_sums = [Direct(5 + h, direct_refs[h], t_qkv.at[h : h + 1]) for h in range(heads)]
    g_down, g_up, g_proj, g_small = (refs[0] for refs in (down_refs, up_refs, proj_refs, direct_refs[heads]))

    gather_start(0, xg, x_hbm)
    proj_rows = span(quarter * (hw // 4), hw // 4)

    def proj_piece(k):
        return piece_copy(8, pg.at[0, proj_rows, my_lanes], pg.at[NT - k, proj_rows, my_lanes], k)

    loads[8].wait()
    for k in range(1, NT):
        proj_piece(k).start()
    for half in range(2):
        pl.when(end == 1)(half_copy(1, cg, t, half, order[1], 0, cot_hbm).start)
    high = grids[0, 0]
    wide = grids[0, 1]
    down = lax.broadcasted_iota(i32, (seq, 1), 0)
    across = lax.broadcasted_iota(i32, (1, seq), 1)
    token_q, pad_q = query_tokens(down, high, wide)
    token_q_across, _ = query_tokens(across, high, wide)
    token_k = key_tokens(down, high, wide)
    token_k_across = key_tokens(across, high, wide)
    mq[...] = one_hot(token_q, across)
    mqt[...] = one_hot(down, token_q_across)
    mk[...] = one_hot(token_k, across)
    mkt[...] = one_hot(down, token_k_across)
    gexp[...] = jnp.zeros_like(gexp)
    tab[...] = jnp.zeros_like(tab)
    loads[3].wait()
    tab[0:heads, 0 : ENTRIES + 3] = rel[...]
    for h in range(heads):
        table = tab[h : h + 1, :]
        lined = pltpu.roll(jnp.broadcast_to(table, (24, TABLE)), TABLE - (GRID - 1), 1)
        uexp[...] = pltpu.roll(lined, 0, 1, stride=1, stride_axis=0)
        for x in range(SPAN):
            gexp[:, x * GRID : (x + 1) * GRID] = uexp[:, x * SPAN : x * SPAN + GRID]
        hankel = gexp[...]
        for r in range(GRID):
            moved = hankel if r == 0 else pltpu.roll(hankel, WIDE - r * GRID, 1)
            bias[h, r * GRID : (r + 1) * GRID, :] = moved[0:GRID, 0:seq]
        bias[h, CELLS:seq, :] = jnp.zeros((seq - CELLS, seq), f32)
        origin = bias[h, GRID - 1 : GRID, :]
        from_class = table[:, ENTRIES : ENTRIES + 1]
        to_class = table[:, ENTRIES + 1 : ENTRIES + 2]
        class_pair = table[:, ENTRIES + 2 : ENTRIES + 3]

        def settle(i, carry):
            part = pl.ds(pl.multiple_of(i * 128, 128), 128)
            place = lax.broadcasted_iota(i32, (128, 1), 0) + i * 128
            _, padded = query_tokens(place, high, wide)
            values = jnp.where(padded, origin, bias[h, part, :])
            values = jnp.where(across == CELLS, to_class, values)
            values = jnp.where(
                place == CELLS, jnp.where(across == CELLS, class_pair, from_class), values
            )
            bias[h, part, :] = jnp.where(token_k_across >= 0, values, masked)
            return carry

        lax.fori_loop(0, seq // 128, settle, 0)

    for i in (0, 4, 5, 6, 7):
        loads[i].wait()
    gain_one, shift_one = gains[0:1, :], biases[0:1, :]

    def project(s):
        normed, _ = normalize(xg[s].astype(f32))
        sent = (normed * gain_one + shift_one).astype(bf16)
        part = block(s)
        n1g[part, :] = sent
        qt[part, :] = ((dot_nt(sent, wqkv[0:hw, :]) + qvb[0:1, :]) * 0.125).astype(bf16)
        kt[part, :] = dot_nt(sent, wqkv[hw : 2 * hw, :]).astype(bf16)
        vt[part, :] = (dot_nt(sent, wqkv[2 * hw : 3 * hw, :]) + qvb[1:2, :]).astype(bf16)

    project(t)
    gather_near(0, xg)
    for half in range(2):
        pl.when(end == 0)(half_copy(1, cg, t, half, order[2], 1, cot_hbm).start)
    gather_take(0, xg, 1)
    project(order[1])
    gather_take(0, xg, 2)
    project(order[2])
    for k in range(1, NT):
        piece_arrived(8, pg.at[k, proj_rows, my_lanes], k)
    proj_all.send(3)
    gather_take(0, xg, 3)
    for half in range(2):
        pl.when(end == 0)(half_copy(1, cg, t, half, order[1], 0, cot_hbm).start)
    forward_both(1, cg, 1)
    project(order[3])
    forward_both(1, cg, 2)
    proj_all.spread_first()

    queries = dot(mq[...], qt[...]).astype(bf16)
    keys = dot(mk[...], kt[...]).astype(bf16)
    values = dot(mk[...], vt[...]).astype(bf16)
    for h in range(heads):
        lanes = slice(h * 64, (h + 1) * 64)
        qh[h] = queries[:, lanes]
        kh[h] = keys[:, lanes]
        vh[h] = values[:, lanes]
    for h in range(heads):
        logits = dot_nt(qh[h], kh[h]) + bias[h]
        raised = jnp.exp(logits - jnp.max(logits, axis=-1, keepdims=True))
        weights = raised * (1.0 / jnp.sum(raised, axis=-1, keepdims=True))
        prob[h] = weights
        rounded = weights.astype(bf16)
        probb[h] = rounded
        op[:, h * 64 : (h + 1) * 64] = dot(rounded, vh[h]).astype(bf16)
    ot[...] = dot_tn(op[...], mq[...]).astype(bf16)

    def mixed_piece(k):
        return piece_copy(2, ot.at[:, block((t + k) % NT)], og.at[NT - k], k)

    for k in (2, 1, 3):
        mixed_piece(k).start()
    forward_both(1, cg, 3)
    og[0] = ot[:, block(t)]
    total = dot_tn(og[0], pg[0])
    loads[2].wait()
    loads[12].wait()
    proj_all.spread_second()
    for k in range(1, NT):
        piece_arrived(2, og.at[k], k)
    proj_all.take(5)
    for k in range(1, NT):
        total = total + dot_tn(og[k], pg[k])
    branch_one = total + obias[0:1, :]
    a1[...] = branch_one
    after_one = xg[t].astype(f32) + scales[0:1, :] * branch_one
    x1[...] = after_one
    normed, inverse = normalize(after_one)
    xhat2[...] = normed
    inv2[...] = jnp.broadcast_to(inverse, inv2.shape)
    n2g[t] = (normed * gains[1:2, :] + biases[1:2, :]).astype(bf16)
    gather_start(3, n2g)

    for i in (9, 10, 11):
        loads[i].wait()
    shift_up = jnp.reshape(b1[...].astype(f32), (1, b1.shape[0]))

    def feed(step, half=None):
        s = order[step]
        inner = slice(None) if half is None else slice(half * half_rows, (half + 1) * half_rows)
        part = block(s) if half is None else span(s * rows + half * half_rows, half_rows)
        before = dot(n2g[s, inner, :], w1[...]) + shift_up
        cumulative = 0.5 * (1.0 + lax.erf(before * 0.7071067811865476))
        slope = cumulative + before * (jnp.exp(-0.5 * before * before) * 0.3989422804014327)
        hid[part, :] = (before * cumulative).astype(bf16)
        grad_rows = (cg[s, inner, :].astype(f32) * scales[1:2, :]).astype(bf16)
        dzg[s, inner, :] = grad_rows
        grad_pre = (dot_nt(grad_rows, w2[...]) * slope).astype(bf16)
        du[part, :] = grad_pre
        back = dot_nt(grad_pre, w1[...])
        if step == 0:
            dn2own[...] = back
        else:
            stage_b[3 - step, inner, :] = back.astype(bf16)
        return jnp.sum(grad_pre.astype(f32), axis=0, keepdims=True)

    loads[1].wait()
    bias_up = feed(0)
    gather_near(3, n2g)
    end_take(1, cg, 1)
    gather_take(3, n2g, 1)
    bias_up = bias_up + feed(1)
    scatter_copy(4, stage_b, dn2r, 2).start()
    end_take(1, cg, 2)
    for half in range(2):
        pl.when(end == 1)(lambda: half_arrived(3, n2g, 2, half))
    bias_up = bias_up + feed(2)
    for half in range(2):
        scatter_send(4, stage_b, dn2r, 1, half)
    end_take(1, cg, 3)
    for half in range(2):
        half_arrived(3, n2g, 3, half)
        pl.when(end == 0)(lambda: half_forward(3, n2g, 3, half))
    bias_up = bias_up + feed(3)
    for half in range(2):
        far_copy(4, stage_b, dn2r, half).start()
    sums[8:9, :] = bias_up
    scatter_merge(4, stage_b, dn2r, 1, 0)
    scatter_merge(4, stage_b, dn2r, 1, 1)
    down_rows = jnp.reshape(dzg[...], (seq, width))
    g_down[0] = dot_tn(hid[...], down_rows).astype(bf16)
    down_sum.send(0)
    up_rows = jnp.reshape(n2g[...], (seq, width))
    g_up[0] = dot_tn(up_rows, du[...]).astype(bf16)
    up_sum.send(0)
    shared = jnp.zeros((1, width), f32)
    for step, s in enumerate(order):
        piece = dot(hid[block(s), :], w2[...])
        shared = shared + jnp.sum(cg[s].astype(f32) * piece, axis=0, keepdims=True)
        if step == 0:
            own[...] = piece
        else:
            stage_c[3 - step] = piece.astype(bf16)
    cot = cg[t].astype(f32)
    cot_sum = jnp.sum(cot, axis=0, keepdims=True)
    sums[5:6, :] = shared + cot_sum * obias[1:2, :]
    sums[7:8, :] = cot_sum * scales[1:2, :]
    down_sum.add_core()
    up_sum.add_core()

    @pl.when(end == 1)
    def _():
        slot_wait(4, dn2r, 0, 0)
        slot_wait(4, dn2r, 0, 1)
        dn2own[...] = dn2own[...] + dn2r[0].astype(f32)

    total = scatter_total(4, dn2r, dn2own[...], (3,))
    normed = xhat2[...]
    sums[3:4, :] = jnp.sum(total, axis=0, keepdims=True)
    sums[1:2, :] = jnp.sum(total * normed, axis=0, keepdims=True)
    after = cg[t].astype(f32) + norm_back(total * gains[1:2, :], normed, inv2[:, 0:1])
    dx1[...] = after
    branch = after * scales[0:1, :]
    grad_rows = branch.astype(bf16)

    def mixed_back(k):
        return piece_copy(6, doz.at[k], dot_t.at[:, block(t)], k)

    for k in (2, 1, 3, 0):
        piece = dot_nt(pg[k], grad_rows).astype(bf16)
        if k == 0:
            dot_t[:, block(t)] = piece
        else:
            doz[k] = piece
            mixed_back(k).start()
    for i in (1, 0, 2):
        scatter_send(5, stage_c, z2r, i)
    sums[4:5, :] = jnp.sum(after * a1[...], axis=0, keepdims=True)
    sums[6:7, :] = jnp.sum(branch, axis=0, keepdims=True)
    for k in range(NT):
        g_proj[k] = dot(og[k], grad_rows).astype(bf16)
    proj_sum.send(0)
    down_sum.add_first()
    up_sum.add_first()
    scatter_merge(5, stage_c, z2r, 1)
    proj_sum.add_core()

    for k in range(1, NT):
        piece_arrived(6, dot_t.at[:, block((t + k) % NT)], k)
    grad_mixed = dot_nt(mq[...], dot_t[...]).astype(bf16)
    for h in range(heads):
        doh[h] = grad_mixed[:, h * 64 : (h + 1) * 64]
    for h in range(heads):
        lanes = slice(h * 64, (h + 1) * 64)

        grad_prob = dot_nt(doh[h], vh[h])
        weights = prob[h]
        crossed = jnp.sum(weights * grad_prob, axis=-1, keepdims=True)
        rounded = (weights * (grad_prob - crossed)).astype(bf16)
        ds[h] = rounded
        dqp[:, lanes] = dot(rounded, kh[h]).astype(bf16) * 0.125
        dvp[:, lanes] = dot_tn(probb[h], doh[h]).astype(bf16)
        dkp[:, lanes] = dot_tn(rounded, qh[h]).astype(bf16)
        part_q = dot(mqt[...], dqp[:, lanes]).astype(bf16)
        part_k = dot(mkt[...], dkp[:, lanes]).astype(bf16)
        part_v = dot(mkt[...], dvp[:, lanes]).astype(bf16)
        dqt[:, lanes] = part_q
        dkt[:, lanes] = part_k
        dvt[:, lanes] = part_v
        for i, part in enumerate((part_q, part_k, part_v)):
            direct_refs[h][0][64 * i : 64 * (i + 1), :] = dot_tn(part, n1g[...]).astype(bf16)
        qkv_sums[h].send()
        if h == 0:
            down_sum.add_second()
            up_sum.add_second()
        elif h == 1:
            proj_sum.add_first()
            scatter_merge(5, stage_c, z2r, 0)
            qkv_sums[0].add_core()
    qkv_sums[1].add_core()

    shift_total = jnp.zeros((1, width), f32)
    gain_total = jnp.zeros((1, width), f32)
    for step in (3, 2, 1, 0):
        s = order[step]
        part = block(s)
        piece = dot(dqt[part, :], wqkv[0:hw, :]) + dot(dkt[part, :], wqkv[hw : 2 * hw, :])
        piece = piece + dot(dvt[part, :], wqkv[2 * hw : 3 * hw, :])
        if step == 0:
            dn2own[...] = piece
        else:
            stage_d[3 - step] = piece.astype(bf16)
        normed, _ = normalize(xg[s].astype(f32))
        shift_total = shift_total + jnp.sum(piece, axis=0, keepdims=True)
        gain_total = gain_total + jnp.sum(piece * normed, axis=0, keepdims=True)
    sums[2:3, :] = shift_total
    sums[0:1, :] = gain_total
    zmr[t] = sums[0:REP, :]

    def small_tensor(k):
        return remote(
            zmr.at[t], zmr.at[t], z_send.at[10, k], z_recv.at[10, NT - k], (dp, (t + k) % NT)
        )

    for k in range(1, NT):
        small_tensor(k).start()
    for i in (0, 1):
        for half in range(2):
            scatter_send(7, stage_d, dn1r, i, half)
    qkv_sums[2].add_core()
    down_sum.spread_first()
    up_sum.spread_first()
    proj_sum.add_second(gpz)

    def proj_exchange(k):
        return piece_copy(9, gpz.at[k], gpz.at[2 * NT - k], k)

    for k in range(1, NT):
        proj_exchange(k).start()
    scatter_send(7, stage_d, dn1r, 2)
    qkv_sums[0].add_parts()

    branch_two = scatter_total(5, z2r, own[...]) + obias[1:2, :]
    outv[...] = (x1[...] + scales[1:2, :] * branch_two).astype(bf16)
    stores = [pltpu.make_async_copy(outv, out, store_sem.at[0])]
    stores[0].start()

    row24 = lax.broadcasted_iota(i32, (24, 1), 0)
    lane_t = lax.broadcasted_iota(i32, (1, TABLE), 1)
    uexp[...] = jnp.zeros_like(uexp)
    gexp[...] = jnp.zeros_like(gexp)
    for h in range(heads):
        grads = ds[h].astype(f32)
        class_row = grads[CELLS : CELLS + 1, :]
        class_column = jnp.sum(
            jnp.where((down != CELLS) & (across == CELLS), grads, 0.0), axis=0, keepdims=True
        )
        cells = jnp.where(across < CELLS, grads, 0.0)
        pad_row = jnp.sum(jnp.where(pad_q, cells, 0.0), axis=0, keepdims=True)
        dsf[...] = jnp.where(pad_q, 0.0, cells)
        blank = jnp.zeros((24, WIDE - seq), f32)
        folded = jnp.zeros((24, WIDE), f32)
        for r in range(GRID):
            cells = jnp.concatenate([dsf[r * GRID : r * GRID + 24, :], blank], axis=1)
            folded = folded + (cells if r == 0 else pltpu.roll(cells, r * GRID, 1))
        padded_row = jnp.concatenate([pad_row, jnp.zeros((1, WIDE - seq), f32)], axis=1)
        folded = jnp.where(row24 < GRID, folded, 0.0) + jnp.where(row24 == GRID - 1, padded_row, 0.0)
        for i in range(GRID):
            gexp[GRID - 1 - i : GRID - i, :] = folded[i : i + 1, :]
        for x in range(SPAN):
            uexp[:, x * SPAN : x * SPAN + GRID] = gexp[:, x * GRID : (x + 1) * GRID]
        lined = pltpu.roll(uexp[...], 0, 1, stride=1, stride_axis=0)
        table = jnp.sum(lined, axis=0, keepdims=True)
        from_class = jnp.sum(jnp.where(across != CELLS, class_row, 0.0), axis=1, keepdims=True)
        class_pair = jnp.sum(jnp.where(across == CELLS, class_row, 0.0), axis=1, keepdims=True)
        to_class = jnp.sum(class_column, axis=1, keepdims=True)
        table = jnp.where(lane_t == ENTRIES, from_class, table)
        table = jnp.where(lane_t == ENTRIES + 1, to_class, table)
        tab[h : h + 1, :] = jnp.where(lane_t == ENTRIES + 2, class_pair, table)
        if h == 1:
            qkv_sums[1].add_parts()
    sums[9:10, 0:hw] = jnp.sum(dqt[...].astype(f32), axis=0, keepdims=True)
    sums[10:11, 0:hw] = jnp.sum(dvt[...].astype(f32), axis=0, keepdims=True)
    sums[9:11, hw:width] = jnp.zeros((2, width - hw), f32)
    for h in range(heads):
        at = 11 + 3 * h
        sums[at : at + 1, :] = tab[h : h + 1, 0:width]
        sums[at + 1 : at + 2, :] = tab[h : h + 1, width : 2 * width]
        sums[at + 2 : at + 3, 0 : TABLE - 2 * width] = tab[h : h + 1, 2 * width : TABLE]
        sums[at + 2 : at + 3, TABLE - 2 * width : width] = jnp.zeros((1, 3 * width - TABLE), f32)
    sums[11 + 3 * heads : SMALL, :] = jnp.zeros((SMALL - 11 - 3 * heads, width), f32)

    scatter_merge(7, stage_d, dn1r, 0, 0)
    scatter_merge(7, stage_d, dn1r, 0, 1)
    for k in range(1, NT):
        piece_arrived(10, zmr.at[(t + k) % NT], k)
    sums[0:REP, :] = zmr[0] + zmr[1] + zmr[2] + zmr[3]
    g_small[...] = sums[...].astype(bf16)
    small_sum.send()
    qkv_sums[2].add_parts()
    small_sum.add_core()
    value = gpz[0].astype(f32)
    for k in range(1, NT):
        piece_arrived(9, gpz.at[NT + k], k)
        value = value + gpz[NT + k].astype(f32)
    t_proj[0, proj_rows, my_lanes] = value.astype(bf16)
    proj_sum.send(3)
    down_sum.spread_second()
    qkv_sums[0].spread()
    scatter_merge(7, stage_d, dn1r, 1, 0)
    scatter_merge(7, stage_d, dn1r, 1, 1)
    qkv_sums[1].spread()
    up_sum.spread_second()
    small_sum.add_parts()
    proj_sum.spread_first()
    qkv_sums[2].spread()
    sources = [(t_down.at[0], t_down_hbm), (t_up.at[0], t_up_hbm), (t_proj.at[0], t_proj_hbm), (t_small.at[0], t_small_hbm)]
    sources += [(t_qkv.at[h], t_qkv_hbm.at[192 * h : 192 * (h + 1), :]) for h in range(heads)]
    sources += [(ingradv, ingrad)]
    stores += [pltpu.make_async_copy(src, dst, store_sem.at[i + 1]) for i, (src, dst) in enumerate(sources)]
    down_sum.take(5)
    stores[1].start()
    total = scatter_total(7, dn1r, dn2own[...], (3,))
    normed, inverse = normalize(xg[t].astype(f32))
    ingradv[...] = dx1[...] + norm_back(total * gain_one, normed, inverse)
    stores[8].start()
    small_sum.spread()
    proj_sum.spread_second()
    up_sum.take(5)
    stores[2].start()
    for h in range(heads):
        qkv_sums[h].take()
        stores[5 + h].start()
    proj_sum.take(5)
    stores[3].start()
    small_sum.take()
    stores[4].start()

    gather_sent(0, xg, x_hbm)
    gather_sent(1, cg, cot_hbm)
    gather_sent(3, n2g)
    for i in range(NT - 1):
        scatter_copy(5, stage_c, z2r, i).wait_send()
    scatter_copy(4, stage_b, dn2r, 2).wait_send()
    scatter_copy(7, stage_d, dn1r, 2).wait_send()
    for half in range(2):
        far_copy(4, stage_b, dn2r, half).wait_send()
        scatter_copy(4, stage_b, dn2r, 1, half).wait_send()
        scatter_copy(7, stage_d, dn1r, 0, half).wait_send()
        scatter_copy(7, stage_d, dn1r, 1, half).wait_send()
    for k in range(1, NT):
        proj_piece(k).wait_send()
        mixed_piece(k).wait_send()
        mixed_back(k).wait_send()
        proj_exchange(k).wait_send()
        small_tensor(k).wait_send()
    for part_sum in (down_sum, up_sum, proj_sum, small_sum, *qkv_sums):
        part_sum.sent()
    proj_all.sent(3)
    for store in stores:
        store.wait()


def finish_kernel(
    down_in, up_in, proj_in, qkv_in, small_in, out_in, ingrad_in,
    out, ingrad, g_qkv, g_qv, g_table, g_proj, g_up, g_up_bias, g_down, g_gains, g_shifts, g_scales, g_biases,
    down_v, up_v, proj_v, qkv_v, down_f, up_f, proj_f, qkv_f, small_v, out_v, ingrad_v, load_sem, store_sem,
):
    width = g_down.shape[1]
    hw = g_proj.shape[0]
    heads, entries = g_table.shape
    parts = []
    for given, rounded, widened, result in (
        (down_in, down_v, down_f, g_down), (up_in, up_v, up_f, g_up),
        (qkv_in, qkv_v, qkv_f, g_qkv), (proj_in, proj_v, proj_f, g_proj),
    ):
        for start in range(0, given.shape[0], PIECE):
            piece = [ref.at[start : start + PIECE, :] for ref in (given, rounded, widened, result)]
            parts.append(piece + [given is qkv_in])
    moved = [(small_in, small_v, None), (out_in, out_v, out), (ingrad_in, ingrad_v, ingrad)]
    count = len(parts)
    loads = [pltpu.make_async_copy(part[0], part[1], load_sem.at[i]) for i, part in enumerate(parts)]
    loads += [pltpu.make_async_copy(src, via, load_sem.at[count + i]) for i, (src, via, _) in enumerate(moved)]
    for copy in loads:
        copy.start()
    stores = []
    by_head = [i for i, part in enumerate(parts) if part[4]]
    for i, (_, rounded, widened, result, mixed) in enumerate(parts):
        if mixed:
            which = i - by_head[0]
            for h, j in enumerate(by_head):
                if which == 0:
                    loads[j].wait()
                widened[64 * h : 64 * (h + 1), :] = parts[j][1][64 * which : 64 * (which + 1), :].astype(f32)
        else:
            loads[i].wait()
            widened[...] = rounded[...].astype(f32)
        stores.append(pltpu.make_async_copy(widened, result, store_sem.at[i]))
        stores[-1].start()
    for i, (_, via, dst) in enumerate(moved):
        loads[count + i].wait()
        if dst is not None:
            stores.append(pltpu.make_async_copy(via, dst, store_sem.at[count + i]))
            stores[-1].start()
    small = small_v[...].astype(f32)
    g_gains[...] = small[0:2, :]
    g_shifts[...] = small[2:4, :]
    g_scales[...] = small[4:6, :]
    g_biases[...] = small[6:8, :]
    g_up_bias[...] = jnp.reshape(small[8:9, :], (width,))
    g_qv[...] = small[9:11, 0:hw]
    for h in range(heads):
        for j in range(3):
            lanes = min(width, entries - j * width)
            g_table[h : h + 1, j * width : j * width + lanes] = small[
                11 + 3 * h + j : 12 + 3 * h + j, 0:lanes
            ]
    for copy in stores:
        copy.wait()


def per_device(
    n_dp, tokens, grids, qkv_weight, qv_bias, rel_table, proj_weight, fc1_weight, fc1_bias, fc2_weight,
    norm_gains, norm_biases, layer_scales, out_biases, cotangent,
):
    rows, width = tokens.shape
    seq = rows * NT
    heads, entries = rel_table.shape
    hw = heads * 64
    ff = fc1_weight.shape[1]
    qkv_rows = jnp.transpose(qkv_weight, (1, 2, 0)).reshape(3 * hw, width)
    vm = pl.BlockSpec(memory_space=pltpu.VMEM)
    anywhere = pl.BlockSpec(memory_space=pl.ANY)

    def many(count, shape, dtype):
        return [pltpu.VMEM(shape, dtype)] * count

    def sems(*shape):
        return [pltpu.SemaphoreType.DMA(shape)]

    half = width // 2
    scratch = [
        pltpu.VMEM((rows, width), bf16), pltpu.VMEM((rows, width), f32), pltpu.VMEM((3 * hw, width), bf16),
        pltpu.VMEM((width, ff), bf16), pltpu.VMEM((ff, width), bf16),
        pltpu.VMEM((2, hw), f32), pltpu.VMEM((heads, entries), f32), pltpu.VMEM((ff,), bf16),
    ]
    scratch += many(4, (2, width), f32) + sems(13) + sems(9)
    scratch += many(4, (NT, rows, width), bf16)
    scratch += many(1, (NT, hw, rows), bf16) + many(1, (NT, hw, width), bf16)
    scratch += many(3, (NT, rows, width), bf16) + many(3, (NT - 1, rows, width), bf16)
    scratch += many(1, (NT, hw, rows), bf16) + sems(11, 2 * NT) + sems(11, 2 * NT) + sems(4, 5, 2)
    scratch += many(4, (seq, seq), bf16)
    scratch += many(1, (heads, seq, seq), f32) + many(1, (24, WIDE), f32) + many(1, (24, TABLE), f32)
    scratch += many(1, (seq, width), bf16) + many(3, (seq, hw), bf16)
    scratch += many(3, (heads, seq, 64), bf16)
    scratch += many(1, (heads, seq, seq), f32) + many(1, (heads, seq, seq), bf16)
    scratch += many(1, (seq, hw), bf16) + many(1, (hw, seq), bf16)
    scratch += many(2, (rows, width), f32) + many(1, (rows, 128), f32) + many(4, (rows, width), f32)
    scratch += many(2, (seq, ff), bf16) + many(1, (hw, seq), bf16) + many(1, (heads, seq, 64), bf16)
    scratch += many(1, (heads, seq, seq), bf16) + many(1, (seq, seq), f32) + many(6, (seq, hw), bf16)
    scratch += many(1, (8, TABLE), f32) + many(1, (SMALL, width), f32) + many(1, (NT, REP, width), f32)
    scratch += many(1, (2 * NT, hw // 4, half), bf16) + sems(5 + heads, 8) + sems(5 + heads, 8)
    for lead, count in ((1, ff), (1, width), (NT, hw)):
        scratch += [
            pltpu.VMEM((lead, count, width), bf16), pltpu.VMEM((lead, count, half), bf16),
            pltpu.VMEM((lead, count, half), bf16), pltpu.VMEM((lead, count // 2, half), bf16),
            pltpu.VMEM((lead, count // 4, half), bf16),
        ]
    for count in (192,) * heads + (SMALL,):
        scratch += [
            pltpu.VMEM((count, width), bf16), pltpu.VMEM((count, half), bf16), pltpu.VMEM((count, half), bf16),
            pltpu.VMEM((CHIPS - 1, count // CHIPS, half), bf16),
        ]
    for lead, count in ((1, ff), (1, width), (1, hw), (heads, 192), (1, SMALL)):
        scratch += many(1, (lead, count, width), bf16)
    flat = [jax.ShapeDtypeStruct((count, width), bf16) for count in (ff, width, hw, 3 * hw, SMALL)]
    output, input_grad, *totals = pl.pallas_call(
        main_kernel,
        out_shape=[
            jax.ShapeDtypeStruct((rows, width), bf16),
            jax.ShapeDtypeStruct((rows, width), f32),
        ]
        + flat,
        in_specs=[pl.BlockSpec(memory_space=pltpu.SMEM)] + [anywhere] * 13,
        out_specs=[anywhere] * 7,
        scratch_shapes=scratch,
        compiler_params=pltpu.CompilerParams(
            collective_id=0, has_side_effects=True, vmem_limit_bytes=60 << 20
        ),
        name="layer",
    )(
        grids, tokens, cotangent, qkv_rows, proj_weight, fc1_weight, fc2_weight,
        qv_bias, rel_table, fc1_bias, norm_gains, norm_biases, layer_scales, out_biases,
    )
    pair = jax.ShapeDtypeStruct((2, width), f32)
    pieces = sum(-(-count // PIECE) for count in (ff, width, hw, 3 * hw))
    results = pl.pallas_call(
        finish_kernel,
        out_shape=(
            jax.ShapeDtypeStruct((rows, width), bf16),
            jax.ShapeDtypeStruct((rows, width), f32),
            jax.ShapeDtypeStruct((3 * hw, width), f32),
            jax.ShapeDtypeStruct((2, hw), f32),
            jax.ShapeDtypeStruct((heads, entries), f32),
            jax.ShapeDtypeStruct((hw, width), f32),
            jax.ShapeDtypeStruct((width, ff), f32),
            jax.ShapeDtypeStruct((ff,), f32),
            jax.ShapeDtypeStruct((ff, width), f32),
            pair, pair, pair, pair,
        ),
        in_specs=[anywhere] * 7,
        out_specs=(
            anywhere, anywhere, anywhere, vm, vm, anywhere, anywhere, vm, anywhere, vm, vm, vm, vm,
        ),
        scratch_shapes=[
            pltpu.VMEM((ff, width), bf16), pltpu.VMEM((width, ff), bf16), pltpu.VMEM((hw, width), bf16),
            pltpu.VMEM((3 * hw, width), bf16),
            pltpu.VMEM((ff, width), f32), pltpu.VMEM((width, ff), f32), pltpu.VMEM((hw, width), f32),
            pltpu.VMEM((3 * hw, width), f32), pltpu.VMEM((SMALL, width), bf16),
            pltpu.VMEM((rows, width), bf16), pltpu.VMEM((rows, width), f32),
            *sems(pieces + 3), *sems(pieces + 3),
        ],
        compiler_params=pltpu.CompilerParams(vmem_limit_bytes=60 << 20),
        name="finish",
    )(*totals, output, input_grad)
    results = list(results)
    stride = GROUP
    while stride < n_dp:
        hops = [(i, i ^ stride) for i in range(n_dp)]
        results[2:] = [value + lax.ppermute(value, "dp", hops) for value in results[2:]]
        stride *= 2
    results[2] = jnp.transpose(results[2].reshape(3, hw, width), (2, 0, 1))
    return tuple(results)


def solution(mesh):
    n_dp = mesh.shape["dp"]
    blocks = P(("dp", "tensor"), None)
    placed = (
        blocks, P("dp", None), P(None, None, "tensor"), P(None, "tensor"), P("tensor", None), P("tensor", None),
        P(None, "tensor"), P("tensor"), P("tensor", None), P(), P(), P(), P(), blocks,
    )
    given = (
        blocks, blocks, P(None, None, "tensor"), P(None, "tensor"), P("tensor", None), P("tensor", None),
        P(None, "tensor"), P("tensor"), P("tensor", None), P(), P(), P(), P(),
    )

    def layer(*arrays):
        return per_device(n_dp, *arrays)

    return jax.shard_map(layer, mesh=mesh, in_specs=placed, out_specs=given, check_vma=False)
```

```python
import jax
import jax.numpy as jnp
from jax import lax
from jax.experimental import pallas as pl
from jax.experimental.pallas import tpu as pltpu
from jax.sharding import PartitionSpec as P

GRID = 22
SPAN = 2 * GRID - 1
CELLS = GRID * GRID
ENTRIES = SPAN * SPAN
MESH = pl.DeviceIdType.MESH
f32 = jnp.float32
bf16 = jnp.bfloat16
i32 = jnp.int32

eps_norm = 1e-06
masked = -1e30
NT = 4
CHIPS = 4
CORES = 2
GROUP = CHIPS * CORES
TABLE = 1920
WIDE = 1024
SMALL = 64
REP = 8
PIECE = 192


def dot(left, right):
    return lax.dot_general(left, right, (((1,), (0,)), ((), ())), preferred_element_type=f32)


def dot_nt(left, right):
    return lax.dot_general(left, right, (((1,), (1,)), ((), ())), preferred_element_type=f32)


def dot_tn(left, right):
    return lax.dot_general(left, right, (((0,), (0,)), ((), ())), preferred_element_type=f32)


def normalize(values):
    center = values - jnp.mean(values, axis=-1, keepdims=True)
    inverse = lax.rsqrt(jnp.mean(center * center, axis=-1, keepdims=True) + eps_norm)
    return center * inverse, inverse


def norm_back(grad_normed, normed, inverse):
    average = jnp.mean(grad_normed, axis=-1, keepdims=True)
    crossed = jnp.mean(grad_normed * normed, axis=-1, keepdims=True)
    return inverse * (grad_normed - average - normed * crossed)


def split_cell(place):
    row = (place * 2979) >> 16
    return row, place - row * GRID


def query_tokens(place, high, wide):
    row, back = split_cell(place)
    inside = (place < CELLS) & (row < high) & (GRID - 1 - back < wide)
    before = jnp.minimum(row, high) * wide + jnp.where(
        row < high, jnp.maximum(back - (GRID - wide), 0), 0
    )
    token = jnp.where(inside, 1 + row * wide + (GRID - 1 - back), high * wide + 1 + place - before)
    token = jnp.where(place == CELLS, 0, jnp.where(place > CELLS, place, token))
    padding = jnp.logical_not(inside) & (place != CELLS)
    return token, padding


def key_tokens(place, high, wide):
    row, back = split_cell(place)
    row = GRID - 1 - row
    column = GRID - 1 - back
    inside = (place < CELLS) & (row < high) & (column < wide)
    token = jnp.where(inside, 1 + row * wide + column, -1)
    return jnp.where(place == CELLS, 0, token)


def one_hot(left, right):
    return jnp.where(left == right, 1.0, 0.0).astype(bf16)


def main_kernel(
    grids, x_hbm, cot_hbm, wqkv_hbm, wproj_hbm, w1_hbm, w2_hbm, qvb_hbm, rel_hbm, b1_hbm,
    gains_hbm, biases_hbm, scales_hbm, obias_hbm,
    out, ingrad, t_down_hbm, t_up_hbm, t_proj_hbm, t_qkv_hbm, t_small_hbm,
    outv, ingradv, wqkv, w1, w2, qvb, rel, b1, gains, biases, scales, obias, load_sem, store_sem,
    xg, cg, dzg, n2g, og, pg, dn2r, z2r, dn1r, stage_b, stage_c, stage_d, doz, z_send, z_recv, z_half,
    mq, mqt, mk, mkt, bias, gexp, uexp,
    n1g, qt, kt, vt, qh, kh, vh, prob, probb, op, ot,
    x1, xhat2, inv2, a1, dx1, own, dn2own,
    hid, du, dot_t, doh, ds, dsf, dqp, dkp, dvp, dqt, dkt, dvt,
    tab, sums, zmr, gpz, p_send, p_recv,
    *plane,
):
    dp = lax.axis_index("dp")
    t = lax.axis_index("tensor")
    rows, width = x_hbm.shape
    seq = rows * NT
    heads = rel.shape[0]
    hw = heads * 64
    base = (dp // GROUP) * GROUP
    mine = dp % GROUP
    core = mine % CORES
    chip_x = (mine // 2) % 2
    chip_y = mine // 4
    to_x = 2 - 4 * chip_x
    to_y = 4 - 8 * chip_y
    sibling = base + mine + 1 - 2 * core
    first_peer = base + mine + (1 - core) * to_x + core * to_y
    second_peer = base + mine + core * to_x + (1 - core) * to_y
    bit_one = (1 - core) * chip_x + core * chip_y
    bit_two = core * chip_x + (1 - core) * chip_y
    quarter = bit_one * 2 + bit_two
    end = ((t - 1) * (t - 2)) // 2
    order = [t, t + 1 - 2 * (t % 2), 2 - t // 2, 3 - 3 * (t // 2)]

    pairs = [
        (x_hbm, xg.at[t]), (cot_hbm, cg.at[t]), (scales_hbm, scales), (rel_hbm, rel), (wqkv_hbm, wqkv),
        (gains_hbm, gains), (biases_hbm, biases), (qvb_hbm, qvb), (wproj_hbm, pg.at[0]), (w1_hbm, w1),
        (w2_hbm, w2), (b1_hbm, b1), (obias_hbm, obias),
    ]
    loads = [pltpu.make_async_copy(src, dst, load_sem.at[i]) for i, (src, dst) in enumerate(pairs)]
    for load in loads:
        load.start()
    barrier = pltpu.get_barrier_semaphore()
    for k in range(1, NT):
        pl.semaphore_signal(barrier, inc=1, device_id=(dp, (t + k) % NT), device_id_type=MESH)
    chip = mine // CORES
    others = [base + ((chip + k) % CHIPS) * CORES + core for k in range(CHIPS)]
    for peer in (sibling, *others[1:]):
        pl.semaphore_signal(barrier, inc=1, device_id=(peer, t), device_id_type=MESH)
    pl.semaphore_wait(barrier, NT - 1 + CHIPS)

    def block(s):
        return pl.ds(pl.multiple_of(s * rows, rows), rows)

    def remote(src, dst, send, recv, device):
        return pltpu.make_async_remote_copy(
            src_ref=src, dst_ref=dst, send_sem=send, recv_sem=recv, device_id=device, device_id_type=MESH
        )

    half_rows = rows // 2

    def half_copy(phase, buf, src, half, dst, way, given=None):
        spot = buf.at[src, half * half_rows : (half + 1) * half_rows, :]
        if given is not None:
            given = given.at[half * half_rows : (half + 1) * half_rows, :]
        return remote(
            spot if given is None else given, spot,
            z_half.at[phase, way, half], z_recv.at[phase, src * 2 + half], (dp, dst),
        )

    def gather_start(phase, buf, given=None):
        for half in range(2):
            half_copy(phase, buf, t, half, order[1], 0, given).start()
            pl.when(end == 0)(half_copy(phase, buf, t, half, order[2], 1, given).start)

    def half_arrived(phase, buf, step, half):
        half_copy(phase, buf, order[step], half, order[1], 0).wait_recv()

    def half_forward(phase, buf, step, half):
        to = order[2] if step == 1 else order[1]
        half_copy(phase, buf, order[step], half, to, 1 + step).start()

    def gather_near(phase, buf):
        @pl.when(end == 0)
        def _():
            for half in range(2):
                for step in (1, 2):
                    half_arrived(phase, buf, step, half)
                    half_forward(phase, buf, step, half)

    def forward_both(phase, buf, step):
        @pl.when(end == 0)
        def _():
            for half in range(2):
                half_arrived(phase, buf, step, half)
                half_forward(phase, buf, step, half)

    def end_take(phase, buf, step):
        for half in range(2):
            pl.when(end == 1)(lambda: half_arrived(phase, buf, step, half))

    def gather_take(phase, buf, step):
        for half in range(2):
            if step < 3:
                pl.when(end == 1)(lambda: half_arrived(phase, buf, step, half))
            else:
                half_arrived(phase, buf, step, half)
                pl.when(end == 0)(lambda: half_forward(phase, buf, step, half))

    def gather_sent(phase, buf, given=None):
        for half in range(2):
            half_copy(phase, buf, t, half, order[1], 0, given).wait_send()

            @pl.when(end == 0)
            def _():
                half_copy(phase, buf, t, half, order[2], 1, given).wait_send()
                for step in (1, 2, 3):
                    half_copy(phase, buf, order[step], half, order[1], 1 + step).wait_send()

    def scatter_part(phase, stage, buf, i, dst, slot, half):
        if half is None:
            return remote(
                stage.at[i], buf.at[slot], z_send.at[phase, i], z_recv.at[phase, slot], (dp, dst)
            )
        part = slice(half * half_rows, (half + 1) * half_rows)
        return remote(
            stage.at[i, part, :], buf.at[slot, part, :],
            z_send.at[phase, i + NT * half], z_recv.at[phase, slot + NT * half], (dp, dst),
        )

    def scatter_copy(phase, stage, buf, i, half=None):
        if i == 2:
            dst, slot = order[1], 2
        else:
            dst = end * order[1] + (1 - end) * order[3 - i]
            slot = end * i + (1 - end) * 3
        return scatter_part(phase, stage, buf, i, dst, slot, half)

    def far_copy(phase, stage, buf, half):
        return scatter_part(phase, stage, buf, 0, order[3], (1 - end) * 3, half)

    def slot_wait(phase, buf, slot, half=None):
        scatter_part(phase, buf, buf, slot, order[1], slot, half).wait_recv()

    def scatter_send(phase, stage, buf, i, half=None):
        if i == 2:
            scatter_copy(phase, stage, buf, i, half).start()
        else:
            pl.when(end == 1)(scatter_copy(phase, stage, buf, i, half).start)

    def scatter_merge(phase, stage, buf, i, half=None):
        part = slice(None) if half is None else slice(half * half_rows, (half + 1) * half_rows)

        @pl.when(end == 0)
        def _():
            slot_wait(phase, buf, i, half)
            stage[i, part, :] = (stage[i, part, :].astype(f32) + buf[i, part, :].astype(f32)).astype(bf16)
            scatter_copy(phase, stage, buf, i, half).start()

    def scatter_total(phase, buf, total, halves=()):
        for slot in (2, 3):
            if slot in halves:
                slot_wait(phase, buf, slot, 0)
                slot_wait(phase, buf, slot, 1)
            else:
                slot_wait(phase, buf, slot)
            total = total + buf[slot].astype(f32)
        return total

    def piece_copy(phase, src, dst, k):
        return remote(
            src, dst, z_send.at[phase, k], z_recv.at[phase, NT - k], (dp, (t + k) % NT)
        )

    def piece_arrived(phase, dst, k):
        remote(dst, dst, z_send.at[phase, k], z_recv.at[phase, k], (dp, (t + k) % NT)).wait_recv()

    half_width = width // 2
    my_lanes = pl.ds(pl.multiple_of(core * half_width, half_width), half_width)
    your_lanes = pl.ds(pl.multiple_of((1 - core) * half_width, half_width), half_width)

    def span(start, count):
        return pl.ds(pl.multiple_of(start, 16), count)

    class Plane:
        def __init__(self, index, refs, target):
            self.index, self.target = index, target
            self.count = target.shape[1]
            self.fours = self.count // 4
            if refs is not None:
                self.given, self.near, self.held, self.one, self.two = refs
                self.lead = self.given.shape[0]

        def copy(self, step, src, dst, peer):
            return remote(
                src, dst, p_send.at[self.index, step], p_recv.at[self.index, step], (peer, t)
            )

        def outgoing(self, step):
            c, f = self.count, self.fours
            if step == 0:
                return self.copy(0, self.given.at[:, :, your_lanes], self.near, sibling)
            if step == 1:
                src = self.held.at[:, span((1 - bit_one) * 2 * f, 2 * f), :]
                return self.copy(1, src, self.one, first_peer)
            if step == 2:
                src = self.held.at[:, span((bit_one * 2 + 1 - bit_two) * f, f), :]
                return self.copy(2, src, self.two, second_peer)
            if step == 3:
                spot, peer = self.target.at[:, span(quarter * f, f), my_lanes], second_peer
            elif step == 4:
                spot, peer = self.target.at[:, span(bit_one * 2 * f, 2 * f), my_lanes], first_peer
            else:
                spot, peer = self.target.at[:, :, my_lanes], sibling
            return self.copy(step, spot, spot, peer)

        def incoming(self, step):
            f = self.fours
            if step < 3:
                return self.outgoing(step)
            if step == 3:
                spot = self.target.at[:, span((bit_one * 2 + 1 - bit_two) * f, f), my_lanes]
            elif step == 4:
                spot = self.target.at[:, span((1 - bit_one) * 2 * f, 2 * f), my_lanes]
            else:
                spot = self.target.at[:, :, your_lanes]
            return self.copy(step, spot, spot, sibling)

        def send(self, step):
            self.outgoing(step).start()

        def take(self, step):
            self.incoming(step).wait_recv()

        def add_core(self):
            self.take(0)
            for q in range(self.lead):
                value = self.given[q, :, my_lanes].astype(f32) + self.near[q].astype(f32)
                self.held[q] = value.astype(bf16)
            self.send(1)

        def add_first(self):
            self.take(1)
            part = span(bit_one * 2 * self.fours, 2 * self.fours)
            for q in range(self.lead):
                value = self.held[q, part, :].astype(f32) + self.one[q].astype(f32)
                self.held[q, part, :] = value.astype(bf16)
            self.send(2)

        def add_second(self, store=None):
            self.take(2)
            part = span(quarter * self.fours, self.fours)
            for q in range(self.lead):
                value = (self.held[q, part, :].astype(f32) + self.two[q].astype(f32)).astype(bf16)
                if store is None:
                    self.target[q, part, my_lanes] = value
                else:
                    store[q] = value
            if store is None:
                self.send(3)

        def spread_first(self):
            self.take(3)
            self.send(4)

        def spread_second(self):
            self.take(4)
            self.send(5)

        def sent(self, first=0):
            for step in range(first, 6):
                self.outgoing(step).wait_send()

    class Direct:
        def __init__(self, index, refs, target):
            self.index, self.target = index, target
            self.fours = target.shape[1] // CHIPS
            self.given, self.near, self.held, self.parts = refs

        def copy(self, step, src, dst, peer):
            return remote(
                src, dst, p_send.at[self.index, step], p_recv.at[self.index, step], (peer, t)
            )

        def rows_of(self, k):
            return span(((chip + k) % CHIPS) * self.fours, self.fours)

        def core_copy(self):
            return self.copy(0, self.given.at[:, your_lanes], self.near, sibling)

        def part_copy(self, k):
            return self.copy(k, self.held.at[self.rows_of(k), :], self.parts.at[k - 1], others[k])

        def back_copy(self, k):
            spot = self.target.at[0, self.rows_of(0), my_lanes]
            return self.copy(3 + k, spot, spot, others[k])

        def pair_copy(self):
            spot = self.target.at[0, :, my_lanes]
            return self.copy(7, spot, spot, sibling)

        def send(self):
            self.core_copy().start()

        def add_core(self):
            self.core_copy().wait_recv()
            value = self.given[:, my_lanes].astype(f32) + self.near[...].astype(f32)
            self.held[...] = value.astype(bf16)
            for k in (2, 1, 3):
                self.part_copy(k).start()

        def add_parts(self):
            value = self.held[self.rows_of(0), :].astype(f32)
            for k in range(1, CHIPS):
                self.part_copy(k).wait_recv()
                value = value + self.parts[k - 1].astype(f32)
            self.target[0, self.rows_of(0), my_lanes] = value.astype(bf16)
            for k in (2, 1, 3):
                self.back_copy(k).start()

        def spread(self):
            for k in range(1, CHIPS):
                spot = self.target.at[0, self.rows_of(CHIPS - k), my_lanes]
                self.copy(3 + k, spot, spot, others[k]).wait_recv()
            self.pair_copy().start()

        def take(self):
            spot = self.target.at[0, :, your_lanes]
            self.copy(7, spot, spot, sibling).wait_recv()

        def sent(self):
            self.core_copy().wait_send()
            for k in range(1, CHIPS):
                self.part_copy(k).wait_send()
                self.back_copy(k).wait_send()
            self.pair_copy().wait_send()

    down_refs, up_refs, proj_refs = (plane[5 * i : 5 * i + 5] for i in range(3))
    direct_refs = [plane[15 + 4 * i : 19 + 4 * i] for i in range(heads + 1)]
    t_down, t_up, t_proj, t_qkv, t_small = plane[19 + 4 * heads :]
    down_sum = Plane(0, down_refs, t_down)
    up_sum = Plane(1, up_refs, t_up)
    proj_sum = Plane(2, proj_refs, t_proj)
    proj_all = Plane(3, None, pg.at[1:NT])
    small_sum = Direct(4, direct_refs[heads], t_small)
    qkv_sums = [Direct(5 + h, direct_refs[h], t_qkv.at[h : h + 1]) for h in range(heads)]
    g_down, g_up, g_proj, g_small = (refs[0] for refs in (down_refs, up_refs, proj_refs, direct_refs[heads]))

    gather_start(0, xg, x_hbm)
    proj_rows = span(quarter * (hw // 4), hw // 4)

    def proj_piece(k):
        return piece_copy(8, pg.at[0, proj_rows, my_lanes], pg.at[NT - k, proj_rows, my_lanes], k)

    loads[8].wait()
    for k in range(1, NT):
        proj_piece(k).start()
    for half in range(2):
        pl.when(end == 1)(half_copy(1, cg, t, half, order[1], 0, cot_hbm).start)
    high = grids[0, 0]
    wide = grids[0, 1]
    down = lax.broadcasted_iota(i32, (seq, 1), 0)
    across = lax.broadcasted_iota(i32, (1, seq), 1)
    token_q, pad_q = query_tokens(down, high, wide)
    token_q_across, _ = query_tokens(across, high, wide)
    token_k = key_tokens(down, high, wide)
    token_k_across = key_tokens(across, high, wide)
    mq[...] = one_hot(token_q, across)
    mqt[...] = one_hot(down, token_q_across)
    mk[...] = one_hot(token_k, across)
    mkt[...] = one_hot(down, token_k_across)
    gexp[...] = jnp.zeros_like(gexp)
    tab[...] = jnp.zeros_like(tab)
    loads[3].wait()
    tab[0:heads, 0 : ENTRIES + 3] = rel[...]
    for h in range(heads):
        table = tab[h : h + 1, :]
        lined = pltpu.roll(jnp.broadcast_to(table, (24, TABLE)), TABLE - (GRID - 1), 1)
        uexp[...] = pltpu.roll(lined, 0, 1, stride=1, stride_axis=0)
        for x in range(SPAN):
            gexp[:, x * GRID : (x + 1) * GRID] = uexp[:, x * SPAN : x * SPAN + GRID]
        hankel = gexp[...]
        for r in range(GRID):
            moved = hankel if r == 0 else pltpu.roll(hankel, WIDE - r * GRID, 1)
            bias[h, r * GRID : (r + 1) * GRID, :] = moved[0:GRID, 0:seq]
        bias[h, CELLS:seq, :] = jnp.zeros((seq - CELLS, seq), f32)
        origin = bias[h, GRID - 1 : GRID, :]
        from_class = table[:, ENTRIES : ENTRIES + 1]
        to_class = table[:, ENTRIES + 1 : ENTRIES + 2]
        class_pair = table[:, ENTRIES + 2 : ENTRIES + 3]

        def settle(i, carry):
            part = pl.ds(pl.multiple_of(i * 128, 128), 128)
            place = lax.broadcasted_iota(i32, (128, 1), 0) + i * 128
            _, padded = query_tokens(place, high, wide)
            values = jnp.where(padded, origin, bias[h, part, :])
            values = jnp.where(across == CELLS, to_class, values)
            values = jnp.where(
                place == CELLS, jnp.where(across == CELLS, class_pair, from_class), values
            )
            bias[h, part, :] = jnp.where(token_k_across >= 0, values, masked)
            return carry

        lax.fori_loop(0, seq // 128, settle, 0)

    for i in (0, 4, 5, 6, 7):
        loads[i].wait()
    gain_one, shift_one = gains[0:1, :], biases[0:1, :]

    def project(s):
        normed, _ = normalize(xg[s].astype(f32))
        sent = (normed * gain_one + shift_one).astype(bf16)
        part = block(s)
        n1g[part, :] = sent
        qt[part, :] = ((dot_nt(sent, wqkv[0:hw, :]) + qvb[0:1, :]) * 0.125).astype(bf16)
        kt[part, :] = dot_nt(sent, wqkv[hw : 2 * hw, :]).astype(bf16)
        vt[part, :] = (dot_nt(sent, wqkv[2 * hw : 3 * hw, :]) + qvb[1:2, :]).astype(bf16)

    project(t)
    gather_near(0, xg)
    for half in range(2):
        pl.when(end == 0)(half_copy(1, cg, t, half, order[2], 1, cot_hbm).start)
    gather_take(0, xg, 1)
    project(order[1])
    gather_take(0, xg, 2)
    project(order[2])
    for k in range(1, NT):
        piece_arrived(8, pg.at[k, proj_rows, my_lanes], k)
    proj_all.send(3)
    gather_take(0, xg, 3)
    for half in range(2):
        pl.when(end == 0)(half_copy(1, cg, t, half, order[1], 0, cot_hbm).start)
    forward_both(1, cg, 1)
    project(order[3])
    forward_both(1, cg, 2)
    proj_all.spread_first()

    queries = dot(mq[...], qt[...]).astype(bf16)
    keys = dot(mk[...], kt[...]).astype(bf16)
    values = dot(mk[...], vt[...]).astype(bf16)
    for h in range(heads):
        lanes = slice(h * 64, (h + 1) * 64)
        qh[h] = queries[:, lanes]
        kh[h] = keys[:, lanes]
        vh[h] = values[:, lanes]
    for h in range(heads):
        logits = dot_nt(qh[h], kh[h]) + bias[h]
        raised = jnp.exp(logits - jnp.max(logits, axis=-1, keepdims=True))
        weights = raised * (1.0 / jnp.sum(raised, axis=-1, keepdims=True))
        prob[h] = weights
        rounded = weights.astype(bf16)
        probb[h] = rounded
        op[:, h * 64 : (h + 1) * 64] = dot(rounded, vh[h]).astype(bf16)
    ot[...] = dot_tn(op[...], mq[...]).astype(bf16)

    def mixed_piece(k):
        return piece_copy(2, ot.at[:, block((t + k) % NT)], og.at[NT - k], k)

    for k in (2, 1, 3):
        mixed_piece(k).start()
    forward_both(1, cg, 3)
    og[0] = ot[:, block(t)]
    total = dot_tn(og[0], pg[0])
    loads[2].wait()
    loads[12].wait()
    proj_all.spread_second()
    for k in range(1, NT):
        piece_arrived(2, og.at[k], k)
    proj_all.take(5)
    for k in range(1, NT):
        total = total + dot_tn(og[k], pg[k])
    branch_one = total + obias[0:1, :]
    a1[...] = branch_one
    after_one = xg[t].astype(f32) + scales[0:1, :] * branch_one
    x1[...] = after_one
    normed, inverse = normalize(after_one)
    xhat2[...] = normed
    inv2[...] = jnp.broadcast_to(inverse, inv2.shape)
    n2g[t] = (normed * gains[1:2, :] + biases[1:2, :]).astype(bf16)
    gather_start(3, n2g)

    for i in (9, 10, 11):
        loads[i].wait()
    shift_up = jnp.reshape(b1[...].astype(f32), (1, b1.shape[0]))

    def feed(step, half=None):
        s = order[step]
        inner = slice(None) if half is None else slice(half * half_rows, (half + 1) * half_rows)
        part = block(s) if half is None else span(s * rows + half * half_rows, half_rows)
        before = dot(n2g[s, inner, :], w1[...]) + shift_up
        cumulative = 0.5 * (1.0 + lax.erf(before * 0.7071067811865476))
        slope = cumulative + before * (jnp.exp(-0.5 * before * before) * 0.3989422804014327)
        hid[part, :] = (before * cumulative).astype(bf16)
        grad_rows = (cg[s, inner, :].astype(f32) * scales[1:2, :]).astype(bf16)
        dzg[s, inner, :] = grad_rows
        grad_pre = (dot_nt(grad_rows, w2[...]) * slope).astype(bf16)
        du[part, :] = grad_pre
        back = dot_nt(grad_pre, w1[...])
        if step == 0:
            dn2own[...] = back
        else:
            stage_b[3 - step, inner, :] = back.astype(bf16)
        return jnp.sum(grad_pre.astype(f32), axis=0, keepdims=True)

    loads[1].wait()
    bias_up = feed(0)
    gather_near(3, n2g)
    end_take(1, cg, 1)
    gather_take(3, n2g, 1)
    bias_up = bias_up + feed(1)
    scatter_copy(4, stage_b, dn2r, 2).start()
    end_take(1, cg, 2)
    for half in range(2):
        pl.when(end == 1)(lambda: half_arrived(3, n2g, 2, half))
    bias_up = bias_up + feed(2)
    for half in range(2):
        scatter_send(4, stage_b, dn2r, 1, half)
    end_take(1, cg, 3)
    for half in range(2):
        half_arrived(3, n2g, 3, half)
        pl.when(end == 0)(lambda: half_forward(3, n2g, 3, half))
    bias_up = bias_up + feed(3)
    for half in range(2):
        far_copy(4, stage_b, dn2r, half).start()
    sums[8:9, :] = bias_up
    scatter_merge(4, stage_b, dn2r, 1, 0)
    scatter_merge(4, stage_b, dn2r, 1, 1)
    down_rows = jnp.reshape(dzg[...], (seq, width))
    g_down[0] = dot_tn(hid[...], down_rows).astype(bf16)
    down_sum.send(0)
    up_rows = jnp.reshape(n2g[...], (seq, width))
    g_up[0] = dot_tn(up_rows, du[...]).astype(bf16)
    up_sum.send(0)
    shared = jnp.zeros((1, width), f32)
    for step, s in enumerate(order):
        piece = dot(hid[block(s), :], w2[...])
        shared = shared + jnp.sum(cg[s].astype(f32) * piece, axis=0, keepdims=True)
        if step == 0:
            own[...] = piece
        else:
            stage_c[3 - step] = piece.astype(bf16)
    cot = cg[t].astype(f32)
    cot_sum = jnp.sum(cot, axis=0, keepdims=True)
    sums[5:6, :] = shared + cot_sum * obias[1:2, :]
    sums[7:8, :] = cot_sum * scales[1:2, :]
    down_sum.add_core()
    up_sum.add_core()

    @pl.when(end == 1)
    def _():
        slot_wait(4, dn2r, 0, 0)
        slot_wait(4, dn2r, 0, 1)
        dn2own[...] = dn2own[...] + dn2r[0].astype(f32)

    total = scatter_total(4, dn2r, dn2own[...], (3,))
    normed = xhat2[...]
    after = cg[t].astype(f32) + norm_back(total * gains[1:2, :], normed, inv2[:, 0:1])
    dx1[...] = after
    branch = after * scales[0:1, :]
    grad_rows = branch.astype(bf16)

    def mixed_back(k):
        return piece_copy(6, doz.at[k], dot_t.at[:, block(t)], k)

    for k in (2, 1, 3, 0):
        piece = dot_nt(pg[k], grad_rows).astype(bf16)
        if k == 0:
            dot_t[:, block(t)] = piece
        else:
            doz[k] = piece
            mixed_back(k).start()
    for i in (1, 0, 2):
        scatter_send(5, stage_c, z2r, i)
    sums[3:4, :] = jnp.sum(total, axis=0, keepdims=True)
    sums[1:2, :] = jnp.sum(total * normed, axis=0, keepdims=True)
    sums[4:5, :] = jnp.sum(after * a1[...], axis=0, keepdims=True)
    sums[6:7, :] = jnp.sum(branch, axis=0, keepdims=True)
    for k in range(NT):
        g_proj[k] = dot(og[k], grad_rows).astype(bf16)
    proj_sum.send(0)
    down_sum.add_first()
    up_sum.add_first()
    proj_sum.add_core()

    for k in range(1, NT):
        piece_arrived(6, dot_t.at[:, block((t + k) % NT)], k)
    grad_mixed = dot_nt(mq[...], dot_t[...]).astype(bf16)
    for h in range(heads):
        doh[h] = grad_mixed[:, h * 64 : (h + 1) * 64]
    for h in range(heads):
        lanes = slice(h * 64, (h + 1) * 64)

        grad_prob = dot_nt(doh[h], vh[h])
        weights = prob[h]
        crossed = jnp.sum(weights * grad_prob, axis=-1, keepdims=True)
        rounded = (weights * (grad_prob - crossed)).astype(bf16)
        ds[h] = rounded
        dqp[:, lanes] = dot(rounded, kh[h]).astype(bf16) * 0.125
        dvp[:, lanes] = dot_tn(probb[h], doh[h]).astype(bf16)
        dkp[:, lanes] = dot_tn(rounded, qh[h]).astype(bf16)
        part_q = dot(mqt[...], dqp[:, lanes]).astype(bf16)
        part_k = dot(mkt[...], dkp[:, lanes]).astype(bf16)
        part_v = dot(mkt[...], dvp[:, lanes]).astype(bf16)
        dqt[:, lanes] = part_q
        dkt[:, lanes] = part_k
        dvt[:, lanes] = part_v
        for i, part in enumerate((part_q, part_k, part_v)):
            direct_refs[h][0][64 * i : 64 * (i + 1), :] = dot_tn(part, n1g[...]).astype(bf16)
        qkv_sums[h].send()
        if h == 0:
            down_sum.add_second()
            up_sum.add_second()
        elif h == 1:
            scatter_merge(5, stage_c, z2r, 1)
            qkv_sums[0].add_core()
    proj_sum.add_first()
    qkv_sums[1].add_core()

    shift_total = jnp.zeros((1, width), f32)
    gain_total = jnp.zeros((1, width), f32)
    for step in (3, 2, 1, 0):
        s = order[step]
        part = block(s)
        piece = dot(dqt[part, :], wqkv[0:hw, :]) + dot(dkt[part, :], wqkv[hw : 2 * hw, :])
        piece = piece + dot(dvt[part, :], wqkv[2 * hw : 3 * hw, :])
        if step == 0:
            dn2own[...] = piece
        else:
            stage_d[3 - step] = piece.astype(bf16)
            if step > 1:
                for half in range(2):
                    scatter_send(7, stage_d, dn1r, 3 - step, half)
        normed, _ = normalize(xg[s].astype(f32))
        shift_total = shift_total + jnp.sum(piece, axis=0, keepdims=True)
        gain_total = gain_total + jnp.sum(piece * normed, axis=0, keepdims=True)
    sums[2:3, :] = shift_total
    sums[0:1, :] = gain_total
    zmr[t] = sums[0:REP, :]

    def small_tensor(k):
        return remote(
            zmr.at[t], zmr.at[t], z_send.at[10, k], z_recv.at[10, NT - k], (dp, (t + k) % NT)
        )

    for k in range(1, NT):
        small_tensor(k).start()
    qkv_sums[2].add_core()
    scatter_merge(5, stage_c, z2r, 0)
    down_sum.spread_first()
    up_sum.spread_first()
    proj_sum.add_second(gpz)

    def proj_exchange(k):
        return piece_copy(9, gpz.at[k], gpz.at[2 * NT - k], k)

    for k in range(1, NT):
        proj_exchange(k).start()
    scatter_send(7, stage_d, dn1r, 2)
    qkv_sums[0].add_parts()

    branch_two = scatter_total(5, z2r, own[...]) + obias[1:2, :]
    outv[...] = (x1[...] + scales[1:2, :] * branch_two).astype(bf16)
    stores = [pltpu.make_async_copy(outv, out, store_sem.at[0])]
    stores[0].start()

    row24 = lax.broadcasted_iota(i32, (24, 1), 0)
    lane_t = lax.broadcasted_iota(i32, (1, TABLE), 1)
    uexp[...] = jnp.zeros_like(uexp)
    gexp[...] = jnp.zeros_like(gexp)
    for h in range(heads):
        grads = ds[h].astype(f32)
        class_row = grads[CELLS : CELLS + 1, :]
        class_column = jnp.sum(
            jnp.where((down != CELLS) & (across == CELLS), grads, 0.0), axis=0, keepdims=True
        )
        cells = jnp.where(across < CELLS, grads, 0.0)
        pad_row = jnp.sum(jnp.where(pad_q, cells, 0.0), axis=0, keepdims=True)
        dsf[...] = jnp.where(pad_q, 0.0, cells)
        blank = jnp.zeros((24, WIDE - seq), f32)
        folded = jnp.zeros((24, WIDE), f32)
        for r in range(GRID):
            cells = jnp.concatenate([dsf[r * GRID : r * GRID + 24, :], blank], axis=1)
            folded = folded + (cells if r == 0 else pltpu.roll(cells, r * GRID, 1))
        padded_row = jnp.concatenate([pad_row, jnp.zeros((1, WIDE - seq), f32)], axis=1)
        folded = jnp.where(row24 < GRID, folded, 0.0) + jnp.where(row24 == GRID - 1, padded_row, 0.0)
        for i in range(GRID):
            gexp[GRID - 1 - i : GRID - i, :] = folded[i : i + 1, :]
        for x in range(SPAN):
            uexp[:, x * SPAN : x * SPAN + GRID] = gexp[:, x * GRID : (x + 1) * GRID]
        lined = pltpu.roll(uexp[...], 0, 1, stride=1, stride_axis=0)
        table = jnp.sum(lined, axis=0, keepdims=True)
        from_class = jnp.sum(jnp.where(across != CELLS, class_row, 0.0), axis=1, keepdims=True)
        class_pair = jnp.sum(jnp.where(across == CELLS, class_row, 0.0), axis=1, keepdims=True)
        to_class = jnp.sum(class_column, axis=1, keepdims=True)
        table = jnp.where(lane_t == ENTRIES, from_class, table)
        table = jnp.where(lane_t == ENTRIES + 1, to_class, table)
        tab[h : h + 1, :] = jnp.where(lane_t == ENTRIES + 2, class_pair, table)
        if h == 1:
            scatter_merge(7, stage_d, dn1r, 0, 0)
            scatter_merge(7, stage_d, dn1r, 0, 1)
            qkv_sums[1].add_parts()
    sums[9:10, 0:hw] = jnp.sum(dqt[...].astype(f32), axis=0, keepdims=True)
    sums[10:11, 0:hw] = jnp.sum(dvt[...].astype(f32), axis=0, keepdims=True)
    sums[9:11, hw:width] = jnp.zeros((2, width - hw), f32)
    for h in range(heads):
        at = 11 + 3 * h
        sums[at : at + 1, :] = tab[h : h + 1, 0:width]
        sums[at + 1 : at + 2, :] = tab[h : h + 1, width : 2 * width]
        sums[at + 2 : at + 3, 0 : TABLE - 2 * width] = tab[h : h + 1, 2 * width : TABLE]
        sums[at + 2 : at + 3, TABLE - 2 * width : width] = jnp.zeros((1, 3 * width - TABLE), f32)
    sums[11 + 3 * heads : SMALL, :] = jnp.zeros((SMALL - 11 - 3 * heads, width), f32)

    for k in range(1, NT):
        piece_arrived(10, zmr.at[(t + k) % NT], k)
    sums[0:REP, :] = zmr[0] + zmr[1] + zmr[2] + zmr[3]
    g_small[...] = sums[...].astype(bf16)
    small_sum.send()
    qkv_sums[2].add_parts()
    small_sum.add_core()
    value = gpz[0].astype(f32)
    for k in range(1, NT):
        piece_arrived(9, gpz.at[NT + k], k)
        value = value + gpz[NT + k].astype(f32)
    t_proj[0, proj_rows, my_lanes] = value.astype(bf16)
    proj_sum.send(3)
    down_sum.spread_second()
    qkv_sums[0].spread()
    scatter_merge(7, stage_d, dn1r, 1, 0)
    scatter_merge(7, stage_d, dn1r, 1, 1)
    qkv_sums[1].spread()
    up_sum.spread_second()
    small_sum.add_parts()
    proj_sum.spread_first()
    qkv_sums[2].spread()
    sources = [(t_down.at[0], t_down_hbm), (t_up.at[0], t_up_hbm), (t_proj.at[0], t_proj_hbm), (t_small.at[0], t_small_hbm)]
    sources += [(t_qkv.at[h], t_qkv_hbm.at[192 * h : 192 * (h + 1), :]) for h in range(heads)]
    sources += [(ingradv, ingrad)]
    stores += [pltpu.make_async_copy(src, dst, store_sem.at[i + 1]) for i, (src, dst) in enumerate(sources)]
    down_sum.take(5)
    stores[1].start()
    total = scatter_total(7, dn1r, dn2own[...], (3,))
    normed, inverse = normalize(xg[t].astype(f32))
    ingradv[...] = dx1[...] + norm_back(total * gain_one, normed, inverse)
    stores[8].start()
    small_sum.spread()
    proj_sum.spread_second()
    up_sum.take(5)
    stores[2].start()
    for h in range(heads):
        qkv_sums[h].take()
        stores[5 + h].start()
    proj_sum.take(5)
    stores[3].start()
    small_sum.take()
    stores[4].start()

    gather_sent(0, xg, x_hbm)
    gather_sent(1, cg, cot_hbm)
    gather_sent(3, n2g)
    for i in range(NT - 1):
        scatter_copy(5, stage_c, z2r, i).wait_send()
    scatter_copy(4, stage_b, dn2r, 2).wait_send()
    scatter_copy(7, stage_d, dn1r, 2).wait_send()
    for half in range(2):
        far_copy(4, stage_b, dn2r, half).wait_send()
        scatter_copy(4, stage_b, dn2r, 1, half).wait_send()
        scatter_copy(7, stage_d, dn1r, 0, half).wait_send()
        scatter_copy(7, stage_d, dn1r, 1, half).wait_send()
    for k in range(1, NT):
        proj_piece(k).wait_send()
        mixed_piece(k).wait_send()
        mixed_back(k).wait_send()
        proj_exchange(k).wait_send()
        small_tensor(k).wait_send()
    for part_sum in (down_sum, up_sum, proj_sum, small_sum, *qkv_sums):
        part_sum.sent()
    proj_all.sent(3)
    for store in stores:
        store.wait()


def finish_kernel(
    down_in, up_in, proj_in, qkv_in, small_in, out_in, ingrad_in,
    out, ingrad, g_qkv, g_qv, g_table, g_proj, g_up, g_up_bias, g_down, g_gains, g_shifts, g_scales, g_biases,
    down_v, up_v, proj_v, qkv_v, down_f, up_f, proj_f, qkv_f, small_v, out_v, ingrad_v, load_sem, store_sem,
):
    width = g_down.shape[1]
    hw = g_proj.shape[0]
    heads, entries = g_table.shape
    parts = []
    for given, rounded, widened, result in (
        (down_in, down_v, down_f, g_down), (up_in, up_v, up_f, g_up),
        (qkv_in, qkv_v, qkv_f, g_qkv), (proj_in, proj_v, proj_f, g_proj),
    ):
        for start in range(0, given.shape[0], PIECE):
            piece = [ref.at[start : start + PIECE, :] for ref in (given, rounded, widened, result)]
            parts.append(piece + [given is qkv_in])
    moved = [(small_in, small_v, None), (out_in, out_v, out), (ingrad_in, ingrad_v, ingrad)]
    count = len(parts)
    loads = [pltpu.make_async_copy(part[0], part[1], load_sem.at[i]) for i, part in enumerate(parts)]
    loads += [pltpu.make_async_copy(src, via, load_sem.at[count + i]) for i, (src, via, _) in enumerate(moved)]
    for copy in loads:
        copy.start()
    stores = []
    by_head = [i for i, part in enumerate(parts) if part[4]]
    for i, (_, rounded, widened, result, mixed) in enumerate(parts):
        if mixed:
            which = i - by_head[0]
            for h, j in enumerate(by_head):
                if which == 0:
                    loads[j].wait()
                widened[64 * h : 64 * (h + 1), :] = parts[j][1][64 * which : 64 * (which + 1), :].astype(f32)
        else:
            loads[i].wait()
            widened[...] = rounded[...].astype(f32)
        stores.append(pltpu.make_async_copy(widened, result, store_sem.at[i]))
        stores[-1].start()
    for i, (_, via, dst) in enumerate(moved):
        loads[count + i].wait()
        if dst is not None:
            stores.append(pltpu.make_async_copy(via, dst, store_sem.at[count + i]))
            stores[-1].start()
    small = small_v[...].astype(f32)
    g_gains[...] = small[0:2, :]
    g_shifts[...] = small[2:4, :]
    g_scales[...] = small[4:6, :]
    g_biases[...] = small[6:8, :]
    g_up_bias[...] = jnp.reshape(small[8:9, :], (width,))
    g_qv[...] = small[9:11, 0:hw]
    for h in range(heads):
        for j in range(3):
            lanes = min(width, entries - j * width)
            g_table[h : h + 1, j * width : j * width + lanes] = small[
                11 + 3 * h + j : 12 + 3 * h + j, 0:lanes
            ]
    for copy in stores:
        copy.wait()


def per_device(
    n_dp, tokens, grids, qkv_weight, qv_bias, rel_table, proj_weight, fc1_weight, fc1_bias, fc2_weight,
    norm_gains, norm_biases, layer_scales, out_biases, cotangent,
):
    rows, width = tokens.shape
    seq = rows * NT
    heads, entries = rel_table.shape
    hw = heads * 64
    ff = fc1_weight.shape[1]
    qkv_rows = jnp.transpose(qkv_weight, (1, 2, 0)).reshape(3 * hw, width)
    vm = pl.BlockSpec(memory_space=pltpu.VMEM)
    anywhere = pl.BlockSpec(memory_space=pl.ANY)

    def many(count, shape, dtype):
        return [pltpu.VMEM(shape, dtype)] * count

    def sems(*shape):
        return [pltpu.SemaphoreType.DMA(shape)]

    half = width // 2
    scratch = [
        pltpu.VMEM((rows, width), bf16), pltpu.VMEM((rows, width), f32), pltpu.VMEM((3 * hw, width), bf16),
        pltpu.VMEM((width, ff), bf16), pltpu.VMEM((ff, width), bf16),
        pltpu.VMEM((2, hw), f32), pltpu.VMEM((heads, entries), f32), pltpu.VMEM((ff,), bf16),
    ]
    scratch += many(4, (2, width), f32) + sems(13) + sems(9)
    scratch += many(4, (NT, rows, width), bf16)
    scratch += many(1, (NT, hw, rows), bf16) + many(1, (NT, hw, width), bf16)
    scratch += many(3, (NT, rows, width), bf16) + many(3, (NT - 1, rows, width), bf16)
    scratch += many(1, (NT, hw, rows), bf16) + sems(11, 2 * NT) + sems(11, 2 * NT) + sems(4, 5, 2)
    scratch += many(4, (seq, seq), bf16)
    scratch += many(1, (heads, seq, seq), f32) + many(1, (24, WIDE), f32) + many(1, (24, TABLE), f32)
    scratch += many(1, (seq, width), bf16) + many(3, (seq, hw), bf16)
    scratch += many(3, (heads, seq, 64), bf16)
    scratch += many(1, (heads, seq, seq), f32) + many(1, (heads, seq, seq), bf16)
    scratch += many(1, (seq, hw), bf16) + many(1, (hw, seq), bf16)
    scratch += many(2, (rows, width), f32) + many(1, (rows, 128), f32) + many(4, (rows, width), f32)
    scratch += many(2, (seq, ff), bf16) + many(1, (hw, seq), bf16) + many(1, (heads, seq, 64), bf16)
    scratch += many(1, (heads, seq, seq), bf16) + many(1, (seq, seq), f32) + many(6, (seq, hw), bf16)
    scratch += many(1, (8, TABLE), f32) + many(1, (SMALL, width), f32) + many(1, (NT, REP, width), f32)
    scratch += many(1, (2 * NT, hw // 4, half), bf16) + sems(5 + heads, 8) + sems(5 + heads, 8)
    for lead, count in ((1, ff), (1, width), (NT, hw)):
        scratch += [
            pltpu.VMEM((lead, count, width), bf16), pltpu.VMEM((lead, count, half), bf16),
            pltpu.VMEM((lead, count, half), bf16), pltpu.VMEM((lead, count // 2, half), bf16),
            pltpu.VMEM((lead, count // 4, half), bf16),
        ]
    for count in (192,) * heads + (SMALL,):
        scratch += [
            pltpu.VMEM((count, width), bf16), pltpu.VMEM((count, half), bf16), pltpu.VMEM((count, half), bf16),
            pltpu.VMEM((CHIPS - 1, count // CHIPS, half), bf16),
        ]
    for lead, count in ((1, ff), (1, width), (1, hw), (heads, 192), (1, SMALL)):
        scratch += many(1, (lead, count, width), bf16)
    flat = [jax.ShapeDtypeStruct((count, width), bf16) for count in (ff, width, hw, 3 * hw, SMALL)]
    output, input_grad, *totals = pl.pallas_call(
        main_kernel,
        out_shape=[
            jax.ShapeDtypeStruct((rows, width), bf16),
            jax.ShapeDtypeStruct((rows, width), f32),
        ]
        + flat,
        in_specs=[pl.BlockSpec(memory_space=pltpu.SMEM)] + [anywhere] * 13,
        out_specs=[anywhere] * 7,
        scratch_shapes=scratch,
        compiler_params=pltpu.CompilerParams(
            collective_id=0, has_side_effects=True, vmem_limit_bytes=60 << 20
        ),
        name="layer",
    )(
        grids, tokens, cotangent, qkv_rows, proj_weight, fc1_weight, fc2_weight,
        qv_bias, rel_table, fc1_bias, norm_gains, norm_biases, layer_scales, out_biases,
    )
    pair = jax.ShapeDtypeStruct((2, width), f32)
    pieces = sum(-(-count // PIECE) for count in (ff, width, hw, 3 * hw))
    results = pl.pallas_call(
        finish_kernel,
        out_shape=(
            jax.ShapeDtypeStruct((rows, width), bf16),
            jax.ShapeDtypeStruct((rows, width), f32),
            jax.ShapeDtypeStruct((3 * hw, width), f32),
            jax.ShapeDtypeStruct((2, hw), f32),
            jax.ShapeDtypeStruct((heads, entries), f32),
            jax.ShapeDtypeStruct((hw, width), f32),
            jax.ShapeDtypeStruct((width, ff), f32),
            jax.ShapeDtypeStruct((ff,), f32),
            jax.ShapeDtypeStruct((ff, width), f32),
            pair, pair, pair, pair,
        ),
        in_specs=[anywhere] * 7,
        out_specs=(
            anywhere, anywhere, anywhere, vm, vm, anywhere, anywhere, vm, anywhere, vm, vm, vm, vm,
        ),
        scratch_shapes=[
            pltpu.VMEM((ff, width), bf16), pltpu.VMEM((width, ff), bf16), pltpu.VMEM((hw, width), bf16),
            pltpu.VMEM((3 * hw, width), bf16),
            pltpu.VMEM((ff, width), f32), pltpu.VMEM((width, ff), f32), pltpu.VMEM((hw, width), f32),
            pltpu.VMEM((3 * hw, width), f32), pltpu.VMEM((SMALL, width), bf16),
            pltpu.VMEM((rows, width), bf16), pltpu.VMEM((rows, width), f32),
            *sems(pieces + 3), *sems(pieces + 3),
        ],
        compiler_params=pltpu.CompilerParams(vmem_limit_bytes=60 << 20),
        name="finish",
    )(*totals, output, input_grad)
    results = list(results)
    stride = GROUP
    while stride < n_dp:
        hops = [(i, i ^ stride) for i in range(n_dp)]
        results[2:] = [value + lax.ppermute(value, "dp", hops) for value in results[2:]]
        stride *= 2
    results[2] = jnp.transpose(results[2].reshape(3, hw, width), (2, 0, 1))
    return tuple(results)


def solution(mesh):
    n_dp = mesh.shape["dp"]
    blocks = P(("dp", "tensor"), None)
    placed = (
        blocks, P("dp", None), P(None, None, "tensor"), P(None, "tensor"), P("tensor", None), P("tensor", None),
        P(None, "tensor"), P("tensor"), P("tensor", None), P(), P(), P(), P(), blocks,
    )
    given = (
        blocks, blocks, P(None, None, "tensor"), P(None, "tensor"), P("tensor", None), P("tensor", None),
        P(None, "tensor"), P("tensor"), P("tensor", None), P(), P(), P(), P(),
    )

    def layer(*arrays):
        return per_device(n_dp, *arrays)

    return jax.shard_map(layer, mesh=mesh, in_specs=placed, out_specs=given, check_vma=False)
```

```python
import jax
import jax.numpy as jnp
from jax import lax
from jax.experimental import pallas as pl
from jax.experimental.pallas import tpu as pltpu
from jax.sharding import PartitionSpec as P

GRID = 22
SPAN = 2 * GRID - 1
CELLS = GRID * GRID
ENTRIES = SPAN * SPAN
MESH = pl.DeviceIdType.MESH
f32 = jnp.float32
bf16 = jnp.bfloat16
i32 = jnp.int32

eps_norm = 1e-06
masked = -1e30
NT = 4
CHIPS = 4
CORES = 2
GROUP = CHIPS * CORES
TABLE = 1920
WIDE = 1024
SMALL = 64
REP = 8
PIECE = 192


def dot(left, right):
    return lax.dot_general(left, right, (((1,), (0,)), ((), ())), preferred_element_type=f32)


def dot_nt(left, right):
    return lax.dot_general(left, right, (((1,), (1,)), ((), ())), preferred_element_type=f32)


def dot_tn(left, right):
    return lax.dot_general(left, right, (((0,), (0,)), ((), ())), preferred_element_type=f32)


def normalize(values):
    center = values - jnp.mean(values, axis=-1, keepdims=True)
    inverse = lax.rsqrt(jnp.mean(center * center, axis=-1, keepdims=True) + eps_norm)
    return center * inverse, inverse


def norm_back(grad_normed, normed, inverse):
    average = jnp.mean(grad_normed, axis=-1, keepdims=True)
    crossed = jnp.mean(grad_normed * normed, axis=-1, keepdims=True)
    return inverse * (grad_normed - average - normed * crossed)


def split_cell(place):
    row = (place * 2979) >> 16
    return row, place - row * GRID


def query_tokens(place, high, wide):
    row, back = split_cell(place)
    inside = (place < CELLS) & (row < high) & (GRID - 1 - back < wide)
    before = jnp.minimum(row, high) * wide + jnp.where(
        row < high, jnp.maximum(back - (GRID - wide), 0), 0
    )
    token = jnp.where(inside, 1 + row * wide + (GRID - 1 - back), high * wide + 1 + place - before)
    token = jnp.where(place == CELLS, 0, jnp.where(place > CELLS, place, token))
    padding = jnp.logical_not(inside) & (place != CELLS)
    return token, padding


def key_tokens(place, high, wide):
    row, back = split_cell(place)
    row = GRID - 1 - row
    column = GRID - 1 - back
    inside = (place < CELLS) & (row < high) & (column < wide)
    token = jnp.where(inside, 1 + row * wide + column, -1)
    return jnp.where(place == CELLS, 0, token)


def one_hot(left, right):
    return jnp.where(left == right, 1.0, 0.0).astype(bf16)


def main_kernel(
    grids, x_hbm, cot_hbm, wqkv_hbm, wproj_hbm, w1_hbm, w2_hbm, qvb_hbm, rel_hbm, b1_hbm,
    gains_hbm, biases_hbm, scales_hbm, obias_hbm,
    out, ingrad, t_down_hbm, t_up_hbm, t_proj_hbm, t_qkv_hbm, t_small_hbm,
    outv, ingradv, wqkv, w1, w2, qvb, rel, b1, gains, biases, scales, obias, load_sem, store_sem,
    xg, cg, dzg, n2g, og, pg, dn2r, z2r, dn1r, stage_b, stage_c, stage_d, doz, z_send, z_recv, z_half,
    mq, mqt, mk, mkt, bias, gexp, uexp,
    n1g, qt, kt, vt, qh, kh, vh, prob, probb, op, ot,
    x1, xhat2, inv2, a1, dx1, own, dn2own,
    hid, du, dot_t, doh, ds, dsf, dqp, dkp, dvp, dqt, dkt, dvt,
    tab, sums, zmr, gpz, p_send, p_recv,
    *plane,
):
    dp = lax.axis_index("dp")
    t = lax.axis_index("tensor")
    rows, width = x_hbm.shape
    seq = rows * NT
    heads = rel.shape[0]
    hw = heads * 64
    base = (dp // GROUP) * GROUP
    mine = dp % GROUP
    core = mine % CORES
    chip_x = (mine // 2) % 2
    chip_y = mine // 4
    to_x = 2 - 4 * chip_x
    to_y = 4 - 8 * chip_y
    sibling = base + mine + 1 - 2 * core
    first_peer = base + mine + (1 - core) * to_x + core * to_y
    second_peer = base + mine + core * to_x + (1 - core) * to_y
    bit_one = (1 - core) * chip_x + core * chip_y
    bit_two = core * chip_x + (1 - core) * chip_y
    quarter = bit_one * 2 + bit_two
    end = ((t - 1) * (t - 2)) // 2
    order = [t, t + 1 - 2 * (t % 2), 2 - t // 2, 3 - 3 * (t // 2)]

    pairs = [
        (x_hbm, xg.at[t]), (cot_hbm, cg.at[t]), (scales_hbm, scales), (rel_hbm, rel), (wqkv_hbm, wqkv),
        (gains_hbm, gains), (biases_hbm, biases), (qvb_hbm, qvb), (wproj_hbm, pg.at[0]), (w1_hbm, w1),
        (w2_hbm, w2), (b1_hbm, b1), (obias_hbm, obias),
    ]
    loads = [pltpu.make_async_copy(src, dst, load_sem.at[i]) for i, (src, dst) in enumerate(pairs)]
    for load in loads:
        load.start()
    barrier = pltpu.get_barrier_semaphore()
    for k in range(1, NT):
        pl.semaphore_signal(barrier, inc=1, device_id=(dp, (t + k) % NT), device_id_type=MESH)
    chip = mine // CORES
    others = [base + ((chip + k) % CHIPS) * CORES + core for k in range(CHIPS)]
    for peer in (sibling, *others[1:]):
        pl.semaphore_signal(barrier, inc=1, device_id=(peer, t), device_id_type=MESH)
    pl.semaphore_wait(barrier, NT - 1 + CHIPS)

    def block(s):
        return pl.ds(pl.multiple_of(s * rows, rows), rows)

    def remote(src, dst, send, recv, device):
        return pltpu.make_async_remote_copy(
            src_ref=src, dst_ref=dst, send_sem=send, recv_sem=recv, device_id=device, device_id_type=MESH
        )

    half_rows = rows // 2

    def half_copy(phase, buf, src, half, dst, way, given=None):
        spot = buf.at[src, half * half_rows : (half + 1) * half_rows, :]
        if given is not None:
            given = given.at[half * half_rows : (half + 1) * half_rows, :]
        return remote(
            spot if given is None else given, spot,
            z_half.at[phase, way, half], z_recv.at[phase, src * 2 + half], (dp, dst),
        )

    def gather_start(phase, buf, given=None):
        for half in range(2):
            half_copy(phase, buf, t, half, order[1], 0, given).start()
            pl.when(end == 0)(half_copy(phase, buf, t, half, order[2], 1, given).start)

    def half_arrived(phase, buf, step, half):
        half_copy(phase, buf, order[step], half, order[1], 0).wait_recv()

    def half_forward(phase, buf, step, half):
        to = order[2] if step == 1 else order[1]
        half_copy(phase, buf, order[step], half, to, 1 + step).start()

    def gather_near(phase, buf):
        @pl.when(end == 0)
        def _():
            for half in range(2):
                for step in (1, 2):
                    half_arrived(phase, buf, step, half)
                    half_forward(phase, buf, step, half)

    def forward_both(phase, buf, step):
        @pl.when(end == 0)
        def _():
            for half in range(2):
                half_arrived(phase, buf, step, half)
                half_forward(phase, buf, step, half)

    def end_take(phase, buf, step):
        for half in range(2):
            pl.when(end == 1)(lambda: half_arrived(phase, buf, step, half))

    def gather_take(phase, buf, step):
        for half in range(2):
            if step < 3:
                pl.when(end == 1)(lambda: half_arrived(phase, buf, step, half))
            else:
                half_arrived(phase, buf, step, half)
                pl.when(end == 0)(lambda: half_forward(phase, buf, step, half))

    def gather_sent(phase, buf, given=None):
        for half in range(2):
            half_copy(phase, buf, t, half, order[1], 0, given).wait_send()

            @pl.when(end == 0)
            def _():
                half_copy(phase, buf, t, half, order[2], 1, given).wait_send()
                for step in (1, 2, 3):
                    half_copy(phase, buf, order[step], half, order[1], 1 + step).wait_send()

    def scatter_part(phase, stage, buf, i, dst, slot, half):
        if half is None:
            return remote(
                stage.at[i], buf.at[slot], z_send.at[phase, i], z_recv.at[phase, slot], (dp, dst)
            )
        part = slice(half * half_rows, (half + 1) * half_rows)
        return remote(
            stage.at[i, part, :], buf.at[slot, part, :],
            z_send.at[phase, i + NT * half], z_recv.at[phase, slot + NT * half], (dp, dst),
        )

    def scatter_copy(phase, stage, buf, i, half=None):
        if i == 2:
            dst, slot = order[1], 2
        else:
            dst = end * order[1] + (1 - end) * order[3 - i]
            slot = end * i + (1 - end) * 3
        return scatter_part(phase, stage, buf, i, dst, slot, half)

    def far_copy(phase, stage, buf, half):
        return scatter_part(phase, stage, buf, 0, order[3], (1 - end) * 3, half)

    def slot_wait(phase, buf, slot, half=None):
        scatter_part(phase, buf, buf, slot, order[1], slot, half).wait_recv()

    def scatter_send(phase, stage, buf, i, half=None):
        if i == 2:
            scatter_copy(phase, stage, buf, i, half).start()
        else:
            pl.when(end == 1)(scatter_copy(phase, stage, buf, i, half).start)

    def scatter_merge(phase, stage, buf, i, half=None):
        part = slice(None) if half is None else slice(half * half_rows, (half + 1) * half_rows)

        @pl.when(end == 0)
        def _():
            slot_wait(phase, buf, i, half)
            stage[i, part, :] = (stage[i, part, :].astype(f32) + buf[i, part, :].astype(f32)).astype(bf16)
            scatter_copy(phase, stage, buf, i, half).start()

    def scatter_total(phase, buf, total, halves=()):
        for slot in (2, 3):
            if slot in halves:
                slot_wait(phase, buf, slot, 0)
                slot_wait(phase, buf, slot, 1)
            else:
                slot_wait(phase, buf, slot)
            total = total + buf[slot].astype(f32)
        return total

    def piece_copy(phase, src, dst, k):
        return remote(
            src, dst, z_send.at[phase, k], z_recv.at[phase, NT - k], (dp, (t + k) % NT)
        )

    def piece_arrived(phase, dst, k):
        remote(dst, dst, z_send.at[phase, k], z_recv.at[phase, k], (dp, (t + k) % NT)).wait_recv()

    half_width = width // 2
    my_lanes = pl.ds(pl.multiple_of(core * half_width, half_width), half_width)
    your_lanes = pl.ds(pl.multiple_of((1 - core) * half_width, half_width), half_width)

    def span(start, count):
        return pl.ds(pl.multiple_of(start, 16), count)

    class Plane:
        def __init__(self, index, refs, target):
            self.index, self.target = index, target
            self.count = target.shape[1]
            self.fours = self.count // 4
            if refs is not None:
                self.given, self.near, self.held, self.one, self.two = refs
                self.lead = self.given.shape[0]

        def copy(self, step, src, dst, peer):
            return remote(
                src, dst, p_send.at[self.index, step], p_recv.at[self.index, step], (peer, t)
            )

        def outgoing(self, step):
            c, f = self.count, self.fours
            if step == 0:
                return self.copy(0, self.given.at[:, :, your_lanes], self.near, sibling)
            if step == 1:
                src = self.held.at[:, span((1 - bit_one) * 2 * f, 2 * f), :]
                return self.copy(1, src, self.one, first_peer)
            if step == 2:
                src = self.held.at[:, span((bit_one * 2 + 1 - bit_two) * f, f), :]
                return self.copy(2, src, self.two, second_peer)
            if step == 3:
                spot, peer = self.target.at[:, span(quarter * f, f), my_lanes], second_peer
            elif step == 4:
                spot, peer = self.target.at[:, span(bit_one * 2 * f, 2 * f), my_lanes], first_peer
            else:
                spot, peer = self.target.at[:, :, my_lanes], sibling
            return self.copy(step, spot, spot, peer)

        def incoming(self, step):
            f = self.fours
            if step < 3:
                return self.outgoing(step)
            if step == 3:
                spot = self.target.at[:, span((bit_one * 2 + 1 - bit_two) * f, f), my_lanes]
            elif step == 4:
                spot = self.target.at[:, span((1 - bit_one) * 2 * f, 2 * f), my_lanes]
            else:
                spot = self.target.at[:, :, your_lanes]
            return self.copy(step, spot, spot, sibling)

        def send(self, step):
            self.outgoing(step).start()

        def take(self, step):
            self.incoming(step).wait_recv()

        def add_core(self):
            self.take(0)
            for q in range(self.lead):
                value = self.given[q, :, my_lanes].astype(f32) + self.near[q].astype(f32)
                self.held[q] = value.astype(bf16)
            self.send(1)

        def add_first(self):
            self.take(1)
            part = span(bit_one * 2 * self.fours, 2 * self.fours)
            for q in range(self.lead):
                value = self.held[q, part, :].astype(f32) + self.one[q].astype(f32)
                self.held[q, part, :] = value.astype(bf16)
            self.send(2)

        def add_second(self, store=None):
            self.take(2)
            part = span(quarter * self.fours, self.fours)
            for q in range(self.lead):
                value = (self.held[q, part, :].astype(f32) + self.two[q].astype(f32)).astype(bf16)
                if store is None:
                    self.target[q, part, my_lanes] = value
                else:
                    store[q] = value
            if store is None:
                self.send(3)

        def spread_first(self):
            self.take(3)
            self.send(4)

        def spread_second(self):
            self.take(4)
            self.send(5)

        def sent(self, first=0):
            for step in range(first, 6):
                self.outgoing(step).wait_send()

    class Direct:
        def __init__(self, index, refs, target):
            self.index, self.target = index, target
            self.fours = target.shape[1] // CHIPS
            self.given, self.near, self.held, self.parts = refs

        def copy(self, step, src, dst, peer):
            return remote(
                src, dst, p_send.at[self.index, step], p_recv.at[self.index, step], (peer, t)
            )

        def rows_of(self, k):
            return span(((chip + k) % CHIPS) * self.fours, self.fours)

        def core_copy(self):
            return self.copy(0, self.given.at[:, your_lanes], self.near, sibling)

        def part_copy(self, k):
            return self.copy(k, self.held.at[self.rows_of(k), :], self.parts.at[k - 1], others[k])

        def back_copy(self, k):
            spot = self.target.at[0, self.rows_of(0), my_lanes]
            return self.copy(3 + k, spot, spot, others[k])

        def pair_copy(self):
            spot = self.target.at[0, :, my_lanes]
            return self.copy(7, spot, spot, sibling)

        def send(self):
            self.core_copy().start()

        def add_core(self):
            self.core_copy().wait_recv()
            value = self.given[:, my_lanes].astype(f32) + self.near[...].astype(f32)
            self.held[...] = value.astype(bf16)
            for k in (2, 1, 3):
                self.part_copy(k).start()

        def add_parts(self):
            value = self.held[self.rows_of(0), :].astype(f32)
            for k in range(1, CHIPS):
                self.part_copy(k).wait_recv()
                value = value + self.parts[k - 1].astype(f32)
            self.target[0, self.rows_of(0), my_lanes] = value.astype(bf16)
            for k in (2, 1, 3):
                self.back_copy(k).start()

        def spread(self):
            for k in range(1, CHIPS):
                spot = self.target.at[0, self.rows_of(CHIPS - k), my_lanes]
                self.copy(3 + k, spot, spot, others[k]).wait_recv()
            self.pair_copy().start()

        def take(self):
            spot = self.target.at[0, :, your_lanes]
            self.copy(7, spot, spot, sibling).wait_recv()

        def sent(self):
            self.core_copy().wait_send()
            for k in range(1, CHIPS):
                self.part_copy(k).wait_send()
                self.back_copy(k).wait_send()
            self.pair_copy().wait_send()

    down_refs, up_refs, proj_refs = (plane[5 * i : 5 * i + 5] for i in range(3))
    direct_refs = [plane[15 + 4 * i : 19 + 4 * i] for i in range(heads + 1)]
    t_down, t_up, t_proj, t_qkv, t_small = plane[19 + 4 * heads :]
    down_sum = Plane(0, down_refs, t_down)
    up_sum = Plane(1, up_refs, t_up)
    proj_sum = Plane(2, proj_refs, t_proj)
    proj_all = Plane(3, None, pg.at[1:NT])
    small_sum = Direct(4, direct_refs[heads], t_small)
    qkv_sums = [Direct(5 + h, direct_refs[h], t_qkv.at[h : h + 1]) for h in range(heads)]
    g_down, g_up, g_proj, g_small = (refs[0] for refs in (down_refs, up_refs, proj_refs, direct_refs[heads]))

    gather_start(0, xg, x_hbm)
    proj_rows = span(quarter * (hw // 4), hw // 4)

    def proj_piece(k):
        return piece_copy(8, pg.at[0, proj_rows, my_lanes], pg.at[NT - k, proj_rows, my_lanes], k)

    loads[8].wait()
    for k in range(1, NT):
        proj_piece(k).start()
    for half in range(2):
        pl.when(end == 1)(half_copy(1, cg, t, half, order[1], 0, cot_hbm).start)
    high = grids[0, 0]
    wide = grids[0, 1]
    down = lax.broadcasted_iota(i32, (seq, 1), 0)
    across = lax.broadcasted_iota(i32, (1, seq), 1)
    token_q, pad_q = query_tokens(down, high, wide)
    token_q_across, _ = query_tokens(across, high, wide)
    token_k = key_tokens(down, high, wide)
    token_k_across = key_tokens(across, high, wide)
    mq[...] = one_hot(token_q, across)
    mqt[...] = one_hot(down, token_q_across)
    mk[...] = one_hot(token_k, across)
    mkt[...] = one_hot(down, token_k_across)
    gexp[...] = jnp.zeros_like(gexp)
    tab[...] = jnp.zeros_like(tab)
    loads[3].wait()
    tab[0:heads, 0 : ENTRIES + 3] = rel[...]
    for h in range(heads):
        table = tab[h : h + 1, :]
        lined = pltpu.roll(jnp.broadcast_to(table, (24, TABLE)), TABLE - (GRID - 1), 1)
        uexp[...] = pltpu.roll(lined, 0, 1, stride=1, stride_axis=0)
        for x in range(SPAN):
            gexp[:, x * GRID : (x + 1) * GRID] = uexp[:, x * SPAN : x * SPAN + GRID]
        hankel = gexp[...]
        for r in range(GRID):
            moved = hankel if r == 0 else pltpu.roll(hankel, WIDE - r * GRID, 1)
            bias[h, r * GRID : (r + 1) * GRID, :] = moved[0:GRID, 0:seq]
        bias[h, CELLS:seq, :] = jnp.zeros((seq - CELLS, seq), f32)
        origin = bias[h, GRID - 1 : GRID, :]
        from_class = table[:, ENTRIES : ENTRIES + 1]
        to_class = table[:, ENTRIES + 1 : ENTRIES + 2]
        class_pair = table[:, ENTRIES + 2 : ENTRIES + 3]

        def settle(i, carry):
            part = pl.ds(pl.multiple_of(i * 128, 128), 128)
            place = lax.broadcasted_iota(i32, (128, 1), 0) + i * 128
            _, padded = query_tokens(place, high, wide)
            values = jnp.where(padded, origin, bias[h, part, :])
            values = jnp.where(across == CELLS, to_class, values)
            values = jnp.where(
                place == CELLS, jnp.where(across == CELLS, class_pair, from_class), values
            )
            bias[h, part, :] = jnp.where(token_k_across >= 0, values, masked)
            return carry

        lax.fori_loop(0, seq // 128, settle, 0)

    for i in (0, 4, 5, 6, 7):
        loads[i].wait()
    gain_one, shift_one = gains[0:1, :], biases[0:1, :]

    def project(s):
        normed, _ = normalize(xg[s].astype(f32))
        sent = (normed * gain_one + shift_one).astype(bf16)
        part = block(s)
        n1g[part, :] = sent
        qt[part, :] = ((dot_nt(sent, wqkv[0:hw, :]) + qvb[0:1, :]) * 0.125).astype(bf16)
        kt[part, :] = dot_nt(sent, wqkv[hw : 2 * hw, :]).astype(bf16)
        vt[part, :] = (dot_nt(sent, wqkv[2 * hw : 3 * hw, :]) + qvb[1:2, :]).astype(bf16)

    project(t)
    gather_near(0, xg)
    for half in range(2):
        pl.when(end == 0)(half_copy(1, cg, t, half, order[2], 1, cot_hbm).start)
    gather_take(0, xg, 1)
    project(order[1])
    gather_take(0, xg, 2)
    project(order[2])
    for k in range(1, NT):
        piece_arrived(8, pg.at[k, proj_rows, my_lanes], k)
    proj_all.send(3)
    gather_take(0, xg, 3)
    for half in range(2):
        pl.when(end == 0)(half_copy(1, cg, t, half, order[1], 0, cot_hbm).start)
    forward_both(1, cg, 1)
    project(order[3])
    forward_both(1, cg, 2)
    proj_all.spread_first()

    queries = dot(mq[...], qt[...]).astype(bf16)
    keys = dot(mk[...], kt[...]).astype(bf16)
    values = dot(mk[...], vt[...]).astype(bf16)
    for h in range(heads):
        lanes = slice(h * 64, (h + 1) * 64)
        qh[h] = queries[:, lanes]
        kh[h] = keys[:, lanes]
        vh[h] = values[:, lanes]
    for h in range(heads):
        logits = dot_nt(qh[h], kh[h]) + bias[h]
        raised = jnp.exp(logits - jnp.max(logits, axis=-1, keepdims=True))
        weights = raised * (1.0 / jnp.sum(raised, axis=-1, keepdims=True))
        prob[h] = weights
        rounded = weights.astype(bf16)
        probb[h] = rounded
        op[:, h * 64 : (h + 1) * 64] = dot(rounded, vh[h]).astype(bf16)
    ot[...] = dot_tn(op[...], mq[...]).astype(bf16)

    def mixed_piece(k):
        return piece_copy(2, ot.at[:, block((t + k) % NT)], og.at[NT - k], k)

    for k in (2, 1, 3):
        mixed_piece(k).start()
    forward_both(1, cg, 3)
    og[0] = ot[:, block(t)]
    total = dot_tn(og[0], pg[0])
    loads[2].wait()
    loads[12].wait()
    proj_all.spread_second()
    for k in range(1, NT):
        piece_arrived(2, og.at[k], k)
    proj_all.take(5)
    for k in range(1, NT):
        total = total + dot_tn(og[k], pg[k])
    branch_one = total + obias[0:1, :]
    a1[...] = branch_one
    after_one = xg[t].astype(f32) + scales[0:1, :] * branch_one
    x1[...] = after_one
    normed, inverse = normalize(after_one)
    xhat2[...] = normed
    inv2[...] = jnp.broadcast_to(inverse, inv2.shape)
    n2g[t] = (normed * gains[1:2, :] + biases[1:2, :]).astype(bf16)
    gather_start(3, n2g)

    for i in (9, 10, 11):
        loads[i].wait()
    shift_up = jnp.reshape(b1[...].astype(f32), (1, b1.shape[0]))

    def feed(step, half=None):
        s = order[step]
        inner = slice(None) if half is None else slice(half * half_rows, (half + 1) * half_rows)
        part = block(s) if half is None else span(s * rows + half * half_rows, half_rows)
        before = dot(n2g[s, inner, :], w1[...]) + shift_up
        cumulative = 0.5 * (1.0 + lax.erf(before * 0.7071067811865476))
        slope = cumulative + before * (jnp.exp(-0.5 * before * before) * 0.3989422804014327)
        hid[part, :] = (before * cumulative).astype(bf16)
        grad_rows = (cg[s, inner, :].astype(f32) * scales[1:2, :]).astype(bf16)
        dzg[s, inner, :] = grad_rows
        grad_pre = (dot_nt(grad_rows, w2[...]) * slope).astype(bf16)
        du[part, :] = grad_pre
        back = dot_nt(grad_pre, w1[...])
        if step == 0:
            dn2own[...] = back
        else:
            stage_b[3 - step, inner, :] = back.astype(bf16)
        return jnp.sum(grad_pre.astype(f32), axis=0, keepdims=True)

    loads[1].wait()
    bias_up = feed(0)
    gather_near(3, n2g)
    end_take(1, cg, 1)
    gather_take(3, n2g, 1)
    bias_up = bias_up + feed(1)
    scatter_copy(4, stage_b, dn2r, 2).start()
    end_take(1, cg, 2)
    for half in range(2):
        pl.when(end == 1)(lambda: half_arrived(3, n2g, 2, half))
    bias_up = bias_up + feed(2)
    for half in range(2):
        scatter_send(4, stage_b, dn2r, 1, half)
    end_take(1, cg, 3)
    for half in range(2):
        half_arrived(3, n2g, 3, half)
        pl.when(end == 0)(lambda: half_forward(3, n2g, 3, half))
    bias_up = bias_up + feed(3)
    for half in range(2):
        far_copy(4, stage_b, dn2r, half).start()
    sums[8:9, :] = bias_up
    scatter_merge(4, stage_b, dn2r, 1, 0)
    scatter_merge(4, stage_b, dn2r, 1, 1)
    down_rows = jnp.reshape(dzg[...], (seq, width))
    g_down[0] = dot_tn(hid[...], down_rows).astype(bf16)
    down_sum.send(0)
    up_rows = jnp.reshape(n2g[...], (seq, width))
    g_up[0] = dot_tn(up_rows, du[...]).astype(bf16)
    up_sum.send(0)
    shared = jnp.zeros((1, width), f32)
    for step, s in enumerate(order):
        piece = dot(hid[block(s), :], w2[...])
        shared = shared + jnp.sum(cg[s].astype(f32) * piece, axis=0, keepdims=True)
        if step == 0:
            own[...] = piece
        else:
            stage_c[3 - step] = piece.astype(bf16)
    cot = cg[t].astype(f32)
    cot_sum = jnp.sum(cot, axis=0, keepdims=True)
    sums[5:6, :] = shared + cot_sum * obias[1:2, :]
    sums[7:8, :] = cot_sum * scales[1:2, :]
    down_sum.add_core()
    up_sum.add_core()

    @pl.when(end == 1)
    def _():
        slot_wait(4, dn2r, 0, 0)
        slot_wait(4, dn2r, 0, 1)
        dn2own[...] = dn2own[...] + dn2r[0].astype(f32)

    total = scatter_total(4, dn2r, dn2own[...], (3,))
    normed = xhat2[...]
    after = cg[t].astype(f32) + norm_back(total * gains[1:2, :], normed, inv2[:, 0:1])
    dx1[...] = after
    branch = after * scales[0:1, :]
    grad_rows = branch.astype(bf16)

    def mixed_back(k):
        return piece_copy(6, doz.at[k], dot_t.at[:, block(t)], k)

    for k in (2, 1, 3, 0):
        piece = dot_nt(pg[k], grad_rows).astype(bf16)
        if k == 0:
            dot_t[:, block(t)] = piece
        else:
            doz[k] = piece
            mixed_back(k).start()
    for i in (1, 0, 2):
        scatter_send(5, stage_c, z2r, i)
    sums[3:4, :] = jnp.sum(total, axis=0, keepdims=True)
    sums[1:2, :] = jnp.sum(total * normed, axis=0, keepdims=True)
    sums[4:5, :] = jnp.sum(after * a1[...], axis=0, keepdims=True)
    sums[6:7, :] = jnp.sum(branch, axis=0, keepdims=True)
    for k in range(NT):
        g_proj[k] = dot(og[k], grad_rows).astype(bf16)
    proj_sum.send(0)
    down_sum.add_first()
    proj_sum.add_core()
    up_sum.add_first()

    for k in range(1, NT):
        piece_arrived(6, dot_t.at[:, block((t + k) % NT)], k)
    grad_mixed = dot_nt(mq[...], dot_t[...]).astype(bf16)
    for h in range(heads):
        doh[h] = grad_mixed[:, h * 64 : (h + 1) * 64]
    for h in range(heads):
        lanes = slice(h * 64, (h + 1) * 64)

        grad_prob = dot_nt(doh[h], vh[h])
        weights = prob[h]
        crossed = jnp.sum(weights * grad_prob, axis=-1, keepdims=True)
        rounded = (weights * (grad_prob - crossed)).astype(bf16)
        ds[h] = rounded
        dqp[:, lanes] = dot(rounded, kh[h]).astype(bf16) * 0.125
        dvp[:, lanes] = dot_tn(probb[h], doh[h]).astype(bf16)
        dkp[:, lanes] = dot_tn(rounded, qh[h]).astype(bf16)
        part_q = dot(mqt[...], dqp[:, lanes]).astype(bf16)
        part_k = dot(mkt[...], dkp[:, lanes]).astype(bf16)
        part_v = dot(mkt[...], dvp[:, lanes]).astype(bf16)
        dqt[:, lanes] = part_q
        dkt[:, lanes] = part_k
        dvt[:, lanes] = part_v
        for i, part in enumerate((part_q, part_k, part_v)):
            direct_refs[h][0][64 * i : 64 * (i + 1), :] = dot_tn(part, n1g[...]).astype(bf16)
        qkv_sums[h].send()
        if h == 0:
            down_sum.add_second()
            up_sum.add_second()
        elif h == 1:
            scatter_merge(5, stage_c, z2r, 1)
            qkv_sums[0].add_core()
    proj_sum.add_first()
    qkv_sums[1].add_core()

    shift_total = jnp.zeros((1, width), f32)
    gain_total = jnp.zeros((1, width), f32)
    for step in (3, 2, 1, 0):
        s = order[step]
        part = block(s)
        piece = dot(dqt[part, :], wqkv[0:hw, :]) + dot(dkt[part, :], wqkv[hw : 2 * hw, :])
        piece = piece + dot(dvt[part, :], wqkv[2 * hw : 3 * hw, :])
        if step == 0:
            dn2own[...] = piece
        else:
            stage_d[3 - step] = piece.astype(bf16)
            if step > 1:
                for half in range(2):
                    scatter_send(7, stage_d, dn1r, 3 - step, half)
        normed, _ = normalize(xg[s].astype(f32))
        shift_total = shift_total + jnp.sum(piece, axis=0, keepdims=True)
        gain_total = gain_total + jnp.sum(piece * normed, axis=0, keepdims=True)
    sums[2:3, :] = shift_total
    sums[0:1, :] = gain_total
    zmr[t] = sums[0:REP, :]

    def small_tensor(k):
        return remote(
            zmr.at[t], zmr.at[t], z_send.at[10, k], z_recv.at[10, NT - k], (dp, (t + k) % NT)
        )

    for k in range(1, NT):
        small_tensor(k).start()
    qkv_sums[2].add_core()
    scatter_merge(5, stage_c, z2r, 0)
    down_sum.spread_first()
    up_sum.spread_first()
    proj_sum.add_second(gpz)

    def proj_exchange(k):
        return piece_copy(9, gpz.at[k], gpz.at[2 * NT - k], k)

    for k in range(1, NT):
        proj_exchange(k).start()
    scatter_send(7, stage_d, dn1r, 2)
    qkv_sums[0].add_parts()

    branch_two = scatter_total(5, z2r, own[...]) + obias[1:2, :]
    outv[...] = (x1[...] + scales[1:2, :] * branch_two).astype(bf16)
    stores = [pltpu.make_async_copy(outv, out, store_sem.at[0])]
    stores[0].start()

    row24 = lax.broadcasted_iota(i32, (24, 1), 0)
    lane_t = lax.broadcasted_iota(i32, (1, TABLE), 1)
    uexp[...] = jnp.zeros_like(uexp)
    gexp[...] = jnp.zeros_like(gexp)
    for h in range(heads):
        grads = ds[h].astype(f32)
        class_row = grads[CELLS : CELLS + 1, :]
        class_column = jnp.sum(
            jnp.where((down != CELLS) & (across == CELLS), grads, 0.0), axis=0, keepdims=True
        )
        cells = jnp.where(across < CELLS, grads, 0.0)
        pad_row = jnp.sum(jnp.where(pad_q, cells, 0.0), axis=0, keepdims=True)
        dsf[...] = jnp.where(pad_q, 0.0, cells)
        blank = jnp.zeros((24, WIDE - seq), f32)
        folded = jnp.zeros((24, WIDE), f32)
        for r in range(GRID):
            cells = jnp.concatenate([dsf[r * GRID : r * GRID + 24, :], blank], axis=1)
            folded = folded + (cells if r == 0 else pltpu.roll(cells, r * GRID, 1))
        padded_row = jnp.concatenate([pad_row, jnp.zeros((1, WIDE - seq), f32)], axis=1)
        folded = jnp.where(row24 < GRID, folded, 0.0) + jnp.where(row24 == GRID - 1, padded_row, 0.0)
        for i in range(GRID):
            gexp[GRID - 1 - i : GRID - i, :] = folded[i : i + 1, :]
        for x in range(SPAN):
            uexp[:, x * SPAN : x * SPAN + GRID] = gexp[:, x * GRID : (x + 1) * GRID]
        lined = pltpu.roll(uexp[...], 0, 1, stride=1, stride_axis=0)
        table = jnp.sum(lined, axis=0, keepdims=True)
        from_class = jnp.sum(jnp.where(across != CELLS, class_row, 0.0), axis=1, keepdims=True)
        class_pair = jnp.sum(jnp.where(across == CELLS, class_row, 0.0), axis=1, keepdims=True)
        to_class = jnp.sum(class_column, axis=1, keepdims=True)
        table = jnp.where(lane_t == ENTRIES, from_class, table)
        table = jnp.where(lane_t == ENTRIES + 1, to_class, table)
        tab[h : h + 1, :] = jnp.where(lane_t == ENTRIES + 2, class_pair, table)
        if h == 1:
            scatter_merge(7, stage_d, dn1r, 0, 0)
            scatter_merge(7, stage_d, dn1r, 0, 1)
            qkv_sums[1].add_parts()
    sums[9:10, 0:hw] = jnp.sum(dqt[...].astype(f32), axis=0, keepdims=True)
    sums[10:11, 0:hw] = jnp.sum(dvt[...].astype(f32), axis=0, keepdims=True)
    sums[9:11, hw:width] = jnp.zeros((2, width - hw), f32)
    for h in range(heads):
        at = 11 + 3 * h
        sums[at : at + 1, :] = tab[h : h + 1, 0:width]
        sums[at + 1 : at + 2, :] = tab[h : h + 1, width : 2 * width]
        sums[at + 2 : at + 3, 0 : TABLE - 2 * width] = tab[h : h + 1, 2 * width : TABLE]
        sums[at + 2 : at + 3, TABLE - 2 * width : width] = jnp.zeros((1, 3 * width - TABLE), f32)
    sums[11 + 3 * heads : SMALL, :] = jnp.zeros((SMALL - 11 - 3 * heads, width), f32)

    for k in range(1, NT):
        piece_arrived(10, zmr.at[(t + k) % NT], k)
    sums[0:REP, :] = zmr[0] + zmr[1] + zmr[2] + zmr[3]
    g_small[...] = sums[...].astype(bf16)
    small_sum.send()
    qkv_sums[2].add_parts()
    small_sum.add_core()
    value = gpz[0].astype(f32)
    for k in range(1, NT):
        piece_arrived(9, gpz.at[NT + k], k)
        value = value + gpz[NT + k].astype(f32)
    t_proj[0, proj_rows, my_lanes] = value.astype(bf16)
    proj_sum.send(3)
    down_sum.spread_second()
    qkv_sums[0].spread()
    scatter_merge(7, stage_d, dn1r, 1, 0)
    scatter_merge(7, stage_d, dn1r, 1, 1)
    qkv_sums[1].spread()
    up_sum.spread_second()
    small_sum.add_parts()
    proj_sum.spread_first()
    qkv_sums[2].spread()
    sources = [(t_down.at[0], t_down_hbm), (t_up.at[0], t_up_hbm), (t_proj.at[0], t_proj_hbm), (t_small.at[0], t_small_hbm)]
    sources += [(t_qkv.at[h], t_qkv_hbm.at[192 * h : 192 * (h + 1), :]) for h in range(heads)]
    sources += [(ingradv, ingrad)]
    stores += [pltpu.make_async_copy(src, dst, store_sem.at[i + 1]) for i, (src, dst) in enumerate(sources)]
    down_sum.take(5)
    stores[1].start()
    total = scatter_total(7, dn1r, dn2own[...], (3,))
    normed, inverse = normalize(xg[t].astype(f32))
    ingradv[...] = dx1[...] + norm_back(total * gain_one, normed, inverse)
    stores[8].start()
    small_sum.spread()
    proj_sum.spread_second()
    up_sum.take(5)
    stores[2].start()
    for h in range(heads):
        qkv_sums[h].take()
        stores[5 + h].start()
    proj_sum.take(5)
    stores[3].start()
    small_sum.take()
    stores[4].start()

    gather_sent(0, xg, x_hbm)
    gather_sent(1, cg, cot_hbm)
    gather_sent(3, n2g)
    for i in range(NT - 1):
        scatter_copy(5, stage_c, z2r, i).wait_send()
    scatter_copy(4, stage_b, dn2r, 2).wait_send()
    scatter_copy(7, stage_d, dn1r, 2).wait_send()
    for half in range(2):
        far_copy(4, stage_b, dn2r, half).wait_send()
        scatter_copy(4, stage_b, dn2r, 1, half).wait_send()
        scatter_copy(7, stage_d, dn1r, 0, half).wait_send()
        scatter_copy(7, stage_d, dn1r, 1, half).wait_send()
    for k in range(1, NT):
        proj_piece(k).wait_send()
        mixed_piece(k).wait_send()
        mixed_back(k).wait_send()
        proj_exchange(k).wait_send()
        small_tensor(k).wait_send()
    for part_sum in (down_sum, up_sum, proj_sum, small_sum, *qkv_sums):
        part_sum.sent()
    proj_all.sent(3)
    for store in stores:
        store.wait()


def finish_kernel(
    down_in, up_in, proj_in, qkv_in, small_in, out_in, ingrad_in,
    out, ingrad, g_qkv, g_qv, g_table, g_proj, g_up, g_up_bias, g_down, g_gains, g_shifts, g_scales, g_biases,
    down_v, up_v, proj_v, qkv_v, down_f, up_f, proj_f, qkv_f, small_v, out_v, ingrad_v, load_sem, store_sem,
):
    width = g_down.shape[1]
    hw = g_proj.shape[0]
    heads, entries = g_table.shape
    parts = []
    for given, rounded, widened, result in (
        (down_in, down_v, down_f, g_down), (up_in, up_v, up_f, g_up),
        (qkv_in, qkv_v, qkv_f, g_qkv), (proj_in, proj_v, proj_f, g_proj),
    ):
        for start in range(0, given.shape[0], PIECE):
            piece = [ref.at[start : start + PIECE, :] for ref in (given, rounded, widened, result)]
            parts.append(piece + [given is qkv_in])
    moved = [(small_in, small_v, None), (out_in, out_v, out), (ingrad_in, ingrad_v, ingrad)]
    count = len(parts)
    loads = [pltpu.make_async_copy(part[0], part[1], load_sem.at[i]) for i, part in enumerate(parts)]
    loads += [pltpu.make_async_copy(src, via, load_sem.at[count + i]) for i, (src, via, _) in enumerate(moved)]
    for copy in loads:
        copy.start()
    stores = []
    by_head = [i for i, part in enumerate(parts) if part[4]]
    for i, (_, rounded, widened, result, mixed) in enumerate(parts):
        if mixed:
            which = i - by_head[0]
            for h, j in enumerate(by_head):
                if which == 0:
                    loads[j].wait()
                widened[64 * h : 64 * (h + 1), :] = parts[j][1][64 * which : 64 * (which + 1), :].astype(f32)
        else:
            loads[i].wait()
            widened[...] = rounded[...].astype(f32)
        stores.append(pltpu.make_async_copy(widened, result, store_sem.at[i]))
        stores[-1].start()
    for i, (_, via, dst) in enumerate(moved):
        loads[count + i].wait()
        if dst is not None:
            stores.append(pltpu.make_async_copy(via, dst, store_sem.at[count + i]))
            stores[-1].start()
    small = small_v[...].astype(f32)
    g_gains[...] = small[0:2, :]
    g_shifts[...] = small[2:4, :]
    g_scales[...] = small[4:6, :]
    g_biases[...] = small[6:8, :]
    g_up_bias[...] = jnp.reshape(small[8:9, :], (width,))
    g_qv[...] = small[9:11, 0:hw]
    for h in range(heads):
        for j in range(3):
            lanes = min(width, entries - j * width)
            g_table[h : h + 1, j * width : j * width + lanes] = small[
                11 + 3 * h + j : 12 + 3 * h + j, 0:lanes
            ]
    for copy in stores:
        copy.wait()


def per_device(
    n_dp, tokens, grids, qkv_weight, qv_bias, rel_table, proj_weight, fc1_weight, fc1_bias, fc2_weight,
    norm_gains, norm_biases, layer_scales, out_biases, cotangent,
):
    rows, width = tokens.shape
    seq = rows * NT
    heads, entries = rel_table.shape
    hw = heads * 64
    ff = fc1_weight.shape[1]
    qkv_rows = jnp.transpose(qkv_weight, (1, 2, 0)).reshape(3 * hw, width)
    vm = pl.BlockSpec(memory_space=pltpu.VMEM)
    anywhere = pl.BlockSpec(memory_space=pl.ANY)

    def many(count, shape, dtype):
        return [pltpu.VMEM(shape, dtype)] * count

    def sems(*shape):
        return [pltpu.SemaphoreType.DMA(shape)]

    half = width // 2
    scratch = [
        pltpu.VMEM((rows, width), bf16), pltpu.VMEM((rows, width), f32), pltpu.VMEM((3 * hw, width), bf16),
        pltpu.VMEM((width, ff), bf16), pltpu.VMEM((ff, width), bf16),
        pltpu.VMEM((2, hw), f32), pltpu.VMEM((heads, entries), f32), pltpu.VMEM((ff,), bf16),
    ]
    scratch += many(4, (2, width), f32) + sems(13) + sems(9)
    scratch += many(4, (NT, rows, width), bf16)
    scratch += many(1, (NT, hw, rows), bf16) + many(1, (NT, hw, width), bf16)
    scratch += many(3, (NT, rows, width), bf16) + many(3, (NT - 1, rows, width), bf16)
    scratch += many(1, (NT, hw, rows), bf16) + sems(11, 2 * NT) + sems(11, 2 * NT) + sems(4, 5, 2)
    scratch += many(4, (seq, seq), bf16)
    scratch += many(1, (heads, seq, seq), f32) + many(1, (24, WIDE), f32) + many(1, (24, TABLE), f32)
    scratch += many(1, (seq, width), bf16) + many(3, (seq, hw), bf16)
    scratch += many(3, (heads, seq, 64), bf16)
    scratch += many(1, (heads, seq, seq), f32) + many(1, (heads, seq, seq), bf16)
    scratch += many(1, (seq, hw), bf16) + many(1, (hw, seq), bf16)
    scratch += many(2, (rows, width), f32) + many(1, (rows, 128), f32) + many(4, (rows, width), f32)
    scratch += many(2, (seq, ff), bf16) + many(1, (hw, seq), bf16) + many(1, (heads, seq, 64), bf16)
    scratch += many(1, (heads, seq, seq), bf16) + many(1, (seq, seq), f32) + many(6, (seq, hw), bf16)
    scratch += many(1, (8, TABLE), f32) + many(1, (SMALL, width), f32) + many(1, (NT, REP, width), f32)
    scratch += many(1, (2 * NT, hw // 4, half), bf16) + sems(5 + heads, 8) + sems(5 + heads, 8)
    for lead, count in ((1, ff), (1, width), (NT, hw)):
        scratch += [
            pltpu.VMEM((lead, count, width), bf16), pltpu.VMEM((lead, count, half), bf16),
            pltpu.VMEM((lead, count, half), bf16), pltpu.VMEM((lead, count // 2, half), bf16),
            pltpu.VMEM((lead, count // 4, half), bf16),
        ]
    for count in (192,) * heads + (SMALL,):
        scratch += [
            pltpu.VMEM((count, width), bf16), pltpu.VMEM((count, half), bf16), pltpu.VMEM((count, half), bf16),
            pltpu.VMEM((CHIPS - 1, count // CHIPS, half), bf16),
        ]
    for lead, count in ((1, ff), (1, width), (1, hw), (heads, 192), (1, SMALL)):
        scratch += many(1, (lead, count, width), bf16)
    flat = [jax.ShapeDtypeStruct((count, width), bf16) for count in (ff, width, hw, 3 * hw, SMALL)]
    output, input_grad, *totals = pl.pallas_call(
        main_kernel,
        out_shape=[
            jax.ShapeDtypeStruct((rows, width), bf16),
            jax.ShapeDtypeStruct((rows, width), f32),
        ]
        + flat,
        in_specs=[pl.BlockSpec(memory_space=pltpu.SMEM)] + [anywhere] * 13,
        out_specs=[anywhere] * 7,
        scratch_shapes=scratch,
        compiler_params=pltpu.CompilerParams(
            collective_id=0, has_side_effects=True, vmem_limit_bytes=60 << 20
        ),
        name="layer",
    )(
        grids, tokens, cotangent, qkv_rows, proj_weight, fc1_weight, fc2_weight,
        qv_bias, rel_table, fc1_bias, norm_gains, norm_biases, layer_scales, out_biases,
    )
    pair = jax.ShapeDtypeStruct((2, width), f32)
    pieces = sum(-(-count // PIECE) for count in (ff, width, hw, 3 * hw))
    results = pl.pallas_call(
        finish_kernel,
        out_shape=(
            jax.ShapeDtypeStruct((rows, width), bf16),
            jax.ShapeDtypeStruct((rows, width), f32),
            jax.ShapeDtypeStruct((3 * hw, width), f32),
            jax.ShapeDtypeStruct((2, hw), f32),
            jax.ShapeDtypeStruct((heads, entries), f32),
            jax.ShapeDtypeStruct((hw, width), f32),
            jax.ShapeDtypeStruct((width, ff), f32),
            jax.ShapeDtypeStruct((ff,), f32),
            jax.ShapeDtypeStruct((ff, width), f32),
            pair, pair, pair, pair,
        ),
        in_specs=[anywhere] * 7,
        out_specs=(
            anywhere, anywhere, anywhere, vm, vm, anywhere, anywhere, vm, anywhere, vm, vm, vm, vm,
        ),
        scratch_shapes=[
            pltpu.VMEM((ff, width), bf16), pltpu.VMEM((width, ff), bf16), pltpu.VMEM((hw, width), bf16),
            pltpu.VMEM((3 * hw, width), bf16),
            pltpu.VMEM((ff, width), f32), pltpu.VMEM((width, ff), f32), pltpu.VMEM((hw, width), f32),
            pltpu.VMEM((3 * hw, width), f32), pltpu.VMEM((SMALL, width), bf16),
            pltpu.VMEM((rows, width), bf16), pltpu.VMEM((rows, width), f32),
            *sems(pieces + 3), *sems(pieces + 3),
        ],
        compiler_params=pltpu.CompilerParams(vmem_limit_bytes=60 << 20),
        name="finish",
    )(*totals, output, input_grad)
    results = list(results)
    stride = GROUP
    while stride < n_dp:
        hops = [(i, i ^ stride) for i in range(n_dp)]
        results[2:] = [value + lax.ppermute(value, "dp", hops) for value in results[2:]]
        stride *= 2
    results[2] = jnp.transpose(results[2].reshape(3, hw, width), (2, 0, 1))
    return tuple(results)


def solution(mesh):
    n_dp = mesh.shape["dp"]
    blocks = P(("dp", "tensor"), None)
    placed = (
        blocks, P("dp", None), P(None, None, "tensor"), P(None, "tensor"), P("tensor", None), P("tensor", None),
        P(None, "tensor"), P("tensor"), P("tensor", None), P(), P(), P(), P(), blocks,
    )
    given = (
        blocks, blocks, P(None, None, "tensor"), P(None, "tensor"), P("tensor", None), P("tensor", None),
        P(None, "tensor"), P("tensor"), P("tensor", None), P(), P(), P(), P(),
    )

    def layer(*arrays):
        return per_device(n_dp, *arrays)

    return jax.shard_map(layer, mesh=mesh, in_specs=placed, out_specs=given, check_vma=False)
```

```python
import jax
import jax.numpy as jnp
from jax import lax
from jax.experimental import pallas as pl
from jax.experimental.pallas import tpu as pltpu
from jax.sharding import PartitionSpec as P

GRID = 22
SPAN = 2 * GRID - 1
CELLS = GRID * GRID
ENTRIES = SPAN * SPAN
MESH = pl.DeviceIdType.MESH
f32 = jnp.float32
bf16 = jnp.bfloat16
i32 = jnp.int32

eps_norm = 1e-06
masked = -1e30
NT = 4
CHIPS = 4
CORES = 2
GROUP = CHIPS * CORES
TABLE = 1920
WIDE = 1024
SMALL = 64
REP = 8
PIECE = 192


def dot(left, right):
    return lax.dot_general(left, right, (((1,), (0,)), ((), ())), preferred_element_type=f32)


def dot_nt(left, right):
    return lax.dot_general(left, right, (((1,), (1,)), ((), ())), preferred_element_type=f32)


def dot_tn(left, right):
    return lax.dot_general(left, right, (((0,), (0,)), ((), ())), preferred_element_type=f32)


def normalize(values):
    center = values - jnp.mean(values, axis=-1, keepdims=True)
    inverse = lax.rsqrt(jnp.mean(center * center, axis=-1, keepdims=True) + eps_norm)
    return center * inverse, inverse


def norm_back(grad_normed, normed, inverse):
    average = jnp.mean(grad_normed, axis=-1, keepdims=True)
    crossed = jnp.mean(grad_normed * normed, axis=-1, keepdims=True)
    return inverse * (grad_normed - average - normed * crossed)


def split_cell(place):
    row = (place * 2979) >> 16
    return row, place - row * GRID


def query_tokens(place, high, wide):
    row, back = split_cell(place)
    inside = (place < CELLS) & (row < high) & (GRID - 1 - back < wide)
    before = jnp.minimum(row, high) * wide + jnp.where(
        row < high, jnp.maximum(back - (GRID - wide), 0), 0
    )
    token = jnp.where(inside, 1 + row * wide + (GRID - 1 - back), high * wide + 1 + place - before)
    token = jnp.where(place == CELLS, 0, jnp.where(place > CELLS, place, token))
    padding = jnp.logical_not(inside) & (place != CELLS)
    return token, padding


def key_tokens(place, high, wide):
    row, back = split_cell(place)
    row = GRID - 1 - row
    column = GRID - 1 - back
    inside = (place < CELLS) & (row < high) & (column < wide)
    token = jnp.where(inside, 1 + row * wide + column, -1)
    return jnp.where(place == CELLS, 0, token)


def one_hot(left, right):
    return jnp.where(left == right, 1.0, 0.0).astype(bf16)


def main_kernel(
    grids, x_hbm, cot_hbm, wqkv_hbm, wproj_hbm, w1_hbm, w2_hbm, qvb_hbm, rel_hbm, b1_hbm,
    gains_hbm, biases_hbm, scales_hbm, obias_hbm,
    out, ingrad, t_down_hbm, t_up_hbm, t_proj_hbm, t_qkv_hbm, t_small_hbm,
    outv, ingradv, wqkv, w1, w2, qvb, rel, b1, gains, biases, scales, obias, load_sem, store_sem,
    xg, cg, dzg, n2g, og, pg, dn2r, z2r, dn1r, stage_b, stage_c, stage_d, doz, z_send, z_recv, z_half,
    mq, mqt, mk, mkt, bias, gexp, uexp,
    n1g, qt, kt, vt, qh, kh, vh, prob, probb, op, ot,
    x1, xhat2, inv2, a1, dx1, own, dn2own,
    hid, du, dot_t, doh, ds, dsf, dqp, dkp, dvp, dqt, dkt, dvt,
    tab, sums, zmr, gpz, p_send, p_recv,
    *plane,
):
    dp = lax.axis_index("dp")
    t = lax.axis_index("tensor")
    rows, width = x_hbm.shape
    seq = rows * NT
    heads = rel.shape[0]
    hw = heads * 64
    base = (dp // GROUP) * GROUP
    mine = dp % GROUP
    core = mine % CORES
    chip_x = (mine // 2) % 2
    chip_y = mine // 4
    to_x = 2 - 4 * chip_x
    to_y = 4 - 8 * chip_y
    sibling = base + mine + 1 - 2 * core
    first_peer = base + mine + (1 - core) * to_x + core * to_y
    second_peer = base + mine + core * to_x + (1 - core) * to_y
    bit_one = (1 - core) * chip_x + core * chip_y
    bit_two = core * chip_x + (1 - core) * chip_y
    quarter = bit_one * 2 + bit_two
    end = ((t - 1) * (t - 2)) // 2
    order = [t, t + 1 - 2 * (t % 2), 2 - t // 2, 3 - 3 * (t // 2)]

    pairs = [
        (x_hbm, xg.at[t]), (cot_hbm, cg.at[t]), (scales_hbm, scales), (rel_hbm, rel), (wqkv_hbm, wqkv),
        (gains_hbm, gains), (biases_hbm, biases), (qvb_hbm, qvb), (wproj_hbm, pg.at[0]), (w1_hbm, w1),
        (w2_hbm, w2), (b1_hbm, b1), (obias_hbm, obias),
    ]
    loads = [pltpu.make_async_copy(src, dst, load_sem.at[i]) for i, (src, dst) in enumerate(pairs)]
    barrier = pltpu.get_barrier_semaphore()
    for k in range(1, NT):
        pl.semaphore_signal(barrier, inc=1, device_id=(dp, (t + k) % NT), device_id_type=MESH)
    chip = mine // CORES
    others = [base + ((chip + k) % CHIPS) * CORES + core for k in range(CHIPS)]
    for peer in (sibling, *others[1:]):
        pl.semaphore_signal(barrier, inc=1, device_id=(peer, t), device_id_type=MESH)
    for load in loads:
        load.start()
    pl.semaphore_wait(barrier, NT - 1 + CHIPS)

    def block(s):
        return pl.ds(pl.multiple_of(s * rows, rows), rows)

    def remote(src, dst, send, recv, device):
        return pltpu.make_async_remote_copy(
            src_ref=src, dst_ref=dst, send_sem=send, recv_sem=recv, device_id=device, device_id_type=MESH
        )

    half_rows = rows // 2

    def half_copy(phase, buf, src, half, dst, way, given=None):
        spot = buf.at[src, half * half_rows : (half + 1) * half_rows, :]
        if given is not None:
            given = given.at[half * half_rows : (half + 1) * half_rows, :]
        return remote(
            spot if given is None else given, spot,
            z_half.at[phase, way, half], z_recv.at[phase, src * 2 + half], (dp, dst),
        )

    def gather_start(phase, buf, given=None):
        for half in range(2):
            half_copy(phase, buf, t, half, order[1], 0, given).start()
            pl.when(end == 0)(half_copy(phase, buf, t, half, order[2], 1, given).start)

    def half_arrived(phase, buf, step, half):
        half_copy(phase, buf, order[step], half, order[1], 0).wait_recv()

    def half_forward(phase, buf, step, half):
        to = order[2] if step == 1 else order[1]
        half_copy(phase, buf, order[step], half, to, 1 + step).start()

    def gather_near(phase, buf):
        @pl.when(end == 0)
        def _():
            for half in range(2):
                for step in (1, 2):
                    half_arrived(phase, buf, step, half)
                    half_forward(phase, buf, step, half)

    def forward_both(phase, buf, step):
        @pl.when(end == 0)
        def _():
            for half in range(2):
                half_arrived(phase, buf, step, half)
                half_forward(phase, buf, step, half)

    def end_take(phase, buf, step):
        for half in range(2):
            pl.when(end == 1)(lambda: half_arrived(phase, buf, step, half))

    def gather_take(phase, buf, step):
        for half in range(2):
            if step < 3:
                pl.when(end == 1)(lambda: half_arrived(phase, buf, step, half))
            else:
                half_arrived(phase, buf, step, half)
                pl.when(end == 0)(lambda: half_forward(phase, buf, step, half))

    def gather_sent(phase, buf, given=None):
        for half in range(2):
            half_copy(phase, buf, t, half, order[1], 0, given).wait_send()

            @pl.when(end == 0)
            def _():
                half_copy(phase, buf, t, half, order[2], 1, given).wait_send()
                for step in (1, 2, 3):
                    half_copy(phase, buf, order[step], half, order[1], 1 + step).wait_send()

    def scatter_part(phase, stage, buf, i, dst, slot, half):
        if half is None:
            return remote(
                stage.at[i], buf.at[slot], z_send.at[phase, i], z_recv.at[phase, slot], (dp, dst)
            )
        part = slice(half * half_rows, (half + 1) * half_rows)
        return remote(
            stage.at[i, part, :], buf.at[slot, part, :],
            z_send.at[phase, i + NT * half], z_recv.at[phase, slot + NT * half], (dp, dst),
        )

    def scatter_copy(phase, stage, buf, i, half=None):
        if i == 2:
            dst, slot = order[1], 2
        else:
            dst = end * order[1] + (1 - end) * order[3 - i]
            slot = end * i + (1 - end) * 3
        return scatter_part(phase, stage, buf, i, dst, slot, half)

    def far_copy(phase, stage, buf, half):
        return scatter_part(phase, stage, buf, 0, order[3], (1 - end) * 3, half)

    def slot_wait(phase, buf, slot, half=None):
        scatter_part(phase, buf, buf, slot, order[1], slot, half).wait_recv()

    def scatter_send(phase, stage, buf, i, half=None):
        if i == 2:
            scatter_copy(phase, stage, buf, i, half).start()
        else:
            pl.when(end == 1)(scatter_copy(phase, stage, buf, i, half).start)

    def scatter_merge(phase, stage, buf, i, half=None):
        part = slice(None) if half is None else slice(half * half_rows, (half + 1) * half_rows)

        @pl.when(end == 0)
        def _():
            slot_wait(phase, buf, i, half)
            stage[i, part, :] = (stage[i, part, :].astype(f32) + buf[i, part, :].astype(f32)).astype(bf16)
            scatter_copy(phase, stage, buf, i, half).start()

    def scatter_total(phase, buf, total, halves=()):
        for slot in (2, 3):
            if slot in halves:
                slot_wait(phase, buf, slot, 0)
                slot_wait(phase, buf, slot, 1)
            else:
                slot_wait(phase, buf, slot)
            total = total + buf[slot].astype(f32)
        return total

    def piece_copy(phase, src, dst, k):
        return remote(
            src, dst, z_send.at[phase, k], z_recv.at[phase, NT - k], (dp, (t + k) % NT)
        )

    def piece_arrived(phase, dst, k):
        remote(dst, dst, z_send.at[phase, k], z_recv.at[phase, k], (dp, (t + k) % NT)).wait_recv()

    half_width = width // 2
    my_lanes = pl.ds(pl.multiple_of(core * half_width, half_width), half_width)
    your_lanes = pl.ds(pl.multiple_of((1 - core) * half_width, half_width), half_width)

    def span(start, count):
        return pl.ds(pl.multiple_of(start, 16), count)

    class Plane:
        def __init__(self, index, refs, target):
            self.index, self.target = index, target
            self.count = target.shape[1]
            self.fours = self.count // 4
            if refs is not None:
                self.given, self.near, self.held, self.one, self.two = refs
                self.lead = self.given.shape[0]

        def copy(self, step, src, dst, peer):
            return remote(
                src, dst, p_send.at[self.index, step], p_recv.at[self.index, step], (peer, t)
            )

        def outgoing(self, step):
            c, f = self.count, self.fours
            if step == 0:
                return self.copy(0, self.given.at[:, :, your_lanes], self.near, sibling)
            if step == 1:
                src = self.held.at[:, span((1 - bit_one) * 2 * f, 2 * f), :]
                return self.copy(1, src, self.one, first_peer)
            if step == 2:
                src = self.held.at[:, span((bit_one * 2 + 1 - bit_two) * f, f), :]
                return self.copy(2, src, self.two, second_peer)
            if step == 3:
                spot, peer = self.target.at[:, span(quarter * f, f), my_lanes], second_peer
            elif step == 4:
                spot, peer = self.target.at[:, span(bit_one * 2 * f, 2 * f), my_lanes], first_peer
            else:
                spot, peer = self.target.at[:, :, my_lanes], sibling
            return self.copy(step, spot, spot, peer)

        def incoming(self, step):
            f = self.fours
            if step < 3:
                return self.outgoing(step)
            if step == 3:
                spot = self.target.at[:, span((bit_one * 2 + 1 - bit_two) * f, f), my_lanes]
            elif step == 4:
                spot = self.target.at[:, span((1 - bit_one) * 2 * f, 2 * f), my_lanes]
            else:
                spot = self.target.at[:, :, your_lanes]
            return self.copy(step, spot, spot, sibling)

        def send(self, step):
            self.outgoing(step).start()

        def take(self, step):
            self.incoming(step).wait_recv()

        def add_core(self):
            self.take(0)
            for q in range(self.lead):
                value = self.given[q, :, my_lanes].astype(f32) + self.near[q].astype(f32)
                self.held[q] = value.astype(bf16)
            self.send(1)

        def add_first(self):
            self.take(1)
            part = span(bit_one * 2 * self.fours, 2 * self.fours)
            for q in range(self.lead):
                value = self.held[q, part, :].astype(f32) + self.one[q].astype(f32)
                self.held[q, part, :] = value.astype(bf16)
            self.send(2)

        def add_second(self, store=None):
            self.take(2)
            part = span(quarter * self.fours, self.fours)
            for q in range(self.lead):
                value = (self.held[q, part, :].astype(f32) + self.two[q].astype(f32)).astype(bf16)
                if store is None:
                    self.target[q, part, my_lanes] = value
                else:
                    store[q] = value
            if store is None:
                self.send(3)

        def spread_first(self):
            self.take(3)
            self.send(4)

        def spread_second(self):
            self.take(4)
            self.send(5)

        def sent(self, first=0):
            for step in range(first, 6):
                self.outgoing(step).wait_send()

    class Direct:
        def __init__(self, index, refs, target):
            self.index, self.target = index, target
            self.fours = target.shape[1] // CHIPS
            self.given, self.near, self.held, self.parts = refs

        def copy(self, step, src, dst, peer):
            return remote(
                src, dst, p_send.at[self.index, step], p_recv.at[self.index, step], (peer, t)
            )

        def rows_of(self, k):
            return span(((chip + k) % CHIPS) * self.fours, self.fours)

        def core_copy(self):
            return self.copy(0, self.given.at[:, your_lanes], self.near, sibling)

        def part_copy(self, k):
            return self.copy(k, self.held.at[self.rows_of(k), :], self.parts.at[k - 1], others[k])

        def back_copy(self, k):
            spot = self.target.at[0, self.rows_of(0), my_lanes]
            return self.copy(3 + k, spot, spot, others[k])

        def pair_copy(self):
            spot = self.target.at[0, :, my_lanes]
            return self.copy(7, spot, spot, sibling)

        def send(self):
            self.core_copy().start()

        def add_core(self):
            self.core_copy().wait_recv()
            value = self.given[:, my_lanes].astype(f32) + self.near[...].astype(f32)
            self.held[...] = value.astype(bf16)
            for k in (2, 1, 3):
                self.part_copy(k).start()

        def add_parts(self):
            value = self.held[self.rows_of(0), :].astype(f32)
            for k in range(1, CHIPS):
                self.part_copy(k).wait_recv()
                value = value + self.parts[k - 1].astype(f32)
            self.target[0, self.rows_of(0), my_lanes] = value.astype(bf16)
            for k in (2, 1, 3):
                self.back_copy(k).start()

        def spread(self):
            for k in range(1, CHIPS):
                spot = self.target.at[0, self.rows_of(CHIPS - k), my_lanes]
                self.copy(3 + k, spot, spot, others[k]).wait_recv()
            self.pair_copy().start()

        def take(self):
            spot = self.target.at[0, :, your_lanes]
            self.copy(7, spot, spot, sibling).wait_recv()

        def sent(self):
            self.core_copy().wait_send()
            for k in range(1, CHIPS):
                self.part_copy(k).wait_send()
                self.back_copy(k).wait_send()
            self.pair_copy().wait_send()

    down_refs, up_refs, proj_refs = (plane[5 * i : 5 * i + 5] for i in range(3))
    direct_refs = [plane[15 + 4 * i : 19 + 4 * i] for i in range(heads + 1)]
    t_down, t_up, t_proj, t_qkv, t_small = plane[19 + 4 * heads :]
    down_sum = Plane(0, down_refs, t_down)
    up_sum = Plane(1, up_refs, t_up)
    proj_sum = Plane(2, proj_refs, t_proj)
    proj_all = Plane(3, None, pg.at[1:NT])
    small_sum = Direct(4, direct_refs[heads], t_small)
    qkv_sums = [Direct(5 + h, direct_refs[h], t_qkv.at[h : h + 1]) for h in range(heads)]
    g_down, g_up, g_proj, g_small = (refs[0] for refs in (down_refs, up_refs, proj_refs, direct_refs[heads]))

    gather_start(0, xg, x_hbm)
    proj_rows = span(quarter * (hw // 4), hw // 4)

    def proj_piece(k):
        return piece_copy(8, pg.at[0, proj_rows, my_lanes], pg.at[NT - k, proj_rows, my_lanes], k)

    loads[8].wait()
    for k in range(1, NT):
        proj_piece(k).start()
    for half in range(2):
        pl.when(end == 1)(half_copy(1, cg, t, half, order[1], 0, cot_hbm).start)
    high = grids[0, 0]
    wide = grids[0, 1]
    down = lax.broadcasted_iota(i32, (seq, 1), 0)
    across = lax.broadcasted_iota(i32, (1, seq), 1)
    token_q, pad_q = query_tokens(down, high, wide)
    token_q_across, _ = query_tokens(across, high, wide)
    token_k = key_tokens(down, high, wide)
    token_k_across = key_tokens(across, high, wide)
    mq[...] = one_hot(token_q, across)
    mqt[...] = one_hot(down, token_q_across)
    mk[...] = one_hot(token_k, across)
    mkt[...] = one_hot(down, token_k_across)
    gexp[...] = jnp.zeros_like(gexp)
    tab[...] = jnp.zeros_like(tab)
    loads[3].wait()
    tab[0:heads, 0 : ENTRIES + 3] = rel[...]
    for h in range(heads):
        table = tab[h : h + 1, :]
        lined = pltpu.roll(jnp.broadcast_to(table, (24, TABLE)), TABLE - (GRID - 1), 1)
        uexp[...] = pltpu.roll(lined, 0, 1, stride=1, stride_axis=0)
        for x in range(SPAN):
            gexp[:, x * GRID : (x + 1) * GRID] = uexp[:, x * SPAN : x * SPAN + GRID]
        hankel = gexp[...]
        for r in range(GRID):
            moved = hankel if r == 0 else pltpu.roll(hankel, WIDE - r * GRID, 1)
            bias[h, r * GRID : (r + 1) * GRID, :] = moved[0:GRID, 0:seq]
        bias[h, CELLS:seq, :] = jnp.zeros((seq - CELLS, seq), f32)
        origin = bias[h, GRID - 1 : GRID, :]
        from_class = table[:, ENTRIES : ENTRIES + 1]
        to_class = table[:, ENTRIES + 1 : ENTRIES + 2]
        class_pair = table[:, ENTRIES + 2 : ENTRIES + 3]

        def settle(i, carry):
            part = pl.ds(pl.multiple_of(i * 128, 128), 128)
            place = lax.broadcasted_iota(i32, (128, 1), 0) + i * 128
            _, padded = query_tokens(place, high, wide)
            values = jnp.where(padded, origin, bias[h, part, :])
            values = jnp.where(across == CELLS, to_class, values)
            values = jnp.where(
                place == CELLS, jnp.where(across == CELLS, class_pair, from_class), values
            )
            bias[h, part, :] = jnp.where(token_k_across >= 0, values, masked)
            return carry

        lax.fori_loop(0, seq // 128, settle, 0)

    for i in (0, 4, 5, 6, 7):
        loads[i].wait()
    gain_one, shift_one = gains[0:1, :], biases[0:1, :]

    def project(s):
        normed, _ = normalize(xg[s].astype(f32))
        sent = (normed * gain_one + shift_one).astype(bf16)
        part = block(s)
        n1g[part, :] = sent
        qt[part, :] = ((dot_nt(sent, wqkv[0:hw, :]) + qvb[0:1, :]) * 0.125).astype(bf16)
        kt[part, :] = dot_nt(sent, wqkv[hw : 2 * hw, :]).astype(bf16)
        vt[part, :] = (dot_nt(sent, wqkv[2 * hw : 3 * hw, :]) + qvb[1:2, :]).astype(bf16)

    project(t)
    gather_near(0, xg)
    for half in range(2):
        pl.when(end == 0)(half_copy(1, cg, t, half, order[2], 1, cot_hbm).start)
    gather_take(0, xg, 1)
    project(order[1])
    gather_take(0, xg, 2)
    project(order[2])
    for k in range(1, NT):
        piece_arrived(8, pg.at[k, proj_rows, my_lanes], k)
    proj_all.send(3)
    gather_take(0, xg, 3)
    for half in range(2):
        pl.when(end == 0)(half_copy(1, cg, t, half, order[1], 0, cot_hbm).start)
    forward_both(1, cg, 1)
    project(order[3])
    forward_both(1, cg, 2)
    proj_all.spread_first()

    queries = dot(mq[...], qt[...]).astype(bf16)
    keys = dot(mk[...], kt[...]).astype(bf16)
    values = dot(mk[...], vt[...]).astype(bf16)
    for h in range(heads):
        lanes = slice(h * 64, (h + 1) * 64)
        qh[h] = queries[:, lanes]
        kh[h] = keys[:, lanes]
        vh[h] = values[:, lanes]
    for h in range(heads):
        logits = dot_nt(qh[h], kh[h]) + bias[h]
        raised = jnp.exp(logits - jnp.max(logits, axis=-1, keepdims=True))
        weights = raised * (1.0 / jnp.sum(raised, axis=-1, keepdims=True))
        prob[h] = weights
        rounded = weights.astype(bf16)
        probb[h] = rounded
        op[:, h * 64 : (h + 1) * 64] = dot(rounded, vh[h]).astype(bf16)
    ot[...] = dot_tn(op[...], mq[...]).astype(bf16)

    def mixed_piece(k):
        return piece_copy(2, ot.at[:, block((t + k) % NT)], og.at[NT - k], k)

    for k in (2, 1, 3):
        mixed_piece(k).start()
    forward_both(1, cg, 3)
    og[0] = ot[:, block(t)]
    total = dot_tn(og[0], pg[0])
    loads[2].wait()
    loads[12].wait()
    proj_all.spread_second()
    for k in range(1, NT):
        piece_arrived(2, og.at[k], k)
    proj_all.take(5)
    for k in range(1, NT):
        total = total + dot_tn(og[k], pg[k])
    branch_one = total + obias[0:1, :]
    a1[...] = branch_one
    after_one = xg[t].astype(f32) + scales[0:1, :] * branch_one
    x1[...] = after_one
    normed, inverse = normalize(after_one)
    xhat2[...] = normed
    inv2[...] = jnp.broadcast_to(inverse, inv2.shape)
    n2g[t] = (normed * gains[1:2, :] + biases[1:2, :]).astype(bf16)
    gather_start(3, n2g)

    for i in (9, 10, 11):
        loads[i].wait()
    shift_up = jnp.reshape(b1[...].astype(f32), (1, b1.shape[0]))

    def feed(step, half=None):
        s = order[step]
        inner = slice(None) if half is None else slice(half * half_rows, (half + 1) * half_rows)
        part = block(s) if half is None else span(s * rows + half * half_rows, half_rows)
        before = dot(n2g[s, inner, :], w1[...]) + shift_up
        cumulative = 0.5 * (1.0 + lax.erf(before * 0.7071067811865476))
        slope = cumulative + before * (jnp.exp(-0.5 * before * before) * 0.3989422804014327)
        hid[part, :] = (before * cumulative).astype(bf16)
        grad_rows = (cg[s, inner, :].astype(f32) * scales[1:2, :]).astype(bf16)
        dzg[s, inner, :] = grad_rows
        grad_pre = (dot_nt(grad_rows, w2[...]) * slope).astype(bf16)
        du[part, :] = grad_pre
        back = dot_nt(grad_pre, w1[...])
        if step == 0:
            dn2own[...] = back
        else:
            stage_b[3 - step, inner, :] = back.astype(bf16)
        return jnp.sum(grad_pre.astype(f32), axis=0, keepdims=True)

    loads[1].wait()
    bias_up = feed(0)
    gather_near(3, n2g)
    end_take(1, cg, 1)
    gather_take(3, n2g, 1)
    bias_up = bias_up + feed(1)
    scatter_copy(4, stage_b, dn2r, 2).start()
    end_take(1, cg, 2)
    for half in range(2):
        pl.when(end == 1)(lambda: half_arrived(3, n2g, 2, half))
    bias_up = bias_up + feed(2)
    for half in range(2):
        scatter_send(4, stage_b, dn2r, 1, half)
    end_take(1, cg, 3)
    for half in range(2):
        half_arrived(3, n2g, 3, half)
        pl.when(end == 0)(lambda: half_forward(3, n2g, 3, half))
    bias_up = bias_up + feed(3)
    for half in range(2):
        far_copy(4, stage_b, dn2r, half).start()
    sums[8:9, :] = bias_up
    scatter_merge(4, stage_b, dn2r, 1, 0)
    scatter_merge(4, stage_b, dn2r, 1, 1)
    down_rows = jnp.reshape(dzg[...], (seq, width))
    g_down[0] = dot_tn(hid[...], down_rows).astype(bf16)
    down_sum.send(0)
    up_rows = jnp.reshape(n2g[...], (seq, width))
    g_up[0] = dot_tn(up_rows, du[...]).astype(bf16)
    up_sum.send(0)
    shared = jnp.zeros((1, width), f32)
    for step, s in enumerate(order):
        piece = dot(hid[block(s), :], w2[...])
        shared = shared + jnp.sum(cg[s].astype(f32) * piece, axis=0, keepdims=True)
        if step == 0:
            own[...] = piece
        else:
            stage_c[3 - step] = piece.astype(bf16)
    cot = cg[t].astype(f32)
    cot_sum = jnp.sum(cot, axis=0, keepdims=True)
    sums[5:6, :] = shared + cot_sum * obias[1:2, :]
    sums[7:8, :] = cot_sum * scales[1:2, :]
    down_sum.add_core()
    up_sum.add_core()

    @pl.when(end == 1)
    def _():
        slot_wait(4, dn2r, 0, 0)
        slot_wait(4, dn2r, 0, 1)
        dn2own[...] = dn2own[...] + dn2r[0].astype(f32)

    total = scatter_total(4, dn2r, dn2own[...], (3,))
    normed = xhat2[...]
    after = cg[t].astype(f32) + norm_back(total * gains[1:2, :], normed, inv2[:, 0:1])
    dx1[...] = after
    branch = after * scales[0:1, :]
    grad_rows = branch.astype(bf16)

    def mixed_back(k):
        return piece_copy(6, doz.at[k], dot_t.at[:, block(t)], k)

    for k in (2, 1, 3, 0):
        piece = dot_nt(pg[k], grad_rows).astype(bf16)
        if k == 0:
            dot_t[:, block(t)] = piece
        else:
            doz[k] = piece
            mixed_back(k).start()
    for i in (1, 0, 2):
        scatter_send(5, stage_c, z2r, i)
    sums[3:4, :] = jnp.sum(total, axis=0, keepdims=True)
    sums[1:2, :] = jnp.sum(total * normed, axis=0, keepdims=True)
    sums[4:5, :] = jnp.sum(after * a1[...], axis=0, keepdims=True)
    sums[6:7, :] = jnp.sum(branch, axis=0, keepdims=True)
    for k in range(NT):
        g_proj[k] = dot(og[k], grad_rows).astype(bf16)
    proj_sum.send(0)
    down_sum.add_first()
    proj_sum.add_core()
    up_sum.add_first()

    for k in range(1, NT):
        piece_arrived(6, dot_t.at[:, block((t + k) % NT)], k)
    grad_mixed = dot_nt(mq[...], dot_t[...]).astype(bf16)
    for h in range(heads):
        doh[h] = grad_mixed[:, h * 64 : (h + 1) * 64]
    for h in range(heads):
        lanes = slice(h * 64, (h + 1) * 64)

        grad_prob = dot_nt(doh[h], vh[h])
        weights = prob[h]
        crossed = jnp.sum(weights * grad_prob, axis=-1, keepdims=True)
        rounded = (weights * (grad_prob - crossed)).astype(bf16)
        ds[h] = rounded
        dqp[:, lanes] = dot(rounded, kh[h]).astype(bf16) * 0.125
        dvp[:, lanes] = dot_tn(probb[h], doh[h]).astype(bf16)
        dkp[:, lanes] = dot_tn(rounded, qh[h]).astype(bf16)
        part_q = dot(mqt[...], dqp[:, lanes]).astype(bf16)
        part_k = dot(mkt[...], dkp[:, lanes]).astype(bf16)
        part_v = dot(mkt[...], dvp[:, lanes]).astype(bf16)
        dqt[:, lanes] = part_q
        dkt[:, lanes] = part_k
        dvt[:, lanes] = part_v
        for i, part in enumerate((part_q, part_k, part_v)):
            direct_refs[h][0][64 * i : 64 * (i + 1), :] = dot_tn(part, n1g[...]).astype(bf16)
        qkv_sums[h].send()
        if h == 0:
            down_sum.add_second()
            up_sum.add_second()
        elif h == 1:
            scatter_merge(5, stage_c, z2r, 1)
            qkv_sums[0].add_core()
    proj_sum.add_first()
    qkv_sums[1].add_core()

    shift_total = jnp.zeros((1, width), f32)
    gain_total = jnp.zeros((1, width), f32)
    for step in (3, 2, 1, 0):
        s = order[step]
        part = block(s)
        piece = dot(dqt[part, :], wqkv[0:hw, :]) + dot(dkt[part, :], wqkv[hw : 2 * hw, :])
        piece = piece + dot(dvt[part, :], wqkv[2 * hw : 3 * hw, :])
        if step == 0:
            dn2own[...] = piece
        else:
            stage_d[3 - step] = piece.astype(bf16)
            if step > 1:
                for half in range(2):
                    scatter_send(7, stage_d, dn1r, 3 - step, half)
        normed, _ = normalize(xg[s].astype(f32))
        shift_total = shift_total + jnp.sum(piece, axis=0, keepdims=True)
        gain_total = gain_total + jnp.sum(piece * normed, axis=0, keepdims=True)
    sums[2:3, :] = shift_total
    sums[0:1, :] = gain_total
    zmr[t] = sums[0:REP, :]

    def small_tensor(k):
        return remote(
            zmr.at[t], zmr.at[t], z_send.at[10, k], z_recv.at[10, NT - k], (dp, (t + k) % NT)
        )

    for k in range(1, NT):
        small_tensor(k).start()
    qkv_sums[2].add_core()
    scatter_merge(5, stage_c, z2r, 0)
    down_sum.spread_first()
    up_sum.spread_first()
    proj_sum.add_second(gpz)

    def proj_exchange(k):
        return piece_copy(9, gpz.at[k], gpz.at[2 * NT - k], k)

    for k in range(1, NT):
        proj_exchange(k).start()
    scatter_send(7, stage_d, dn1r, 2)
    qkv_sums[0].add_parts()

    branch_two = scatter_total(5, z2r, own[...]) + obias[1:2, :]
    outv[...] = (x1[...] + scales[1:2, :] * branch_two).astype(bf16)
    stores = [pltpu.make_async_copy(outv, out, store_sem.at[0])]
    stores[0].start()

    row24 = lax.broadcasted_iota(i32, (24, 1), 0)
    lane_t = lax.broadcasted_iota(i32, (1, TABLE), 1)
    uexp[...] = jnp.zeros_like(uexp)
    gexp[...] = jnp.zeros_like(gexp)
    for h in range(heads):
        grads = ds[h].astype(f32)
        class_row = grads[CELLS : CELLS + 1, :]
        class_column = jnp.sum(
            jnp.where((down != CELLS) & (across == CELLS), grads, 0.0), axis=0, keepdims=True
        )
        cells = jnp.where(across < CELLS, grads, 0.0)
        pad_row = jnp.sum(jnp.where(pad_q, cells, 0.0), axis=0, keepdims=True)
        dsf[...] = jnp.where(pad_q, 0.0, cells)
        blank = jnp.zeros((24, WIDE - seq), f32)
        folded = jnp.zeros((24, WIDE), f32)
        for r in range(GRID):
            cells = jnp.concatenate([dsf[r * GRID : r * GRID + 24, :], blank], axis=1)
            folded = folded + (cells if r == 0 else pltpu.roll(cells, r * GRID, 1))
        padded_row = jnp.concatenate([pad_row, jnp.zeros((1, WIDE - seq), f32)], axis=1)
        folded = jnp.where(row24 < GRID, folded, 0.0) + jnp.where(row24 == GRID - 1, padded_row, 0.0)
        for i in range(GRID):
            gexp[GRID - 1 - i : GRID - i, :] = folded[i : i + 1, :]
        for x in range(SPAN):
            uexp[:, x * SPAN : x * SPAN + GRID] = gexp[:, x * GRID : (x + 1) * GRID]
        lined = pltpu.roll(uexp[...], 0, 1, stride=1, stride_axis=0)
        table = jnp.sum(lined, axis=0, keepdims=True)
        from_class = jnp.sum(jnp.where(across != CELLS, class_row, 0.0), axis=1, keepdims=True)
        class_pair = jnp.sum(jnp.where(across == CELLS, class_row, 0.0), axis=1, keepdims=True)
        to_class = jnp.sum(class_column, axis=1, keepdims=True)
        table = jnp.where(lane_t == ENTRIES, from_class, table)
        table = jnp.where(lane_t == ENTRIES + 1, to_class, table)
        tab[h : h + 1, :] = jnp.where(lane_t == ENTRIES + 2, class_pair, table)
        if h == 1:
            scatter_merge(7, stage_d, dn1r, 0, 0)
            scatter_merge(7, stage_d, dn1r, 0, 1)
            qkv_sums[1].add_parts()
    sums[9:10, 0:hw] = jnp.sum(dqt[...].astype(f32), axis=0, keepdims=True)
    sums[10:11, 0:hw] = jnp.sum(dvt[...].astype(f32), axis=0, keepdims=True)
    sums[9:11, hw:width] = jnp.zeros((2, width - hw), f32)
    for h in range(heads):
        at = 11 + 3 * h
        sums[at : at + 1, :] = tab[h : h + 1, 0:width]
        sums[at + 1 : at + 2, :] = tab[h : h + 1, width : 2 * width]
        sums[at + 2 : at + 3, 0 : TABLE - 2 * width] = tab[h : h + 1, 2 * width : TABLE]
        sums[at + 2 : at + 3, TABLE - 2 * width : width] = jnp.zeros((1, 3 * width - TABLE), f32)
    sums[11 + 3 * heads : SMALL, :] = jnp.zeros((SMALL - 11 - 3 * heads, width), f32)

    for k in range(1, NT):
        piece_arrived(10, zmr.at[(t + k) % NT], k)
    sums[0:REP, :] = zmr[0] + zmr[1] + zmr[2] + zmr[3]
    g_small[...] = sums[...].astype(bf16)
    small_sum.send()
    qkv_sums[2].add_parts()
    small_sum.add_core()
    value = gpz[0].astype(f32)
    for k in range(1, NT):
        piece_arrived(9, gpz.at[NT + k], k)
        value = value + gpz[NT + k].astype(f32)
    t_proj[0, proj_rows, my_lanes] = value.astype(bf16)
    proj_sum.send(3)
    down_sum.spread_second()
    qkv_sums[0].spread()
    scatter_merge(7, stage_d, dn1r, 1, 0)
    scatter_merge(7, stage_d, dn1r, 1, 1)
    qkv_sums[1].spread()
    up_sum.spread_second()
    small_sum.add_parts()
    proj_sum.spread_first()
    qkv_sums[2].spread()
    sources = [(t_down.at[0], t_down_hbm), (t_up.at[0], t_up_hbm), (t_proj.at[0], t_proj_hbm), (t_small.at[0], t_small_hbm)]
    sources += [(t_qkv.at[h], t_qkv_hbm.at[192 * h : 192 * (h + 1), :]) for h in range(heads)]
    sources += [(ingradv, ingrad)]
    stores += [pltpu.make_async_copy(src, dst, store_sem.at[i + 1]) for i, (src, dst) in enumerate(sources)]
    down_sum.take(5)
    stores[1].start()
    total = scatter_total(7, dn1r, dn2own[...], (3,))
    normed, inverse = normalize(xg[t].astype(f32))
    ingradv[...] = dx1[...] + norm_back(total * gain_one, normed, inverse)
    stores[8].start()
    small_sum.spread()
    proj_sum.spread_second()
    up_sum.take(5)
    stores[2].start()
    for h in range(heads):
        qkv_sums[h].take()
        stores[5 + h].start()
    proj_sum.take(5)
    stores[3].start()
    small_sum.take()
    stores[4].start()

    gather_sent(0, xg, x_hbm)
    gather_sent(1, cg, cot_hbm)
    gather_sent(3, n2g)
    for i in range(NT - 1):
        scatter_copy(5, stage_c, z2r, i).wait_send()
    scatter_copy(4, stage_b, dn2r, 2).wait_send()
    scatter_copy(7, stage_d, dn1r, 2).wait_send()
    for half in range(2):
        far_copy(4, stage_b, dn2r, half).wait_send()
        scatter_copy(4, stage_b, dn2r, 1, half).wait_send()
        scatter_copy(7, stage_d, dn1r, 0, half).wait_send()
        scatter_copy(7, stage_d, dn1r, 1, half).wait_send()
    for k in range(1, NT):
        proj_piece(k).wait_send()
        mixed_piece(k).wait_send()
        mixed_back(k).wait_send()
        proj_exchange(k).wait_send()
        small_tensor(k).wait_send()
    for part_sum in (down_sum, up_sum, proj_sum, small_sum, *qkv_sums):
        part_sum.sent()
    proj_all.sent(3)
    for store in stores:
        store.wait()


def finish_kernel(
    down_in, up_in, proj_in, qkv_in, small_in, out_in, ingrad_in,
    out, ingrad, g_qkv, g_qv, g_table, g_proj, g_up, g_up_bias, g_down, g_gains, g_shifts, g_scales, g_biases,
    down_v, up_v, proj_v, qkv_v, down_f, up_f, proj_f, qkv_f, small_v, out_v, ingrad_v, load_sem, store_sem,
):
    width = g_down.shape[1]
    hw = g_proj.shape[0]
    heads, entries = g_table.shape
    parts = []
    for given, rounded, widened, result in (
        (down_in, down_v, down_f, g_down), (up_in, up_v, up_f, g_up),
        (qkv_in, qkv_v, qkv_f, g_qkv), (proj_in, proj_v, proj_f, g_proj),
    ):
        for start in range(0, given.shape[0], PIECE):
            piece = [ref.at[start : start + PIECE, :] for ref in (given, rounded, widened, result)]
            parts.append(piece + [given is qkv_in])
    moved = [(small_in, small_v, None), (out_in, out_v, out), (ingrad_in, ingrad_v, ingrad)]
    count = len(parts)
    loads = [pltpu.make_async_copy(part[0], part[1], load_sem.at[i]) for i, part in enumerate(parts)]
    loads += [pltpu.make_async_copy(src, via, load_sem.at[count + i]) for i, (src, via, _) in enumerate(moved)]
    for copy in loads:
        copy.start()
    stores = []
    by_head = [i for i, part in enumerate(parts) if part[4]]
    for i, (_, rounded, widened, result, mixed) in enumerate(parts):
        if mixed:
            which = i - by_head[0]
            for h, j in enumerate(by_head):
                if which == 0:
                    loads[j].wait()
                widened[64 * h : 64 * (h + 1), :] = parts[j][1][64 * which : 64 * (which + 1), :].astype(f32)
        else:
            loads[i].wait()
            widened[...] = rounded[...].astype(f32)
        stores.append(pltpu.make_async_copy(widened, result, store_sem.at[i]))
        stores[-1].start()
    for i, (_, via, dst) in enumerate(moved):
        loads[count + i].wait()
        if dst is not None:
            stores.append(pltpu.make_async_copy(via, dst, store_sem.at[count + i]))
            stores[-1].start()
    small = small_v[...].astype(f32)
    g_gains[...] = small[0:2, :]
    g_shifts[...] = small[2:4, :]
    g_scales[...] = small[4:6, :]
    g_biases[...] = small[6:8, :]
    g_up_bias[...] = jnp.reshape(small[8:9, :], (width,))
    g_qv[...] = small[9:11, 0:hw]
    for h in range(heads):
        for j in range(3):
            lanes = min(width, entries - j * width)
            g_table[h : h + 1, j * width : j * width + lanes] = small[
                11 + 3 * h + j : 12 + 3 * h + j, 0:lanes
            ]
    for copy in stores:
        copy.wait()


def per_device(
    n_dp, tokens, grids, qkv_weight, qv_bias, rel_table, proj_weight, fc1_weight, fc1_bias, fc2_weight,
    norm_gains, norm_biases, layer_scales, out_biases, cotangent,
):
    rows, width = tokens.shape
    seq = rows * NT
    heads, entries = rel_table.shape
    hw = heads * 64
    ff = fc1_weight.shape[1]
    qkv_rows = jnp.transpose(qkv_weight, (1, 2, 0)).reshape(3 * hw, width)
    vm = pl.BlockSpec(memory_space=pltpu.VMEM)
    anywhere = pl.BlockSpec(memory_space=pl.ANY)

    def many(count, shape, dtype):
        return [pltpu.VMEM(shape, dtype)] * count

    def sems(*shape):
        return [pltpu.SemaphoreType.DMA(shape)]

    half = width // 2
    scratch = [
        pltpu.VMEM((rows, width), bf16), pltpu.VMEM((rows, width), f32), pltpu.VMEM((3 * hw, width), bf16),
        pltpu.VMEM((width, ff), bf16), pltpu.VMEM((ff, width), bf16),
        pltpu.VMEM((2, hw), f32), pltpu.VMEM((heads, entries), f32), pltpu.VMEM((ff,), bf16),
    ]
    scratch += many(4, (2, width), f32) + sems(13) + sems(9)
    scratch += many(4, (NT, rows, width), bf16)
    scratch += many(1, (NT, hw, rows), bf16) + many(1, (NT, hw, width), bf16)
    scratch += many(3, (NT, rows, width), bf16) + many(3, (NT - 1, rows, width), bf16)
    scratch += many(1, (NT, hw, rows), bf16) + sems(11, 2 * NT) + sems(11, 2 * NT) + sems(4, 5, 2)
    scratch += many(4, (seq, seq), bf16)
    scratch += many(1, (heads, seq, seq), f32) + many(1, (24, WIDE), f32) + many(1, (24, TABLE), f32)
    scratch += many(1, (seq, width), bf16) + many(3, (seq, hw), bf16)
    scratch += many(3, (heads, seq, 64), bf16)
    scratch += many(1, (heads, seq, seq), f32) + many(1, (heads, seq, seq), bf16)
    scratch += many(1, (seq, hw), bf16) + many(1, (hw, seq), bf16)
    scratch += many(2, (rows, width), f32) + many(1, (rows, 128), f32) + many(4, (rows, width), f32)
    scratch += many(2, (seq, ff), bf16) + many(1, (hw, seq), bf16) + many(1, (heads, seq, 64), bf16)
    scratch += many(1, (heads, seq, seq), bf16) + many(1, (seq, seq), f32) + many(6, (seq, hw), bf16)
    scratch += many(1, (8, TABLE), f32) + many(1, (SMALL, width), f32) + many(1, (NT, REP, width), f32)
    scratch += many(1, (2 * NT, hw // 4, half), bf16) + sems(5 + heads, 8) + sems(5 + heads, 8)
    for lead, count in ((1, ff), (1, width), (NT, hw)):
        scratch += [
            pltpu.VMEM((lead, count, width), bf16), pltpu.VMEM((lead, count, half), bf16),
            pltpu.VMEM((lead, count, half), bf16), pltpu.VMEM((lead, count // 2, half), bf16),
            pltpu.VMEM((lead, count // 4, half), bf16),
        ]
    for count in (192,) * heads + (SMALL,):
        scratch += [
            pltpu.VMEM((count, width), bf16), pltpu.VMEM((count, half), bf16), pltpu.VMEM((count, half), bf16),
            pltpu.VMEM((CHIPS - 1, count // CHIPS, half), bf16),
        ]
    for lead, count in ((1, ff), (1, width), (1, hw), (heads, 192), (1, SMALL)):
        scratch += many(1, (lead, count, width), bf16)
    flat = [jax.ShapeDtypeStruct((count, width), bf16) for count in (ff, width, hw, 3 * hw, SMALL)]
    output, input_grad, *totals = pl.pallas_call(
        main_kernel,
        out_shape=[
            jax.ShapeDtypeStruct((rows, width), bf16),
            jax.ShapeDtypeStruct((rows, width), f32),
        ]
        + flat,
        in_specs=[pl.BlockSpec(memory_space=pltpu.SMEM)] + [anywhere] * 13,
        out_specs=[anywhere] * 7,
        scratch_shapes=scratch,
        compiler_params=pltpu.CompilerParams(
            collective_id=0, has_side_effects=True, vmem_limit_bytes=60 << 20
        ),
        name="layer",
    )(
        grids, tokens, cotangent, qkv_rows, proj_weight, fc1_weight, fc2_weight,
        qv_bias, rel_table, fc1_bias, norm_gains, norm_biases, layer_scales, out_biases,
    )
    pair = jax.ShapeDtypeStruct((2, width), f32)
    pieces = sum(-(-count // PIECE) for count in (ff, width, hw, 3 * hw))
    results = pl.pallas_call(
        finish_kernel,
        out_shape=(
            jax.ShapeDtypeStruct((rows, width), bf16),
            jax.ShapeDtypeStruct((rows, width), f32),
            jax.ShapeDtypeStruct((3 * hw, width), f32),
            jax.ShapeDtypeStruct((2, hw), f32),
            jax.ShapeDtypeStruct((heads, entries), f32),
            jax.ShapeDtypeStruct((hw, width), f32),
            jax.ShapeDtypeStruct((width, ff), f32),
            jax.ShapeDtypeStruct((ff,), f32),
            jax.ShapeDtypeStruct((ff, width), f32),
            pair, pair, pair, pair,
        ),
        in_specs=[anywhere] * 7,
        out_specs=(
            anywhere, anywhere, anywhere, vm, vm, anywhere, anywhere, vm, anywhere, vm, vm, vm, vm,
        ),
        scratch_shapes=[
            pltpu.VMEM((ff, width), bf16), pltpu.VMEM((width, ff), bf16), pltpu.VMEM((hw, width), bf16),
            pltpu.VMEM((3 * hw, width), bf16),
            pltpu.VMEM((ff, width), f32), pltpu.VMEM((width, ff), f32), pltpu.VMEM((hw, width), f32),
            pltpu.VMEM((3 * hw, width), f32), pltpu.VMEM((SMALL, width), bf16),
            pltpu.VMEM((rows, width), bf16), pltpu.VMEM((rows, width), f32),
            *sems(pieces + 3), *sems(pieces + 3),
        ],
        compiler_params=pltpu.CompilerParams(vmem_limit_bytes=60 << 20),
        name="finish",
    )(*totals, output, input_grad)
    results = list(results)
    stride = GROUP
    while stride < n_dp:
        hops = [(i, i ^ stride) for i in range(n_dp)]
        results[2:] = [value + lax.ppermute(value, "dp", hops) for value in results[2:]]
        stride *= 2
    results[2] = jnp.transpose(results[2].reshape(3, hw, width), (2, 0, 1))
    return tuple(results)


def solution(mesh):
    n_dp = mesh.shape["dp"]
    blocks = P(("dp", "tensor"), None)
    placed = (
        blocks, P("dp", None), P(None, None, "tensor"), P(None, "tensor"), P("tensor", None), P("tensor", None),
        P(None, "tensor"), P("tensor"), P("tensor", None), P(), P(), P(), P(), blocks,
    )
    given = (
        blocks, blocks, P(None, None, "tensor"), P(None, "tensor"), P("tensor", None), P("tensor", None),
        P(None, "tensor"), P("tensor"), P("tensor", None), P(), P(), P(), P(),
    )

    def layer(*arrays):
        return per_device(n_dp, *arrays)

    return jax.shard_map(layer, mesh=mesh, in_specs=placed, out_specs=given, check_vma=False)
```
